32 devices in a mesh: depth: 8 (over z, x), rows: 4 (over y, core).
Axes of the slice: x: 2, y: 2, z: 4, core: 2. Of those that a mesh axis runs over, the one named last changes fastest.
Arguments:
- log_density: float32 [32, 512, 2048], P('depth', 'rows'), may hold values from -6 to 6
Outputs:
- frame: float32 [4, 512, 8, 256], P(None, 'rows', 'depth')
The draws below stay inside these ranges and needn't reach their ends.
All inputs are finite; a program needn't handle non-finite values.
Results may differ from the reference program's by a relative error of at most 0.00002.
Values sent between devices are 32-bit elements; how exact they have to be, the bound alone decides.
A program may use at most 64 MiB of HBM per device.

```python
import jax
import jax.numpy as jnp
from jax import lax

W = 2048
NZ = 32
H = 512
WB = 256
N_DEPTH = 8


def shard_levels(own_key, dims, cuts, smallest, high):
    factor_of, own = 1.0, jax.random.fold_in(own_key, 6)
    for dim, blocks in cuts:
        steps = jnp.exp(jax.random.uniform(jax.random.fold_in(own, dim), (blocks,), jnp.float32, smallest / len(cuts), high / len(cuts)))
        factor_of = factor_of * jnp.repeat(steps, dims[dim] // blocks).reshape([-1 if axis == dim else 1 for axis in range(len(dims))])
    return factor_of


def bell_draw(own_key, extent, deviation, most, cuts=(), held_as=jnp.bfloat16):
    entries = deviation * jax.random.normal(own_key, extent, jnp.float32)
    if cuts:
        entries = entries * shard_levels(own_key, extent, cuts, -0.22, 0.18)
    return jnp.clip(entries, -most, most).astype(held_as)


def setup_inputs(seed: int = 0) -> dict:
    splits = jax.random.split(jax.random.key(seed), 2)
    return {
        "log_density": bell_draw(splits[0], (NZ, H, W), 1.0, 6.0, ((0, 8), (1, 4)), jnp.float32),
    }


def shade_slab(padded, extinction, count):

    def advance(carry, index):
        accum_colour, accum_opacity = carry
        planes = lax.dynamic_slice_in_dim(padded, index, 3, 0)
        centre = planes[1, 1:-1, 1:-1]
        grad_z = 0.5 * (planes[2, 1:-1, 1:-1] - planes[0, 1:-1, 1:-1])
        grad_y = 0.5 * (planes[1, 2:, 1:-1] - planes[1, :-2, 1:-1])
        grad_x = 0.5 * (planes[1, 1:-1, 2:] - planes[1, 1:-1, :-2])
        length = jnp.sqrt(grad_z * grad_z + grad_y * grad_y + grad_x * grad_x + 1.0)
        facing = (0.6 * grad_z + 0.48 * grad_y + 0.64 * grad_x) / length
        shading = 0.3 + 0.7 * jnp.abs(facing)
        colour = jnp.stack([jax.nn.sigmoid(2.0 * centre), jnp.exp(-centre * centre), jax.nn.sigmoid(-2.0 * centre)]) * shading
        opacity = 1.0 - jnp.exp(-extinction * jnp.exp(1.5 * centre))
        weight = (1.0 - accum_opacity) * opacity
        return ((accum_colour + weight * colour, accum_opacity + weight), None)
    height = padded.shape[1] - 2
    width = padded.shape[2] - 2
    start = (jnp.zeros((3, height, width), jnp.float32), jnp.zeros((height, width), jnp.float32))
    (colour_sum, opacity_sum), _ = lax.scan(advance, start, jnp.arange(count, dtype=jnp.int32))
    return jnp.concatenate([colour_sum, opacity_sum[None]], axis=0)

def reference(log_density):
    padded = jnp.pad(log_density, 1)
    image = shade_slab(padded, 0.5 / NZ, NZ)
    return image.reshape(4, H, WB, N_DEPTH).transpose(0, 1, 3, 2)
```

```python
import functools

import jax
import jax.numpy as jnp
from jax import lax
from jax.experimental import pallas as pl
from jax.experimental.pallas import tpu as pltpu
from jax.sharding import PartitionSpec as P

MESH = pl.DeviceIdType.MESH
TILE = 8
LANES = 128
BLOCK = 256


def with_halo(shard, sides, width):
    for axis, dim in sides:
        size, length = (lax.axis_size(axis), shard.shape[dim])
        up = [(i, (i + 1) % size) for i in range(size - 1)]
        down = [(j, i) for i, j in up]
        last = lax.slice_in_dim(shard, length - width, length, axis=dim)
        leading = lax.slice_in_dim(shard, 0, width, axis=dim)
        before = lax.ppermute(last, axis, up)
        after = lax.ppermute(leading, axis, down)
        shard = jnp.concatenate([before, shard, after], axis=dim)
    return shard


def shade_slab(padded, extinction, count):

    def advance(carry, index):
        accum_colour, accum_opacity = carry
        planes = lax.dynamic_slice_in_dim(padded, index, 3, 0)
        centre = planes[1, 1:-1, 1:-1]
        grad_z = 0.5 * (planes[2, 1:-1, 1:-1] - planes[0, 1:-1, 1:-1])
        grad_y = 0.5 * (planes[1, 2:, 1:-1] - planes[1, :-2, 1:-1])
        grad_x = 0.5 * (planes[1, 1:-1, 2:] - planes[1, 1:-1, :-2])
        length = jnp.sqrt(grad_z * grad_z + grad_y * grad_y + grad_x * grad_x + 1.0)
        facing = (0.6 * grad_z + 0.48 * grad_y + 0.64 * grad_x) / length
        shading = 0.3 + 0.7 * jnp.abs(facing)
        colour = (
            jnp.stack(
                [
                    jax.nn.sigmoid(2.0 * centre),
                    jnp.exp(-centre * centre),
                    jax.nn.sigmoid(-2.0 * centre),
                ]
            )
            * shading
        )
        opacity = 1.0 - jnp.exp(-extinction * jnp.exp(1.5 * centre))
        weight = (1.0 - accum_opacity) * opacity
        return ((accum_colour + weight * colour, accum_opacity + weight), None)

    height = padded.shape[1] - 2
    width = padded.shape[2] - 2
    start = (jnp.zeros((3, height, width), jnp.float32), jnp.zeros((height, width), jnp.float32))
    (colour_sum, opacity_sum), _ = lax.scan(advance, start, jnp.arange(count, dtype=jnp.int32))
    return jnp.concatenate([colour_sum, opacity_sum[None]], axis=0)


def over_pixels(nearer, farther, channel_axis):
    coverage = lax.slice_in_dim(nearer, 3, 4, axis=channel_axis)
    return nearer + (1.0 - coverage) * farther


def local_general(log_density):
    slices, row_count, width = log_density.shape
    depth_count = lax.axis_size("depth")
    classes = width // depth_count
    padded = with_halo(log_density, (("depth", 0), ("rows", 1)), 1)
    padded = jnp.pad(padded, ((0, 0), (0, 0), (1, 1)))
    image = shade_slab(padded, 0.5 / (slices * depth_count), slices)
    partial_value = image.reshape(4, row_count, classes, depth_count).transpose(0, 1, 3, 2)
    layers = lax.all_to_all(partial_value[None], "depth", split_axis=3, concat_axis=0, tiled=True)
    while layers.shape[0] > 1:
        paired = layers.reshape((layers.shape[0] // 2, 2) + layers.shape[1:])
        layers = over_pixels(paired[:, 0], paired[:, 1], 1)
    return layers[0]


def bit_reversed(value, bits):
    return sum(((value >> b) & 1) << (bits - 1 - b) for b in range(bits))


def kernel(depth, rows, vol_ref, edge_ref, out_ref, cells, edges, spread, image, *rest):
    S, tiles, _, W = vol_ref.shape
    chunks = tiles // 2
    groups = depth // 2
    steps = groups.bit_length() - 1
    part = LANES * depth
    span = pl.ds(LANES, W)
    extinction = 0.5 / (S * depth)

    held, came = rest[: steps + 1], rest[steps + 1 : 2 * steps + 1]
    (own_sem, own_edge_sem, pair_send, pair_recv, edge_send, edge_recv, row_send, row_recv,
     face_send, face_recv, part_send, part_recv, last_send, last_recv) = rest[2 * steps + 1 :]

    me, row = lax.axis_index("depth"), lax.axis_index("rows")
    x, z = lax.rem(me, 2), me // 2
    first = me - x
    partner = first + 1 - x
    mine = 1 + S * x

    near = [(partner, row, None)]
    offsets = [(-1, z >= 1), (1, z <= groups - 2)]
    for d, there in offsets:
        near.append((me + 2 * d, row, there))
    for k in range(1, steps):
        near.append((2 * (z + (1 << k) * (1 - 2 * (lax.rem(z // (1 << k), 2)))) + x, row, None))
    for d, there in ((-1, row >= 1), (1, row <= rows - 2)):
        near.append((first, row + d, there))
        near.append((first + 1, row + d, there))
    barrier = pltpu.get_barrier_semaphore()
    count = 0
    for dd, rr, there in near:
        def greet(dd=dd, rr=rr):
            pl.semaphore_signal(barrier, inc=1, device_id=(dd, rr), device_id_type=MESH)
        if there is None:
            greet()
            count = count + 1
        else:
            pl.when(there)(greet)
            count = count + there.astype(jnp.int32)

    own = pltpu.make_async_copy(
        vol_ref.at[:, pl.ds(x * chunks, chunks)],
        cells.at[pl.ds(mine, S), pl.ds(1, chunks), :, span],
        own_sem,
    )
    own.start()
    own_edge = pltpu.make_async_copy(edge_ref.at[2 - x], edges.at[1 - x, x], own_edge_sem)
    own_edge.start()
    pl.semaphore_wait(barrier, count)

    def pair_copy(c):
        return pltpu.make_async_remote_copy(
            src_ref=vol_ref.at[:, (1 - x) * chunks + c],
            dst_ref=cells.at[pl.ds(mine, S), 1 + c, :, span],
            send_sem=pair_send.at[c], recv_sem=pair_recv.at[c],
            device_id=(partner, row), device_id_type=MESH,
        )

    def edge_copy():
        return pltpu.make_async_remote_copy(
            src_ref=edge_ref.at[1 + x], dst_ref=edges.at[x, x],
            send_sem=edge_send, recv_sem=edge_recv,
            device_id=(partner, row), device_id_type=MESH,
        )

    def row_copy(direction):
        return pltpu.make_async_remote_copy(
            src_ref=edge_ref.at[3 - 3 * direction], dst_ref=edges.at[direction, x],
            send_sem=row_send.at[direction], recv_sem=row_recv.at[x],
            device_id=(first + direction, row + 1 - 2 * direction), device_id_type=MESH,
        )

    def row_arrival(source):
        return pltpu.make_async_remote_copy(
            src_ref=edge_ref.at[0], dst_ref=edges.at[x, source],
            send_sem=row_send.at[0], recv_sem=row_recv.at[source],
            device_id=(partner, row), device_id_type=MESH,
        )

    def face_copy(direction, c):
        return pltpu.make_async_remote_copy(
            src_ref=cells.at[2 * S if direction == 0 else 1, 1 + c, :, span],
            dst_ref=cells.at[0 if direction == 0 else 2 * S + 1, 1 + c, :, span],
            send_sem=face_send.at[direction, c], recv_sem=face_recv.at[direction, c],
            device_id=(me + (2 if direction == 0 else -2), row), device_id_type=MESH,
        )

    def part_copy(k, c):
        half = groups >> (k + 1)
        bit = lax.rem(z // (1 << k), 2)
        return pltpu.make_async_remote_copy(
            src_ref=held[k].at[c, pl.ds((1 - bit) * half, half)], dst_ref=came[k].at[c],
            send_sem=part_send.at[k, c], recv_sem=part_recv.at[k, c],
            device_id=(me + 2 * (1 << k) * (1 - 2 * bit), row), device_id_type=MESH,
        )

    def last_copy(c):
        return pltpu.make_async_remote_copy(
            src_ref=held[steps].at[c, 0, 1 - x], dst_ref=out_ref.at[:, x * chunks + c],
            send_sem=last_send.at[c], recv_sem=last_recv.at[c],
            device_id=(partner, row), device_id_type=MESH,
        )

    edge_copy().start()

    @pl.loop(0, chunks)
    def _(c):
        pair_copy(c).start()

    has_next_row, has_prev_row = row <= rows - 2, row >= 1
    has_next, has_prev = z <= groups - 2, z >= 1
    has_edge = jnp.logical_or(jnp.logical_and(x == 0, has_prev_row), jnp.logical_and(x == 1, has_next_row))
    pl.when(has_next_row)(lambda: row_copy(0).start())
    pl.when(has_prev_row)(lambda: row_copy(1).start())

    @pl.loop(0, 2 * S + 2)
    def _(s):
        cells[s, :, :, 0:LANES] = jnp.zeros((chunks + 2, TILE, LANES), jnp.float32)
        cells[s, :, :, LANES + W :] = jnp.zeros((chunks + 2, TILE, LANES), jnp.float32)

    @pl.when(jnp.logical_not(has_prev))
    def _():
        @pl.loop(0, chunks)
        def _(c):
            cells[0, 1 + c, :, span] = jnp.zeros((TILE, W), jnp.float32)

    @pl.when(jnp.logical_not(has_next))
    def _():
        @pl.loop(0, chunks)
        def _(c):
            cells[2 * S + 1, 1 + c, :, span] = jnp.zeros((TILE, W), jnp.float32)

    @pl.loop(0, part // 16)
    def _(b):
        at = lax.broadcasted_iota(jnp.int32, (16, part), 0) + b * 16
        to = lax.broadcasted_iota(jnp.int32, (16, part), 1)
        source = (to % LANES) * depth + to // LANES
        spread[pl.ds(pl.multiple_of(b * 16, 16), 16), :] = jnp.where(at == source, 1.0, 0.0).astype(jnp.bfloat16)

    own.wait()
    own_edge.wait()
    edge_copy().wait()
    pl.when(has_next_row)(lambda: row_copy(0).wait_send())
    pl.when(has_prev_row)(lambda: row_copy(1).wait_send())

    @pl.when(has_edge)
    def _():
        row_arrival(0).wait_recv()
        row_arrival(1).wait_recv()

    @pl.when(jnp.logical_not(has_edge))
    def _():
        edges[x] = jnp.zeros(edges.shape[1:], jnp.float32)

    for s in range(2 * S):
        cells[1 + s, 0, TILE - 1 : TILE, LANES : LANES + W] = edges[0, s // S, s % S : s % S + 1, :]
        cells[1 + s, chunks + 1, 0:1, LANES : LANES + W] = edges[1, s // S, s % S : s % S + 1, :]

    row_of = lax.broadcasted_iota(jnp.int32, (TILE, BLOCK), 0)
    is_top, is_bottom = row_of == 0, row_of == TILE - 1

    def shade(c):
        t = 1 + c

        def columns(b, carry):
            base = pl.multiple_of(b * BLOCK, BLOCK)
            mid = pl.ds(pl.multiple_of(base + LANES, LANES), BLOCK)
            red = green = blue = alpha = jnp.zeros((TILE, BLOCK), jnp.float32)
            before = cells[0, t, :, mid]
            wide = cells[1, t, :, pl.ds(base, BLOCK + 2 * LANES)]
            for s in range(1, 2 * S + 1):
                centre = wide[:, LANES : LANES + BLOCK]
                if s < 2 * S:
                    wide_after = cells[s + 1, t, :, pl.ds(base, BLOCK + 2 * LANES)]
                    after = wide_after[:, LANES : LANES + BLOCK]
                else:
                    wide_after, after = None, cells[s + 1, t, :, mid]
                left = pltpu.roll(wide, 1, 1)[:, LANES : LANES + BLOCK]
                right = pltpu.roll(wide, BLOCK + 2 * LANES - 1, 1)[:, LANES : LANES + BLOCK]
                above = jnp.where(is_top, cells[s, t - 1, TILE - 1 : TILE, mid], pltpu.roll(centre, 1, 0))
                below = jnp.where(is_bottom, cells[s, t + 1, 0:1, mid], pltpu.roll(centre, TILE - 1, 0))
                dz, dy, dx = after - before, below - above, right - left
                square = dz * dz + dy * dy + dx * dx + 4.0
                facing = 0.42 * dz + 0.336 * dy + 0.448 * dx
                shading = 0.3 + jnp.abs(facing) * lax.rsqrt(square)
                opacity = 1.0 - jnp.exp(-extinction * jnp.exp(1.5 * centre))
                weight = (1.0 - alpha) * opacity
                lit = weight * shading
                half = 0.5 * lit
                swing = half * jnp.tanh(centre)
                red = red + (half + swing)
                green = green + lit * jnp.exp(-centre * centre)
                blue = blue + (half - swing)
                alpha = alpha + weight
                before, wide = centre, wide_after
            for ch, value in enumerate((red, green, blue, alpha)):
                image[ch, :, pl.ds(base, BLOCK)] = value
            return carry

        lax.fori_loop(0, W // BLOCK, columns, 0)
        for g in range(W // part):
            piece = image[:, :, g * part : (g + 1) * part].reshape(4 * TILE, part)
            high = piece.astype(jnp.bfloat16)
            low = (piece - high.astype(jnp.float32)).astype(jnp.bfloat16)
            both = jnp.dot(
                jnp.concatenate([high, low], axis=0), spread[...], preferred_element_type=jnp.float32
            )
            sorted_ = both[: 4 * TILE] + both[4 * TILE :]
            for j in range(depth):
                place = bit_reversed(j // 2, steps)
                held[0][c, place, j % 2, :, :, g * LANES : (g + 1) * LANES] = sorted_[
                    :, j * LANES : (j + 1) * LANES
                ].reshape(4, TILE, LANES)

    def combine(k, c):
        half = groups >> (k + 1)
        bit = lax.rem(z // (1 << k), 2)
        copy = part_copy(k, c)
        copy.wait_recv()

        def join(near_of, far_of):
            for i in range(half):
                for p in range(2):
                    near, far = near_of(i, p), far_of(i, p)
                    clear = 1.0 - near[3]
                    for ch in range(4):
                        held[k + 1][c, i, p, ch] = near[ch] + clear * far[ch]

        def kept(i, p):
            return held[k][c, bit * half + i, p]

        def received(i, p):
            return came[k][c, i, p]

        pl.when(bit == 0)(lambda: join(kept, received))
        pl.when(bit == 1)(lambda: join(received, kept))

    @pl.loop(0, chunks + steps + 1)
    def _(i):
        @pl.when(i < chunks)
        def _():
            pair_copy(i).wait_recv()
            pl.when(has_next)(lambda: face_copy(0, i).start())
            pl.when(has_prev)(lambda: face_copy(1, i).start())

        @pl.when(jnp.logical_and(i >= 1, i <= chunks))
        def _():
            c = i - 1
            pl.when(has_prev)(lambda: face_copy(0, c).wait_recv())
            pl.when(has_next)(lambda: face_copy(1, c).wait_recv())
            shade(c)
            part_copy(0, c).start()

        for k in range(steps):

            @pl.when(jnp.logical_and(i >= k + 2, i <= chunks + k + 1))
            def _(k=k):
                c = i - 2 - k
                combine(k, c)
                if k + 1 < steps:
                    part_copy(k + 1, c).start()
                else:
                    out_ref[:, x * chunks + c] = held[steps][c, 0, x]
                    last_copy(c).start()

    @pl.loop(0, chunks)
    def _(c):
        pair_copy(c).wait_send()
        pl.when(has_next)(lambda: face_copy(0, c).wait_send())
        pl.when(has_prev)(lambda: face_copy(1, c).wait_send())
        for k in range(steps):
            part_copy(k, c).wait_send()
        last_copy(c).wait()


def local(log_density):
    S, R, W = log_density.shape
    depth, rows = lax.axis_size("depth"), lax.axis_size("rows")
    groups = depth // 2
    fits = (
        depth >= 4
        and depth & (depth - 1) == 0
        and W % (LANES * depth) == 0
        and W % BLOCK == 0
        and R % (2 * TILE) == 0
    )
    if not fits:
        return local_general(log_density)
    steps = groups.bit_length() - 1
    tiles = R // TILE
    chunks = tiles // 2
    Cw = W // depth
    edge_rows = jnp.stack([log_density[:, r] for r in (0, R // 2 - 1, R // 2, R - 1)])
    F32 = jnp.float32
    parts = [pltpu.VMEM((chunks, groups >> k, 2, 4, TILE, Cw), F32) for k in range(steps + 1)]
    arrivals = [pltpu.VMEM((chunks, groups >> (k + 1), 2, 4, TILE, Cw), F32) for k in range(steps)]
    DMA = pltpu.SemaphoreType.DMA
    out = pl.pallas_call(
        functools.partial(kernel, depth, rows),
        out_shape=jax.ShapeDtypeStruct((4, tiles, TILE, Cw), F32),
        in_specs=[pl.BlockSpec(memory_space=pl.ANY)] * 2,
        out_specs=pl.BlockSpec(memory_space=pltpu.VMEM),
        scratch_shapes=[
            pltpu.VMEM((2 * S + 2, chunks + 2, TILE, W + 2 * LANES), F32),
            pltpu.VMEM((2, 2, S, W), F32),
            pltpu.VMEM((LANES * depth, LANES * depth), jnp.bfloat16),
            pltpu.VMEM((4, TILE, W), F32),
            *parts,
            *arrivals,
            DMA, DMA,
            DMA((chunks,)), DMA((chunks,)),
            DMA, DMA,
            DMA((2,)), DMA((2,)),
            DMA((2, chunks)), DMA((2, chunks)),
            DMA((steps, chunks)), DMA((steps, chunks)),
            DMA((chunks,)), DMA((chunks,)),
        ],
        compiler_params=pltpu.CompilerParams(
            collective_id=0, has_side_effects=True, vmem_limit_bytes=40 * 1024 * 1024
        ),
    )(log_density.reshape(S, tiles, TILE, W), edge_rows)
    return out.reshape(4, R, 1, Cw)


def solution(mesh):
    placed = (P("depth", "rows", None),)
    return jax.shard_map(
        local, mesh=mesh, in_specs=placed, out_specs=P(None, "rows", "depth", None), check_vma=False
    )
```

```python
import functools
import math

import jax
import jax.numpy as jnp
from jax import lax
from jax.experimental import pallas as pl
from jax.experimental.pallas import tpu as pltpu
from jax.sharding import PartitionSpec as P

MESH = pl.DeviceIdType.MESH
TILE = 8
LANES = 128
BLOCK = 256
AHEAD = 3
LOG2E = 1.4426950408889634


def with_halo(shard, sides, width):
    for axis, dim in sides:
        size, length = (lax.axis_size(axis), shard.shape[dim])
        up = [(i, (i + 1) % size) for i in range(size - 1)]
        down = [(j, i) for i, j in up]
        last = lax.slice_in_dim(shard, length - width, length, axis=dim)
        leading = lax.slice_in_dim(shard, 0, width, axis=dim)
        before = lax.ppermute(last, axis, up)
        after = lax.ppermute(leading, axis, down)
        shard = jnp.concatenate([before, shard, after], axis=dim)
    return shard


def shade_slab(padded, extinction, count):

    def advance(carry, index):
        accum_colour, accum_opacity = carry
        planes = lax.dynamic_slice_in_dim(padded, index, 3, 0)
        centre = planes[1, 1:-1, 1:-1]
        grad_z = 0.5 * (planes[2, 1:-1, 1:-1] - planes[0, 1:-1, 1:-1])
        grad_y = 0.5 * (planes[1, 2:, 1:-1] - planes[1, :-2, 1:-1])
        grad_x = 0.5 * (planes[1, 1:-1, 2:] - planes[1, 1:-1, :-2])
        length = jnp.sqrt(grad_z * grad_z + grad_y * grad_y + grad_x * grad_x + 1.0)
        facing = (0.6 * grad_z + 0.48 * grad_y + 0.64 * grad_x) / length
        shading = 0.3 + 0.7 * jnp.abs(facing)
        colour = (
            jnp.stack(
                [
                    jax.nn.sigmoid(2.0 * centre),
                    jnp.exp(-centre * centre),
                    jax.nn.sigmoid(-2.0 * centre),
                ]
            )
            * shading
        )
        opacity = 1.0 - jnp.exp(-extinction * jnp.exp(1.5 * centre))
        weight = (1.0 - accum_opacity) * opacity
        return ((accum_colour + weight * colour, accum_opacity + weight), None)

    height = padded.shape[1] - 2
    width = padded.shape[2] - 2
    start = (jnp.zeros((3, height, width), jnp.float32), jnp.zeros((height, width), jnp.float32))
    (colour_sum, opacity_sum), _ = lax.scan(advance, start, jnp.arange(count, dtype=jnp.int32))
    return jnp.concatenate([colour_sum, opacity_sum[None]], axis=0)


def over_pixels(nearer, farther, channel_axis):
    coverage = lax.slice_in_dim(nearer, 3, 4, axis=channel_axis)
    return nearer + (1.0 - coverage) * farther


def local_general(log_density):
    slices, row_count, width = log_density.shape
    depth_count = lax.axis_size("depth")
    classes = width // depth_count
    padded = with_halo(log_density, (("depth", 0), ("rows", 1)), 1)
    padded = jnp.pad(padded, ((0, 0), (0, 0), (1, 1)))
    image = shade_slab(padded, 0.5 / (slices * depth_count), slices)
    partial_value = image.reshape(4, row_count, classes, depth_count).transpose(0, 1, 3, 2)
    layers = lax.all_to_all(partial_value[None], "depth", split_axis=3, concat_axis=0, tiled=True)
    while layers.shape[0] > 1:
        paired = layers.reshape((layers.shape[0] // 2, 2) + layers.shape[1:])
        layers = over_pixels(paired[:, 0], paired[:, 1], 1)
    return layers[0]


def bit_reversed(value, bits):
    return sum(((value >> b) & 1) << (bits - 1 - b) for b in range(bits))


def kernel(depth, rows, vol_ref, edge_ref, out_ref, cells, edges, spread, image, *rest):
    S, tiles, _, W = vol_ref.shape
    chunks = tiles // 2
    groups = depth // 2
    steps = groups.bit_length() - 1
    ahead = min(AHEAD, chunks)
    part = LANES * depth
    span = pl.ds(LANES, W)
    log_extinction = math.log2(0.5 / (S * depth) * LOG2E)

    held, came = rest[: steps + 1], rest[steps + 1 : 2 * steps + 1]
    (own_sem, own_edge_sem, pair_send, pair_recv, edge_send, edge_recv, row_send, row_recv,
     face_send, face_recv, part_send, part_recv, last_send, last_recv) = rest[2 * steps + 1 :]

    me, row = lax.axis_index("depth"), lax.axis_index("rows")
    x, z = lax.rem(me, 2), me // 2
    first = me - x
    partner = first + 1 - x
    mine = 1 + S * x

    near = [(partner, row, None)]
    offsets = [(-1, z >= 1), (1, z <= groups - 2)]
    for d, there in offsets:
        near.append((me + 2 * d, row, there))
    for k in range(1, steps):
        near.append((2 * (z + (1 << k) * (1 - 2 * (lax.rem(z // (1 << k), 2)))) + x, row, None))
    for d, there in ((-1, row >= 1), (1, row <= rows - 2)):
        near.append((first, row + d, there))
        near.append((first + 1, row + d, there))
    barrier = pltpu.get_barrier_semaphore()
    count = 0
    for dd, rr, there in near:
        def greet(dd=dd, rr=rr):
            pl.semaphore_signal(barrier, inc=1, device_id=(dd, rr), device_id_type=MESH)
        if there is None:
            greet()
            count = count + 1
        else:
            pl.when(there)(greet)
            count = count + there.astype(jnp.int32)

    own = pltpu.make_async_copy(
        vol_ref.at[:, pl.ds(x * chunks, chunks)],
        cells.at[pl.ds(mine, S), pl.ds(1, chunks), :, span],
        own_sem,
    )
    own.start()
    own_edge = pltpu.make_async_copy(edge_ref.at[2 - x], edges.at[1 - x, x], own_edge_sem)
    own_edge.start()
    pl.semaphore_wait(barrier, count)

    def pair_copy(c):
        return pltpu.make_async_remote_copy(
            src_ref=vol_ref.at[:, (1 - x) * chunks + c],
            dst_ref=cells.at[pl.ds(mine, S), 1 + c, :, span],
            send_sem=pair_send.at[c], recv_sem=pair_recv.at[c],
            device_id=(partner, row), device_id_type=MESH,
        )

    def edge_copy():
        return pltpu.make_async_remote_copy(
            src_ref=edge_ref.at[1 + x], dst_ref=edges.at[x, x],
            send_sem=edge_send, recv_sem=edge_recv,
            device_id=(partner, row), device_id_type=MESH,
        )

    def row_copy(direction):
        return pltpu.make_async_remote_copy(
            src_ref=edge_ref.at[3 - 3 * direction], dst_ref=edges.at[direction, x],
            send_sem=row_send.at[direction], recv_sem=row_recv.at[x],
            device_id=(first + direction, row + 1 - 2 * direction), device_id_type=MESH,
        )

    def row_arrival(source):
        return pltpu.make_async_remote_copy(
            src_ref=edge_ref.at[0], dst_ref=edges.at[x, source],
            send_sem=row_send.at[0], recv_sem=row_recv.at[source],
            device_id=(partner, row), device_id_type=MESH,
        )

    def face_copy(direction, c):
        return pltpu.make_async_remote_copy(
            src_ref=cells.at[2 * S if direction == 0 else 1, 1 + c, :, span],
            dst_ref=cells.at[0 if direction == 0 else 2 * S + 1, 1 + c, :, span],
            send_sem=face_send.at[direction, c], recv_sem=face_recv.at[direction, c],
            device_id=(me + (2 if direction == 0 else -2), row), device_id_type=MESH,
        )

    def part_copy(k, c):
        half = groups >> (k + 1)
        bit = lax.rem(z // (1 << k), 2)
        return pltpu.make_async_remote_copy(
            src_ref=held[k].at[c, pl.ds((1 - bit) * half, half)], dst_ref=came[k].at[c],
            send_sem=part_send.at[k, c], recv_sem=part_recv.at[k, c],
            device_id=(me + 2 * (1 << k) * (1 - 2 * bit), row), device_id_type=MESH,
        )

    def last_copy(c):
        return pltpu.make_async_remote_copy(
            src_ref=held[steps].at[c, 0, 1 - x], dst_ref=out_ref.at[:, x * chunks + c],
            send_sem=last_send.at[c], recv_sem=last_recv.at[c],
            device_id=(partner, row), device_id_type=MESH,
        )

    edge_copy().start()

    @pl.loop(0, ahead)
    def _(c):
        pair_copy(c).start()

    has_next_row, has_prev_row = row <= rows - 2, row >= 1
    has_next, has_prev = z <= groups - 2, z >= 1
    has_edge = jnp.logical_or(jnp.logical_and(x == 0, has_prev_row), jnp.logical_and(x == 1, has_next_row))
    pl.when(has_next_row)(lambda: row_copy(0).start())
    pl.when(has_prev_row)(lambda: row_copy(1).start())

    @pl.loop(0, 2 * S + 2)
    def _(s):
        cells[s, :, :, 0:LANES] = jnp.zeros((chunks + 2, TILE, LANES), jnp.float32)
        cells[s, :, :, LANES + W :] = jnp.zeros((chunks + 2, TILE, LANES), jnp.float32)

    @pl.when(jnp.logical_not(has_prev))
    def _():
        @pl.loop(0, chunks)
        def _(c):
            cells[0, 1 + c, :, span] = jnp.zeros((TILE, W), jnp.float32)

    @pl.when(jnp.logical_not(has_next))
    def _():
        @pl.loop(0, chunks)
        def _(c):
            cells[2 * S + 1, 1 + c, :, span] = jnp.zeros((TILE, W), jnp.float32)

    @pl.loop(0, part // 16)
    def _(b):
        at = lax.broadcasted_iota(jnp.int32, (16, part), 0) + b * 16
        to = lax.broadcasted_iota(jnp.int32, (16, part), 1)
        source = (to % LANES) * depth + to // LANES
        spread[pl.ds(pl.multiple_of(b * 16, 16), 16), :] = jnp.where(at == source, 1.0, 0.0).astype(jnp.bfloat16)

    own.wait()
    own_edge.wait()
    edge_copy().wait()
    pl.when(has_next_row)(lambda: row_copy(0).wait_send())
    pl.when(has_prev_row)(lambda: row_copy(1).wait_send())

    @pl.when(has_edge)
    def _():
        row_arrival(0).wait_recv()
        row_arrival(1).wait_recv()

    @pl.when(jnp.logical_not(has_edge))
    def _():
        edges[x] = jnp.zeros(edges.shape[1:], jnp.float32)

    for s in range(2 * S):
        cells[1 + s, 0, TILE - 1 : TILE, LANES : LANES + W] = edges[0, s // S, s % S : s % S + 1, :]
        cells[1 + s, chunks + 1, 0:1, LANES : LANES + W] = edges[1, s // S, s % S : s % S + 1, :]

    row_of = lax.broadcasted_iota(jnp.int32, (TILE, BLOCK), 0)
    is_top, is_bottom = row_of == 0, row_of == TILE - 1

    def shade(c):
        t = 1 + c

        def columns(b, carry):
            base = pl.multiple_of(b * BLOCK, BLOCK)
            mid = pl.ds(pl.multiple_of(base + LANES, LANES), BLOCK)
            both = swing = green = alpha = jnp.zeros((TILE, BLOCK), jnp.float32)
            before = cells[0, t, :, mid]
            wide = cells[1, t, :, pl.ds(base, BLOCK + 2 * LANES)]
            for s in range(1, 2 * S + 1):
                centre = wide[:, LANES : LANES + BLOCK]
                if s < 2 * S:
                    wide_after = cells[s + 1, t, :, pl.ds(base, BLOCK + 2 * LANES)]
                    after = wide_after[:, LANES : LANES + BLOCK]
                else:
                    wide_after, after = None, cells[s + 1, t, :, mid]
                left = pltpu.roll(wide, 1, 1)[:, LANES : LANES + BLOCK]
                right = pltpu.roll(wide, BLOCK + 2 * LANES - 1, 1)[:, LANES : LANES + BLOCK]
                above = jnp.where(is_top, cells[s, t - 1, TILE - 1 : TILE, mid], pltpu.roll(centre, 1, 0))
                below = jnp.where(is_bottom, cells[s, t + 1, 0:1, mid], pltpu.roll(centre, TILE - 1, 0))
                dz, dy, dx = after - before, below - above, right - left
                square = dz * dz + dy * dy + (dx * dx + 4.0)
                facing = 1.25 * dz + dy + (0.64 / 0.48) * dx
                shading = jnp.abs(facing) * lax.rsqrt(square) + 0.3 / 0.336
                opacity = 1.0 - jnp.exp2(-jnp.exp2((1.5 * LOG2E) * centre + log_extinction))
                weight = (1.0 - alpha) * opacity
                lit = weight * shading
                both = both + lit
                swing = swing + lit * jnp.tanh(centre)
                green = green + lit * jnp.exp2(centre * (centre * -LOG2E))
                alpha = alpha + weight
                before, wide = centre, wide_after
            both, swing = (0.5 * 0.336) * both, (0.5 * 0.336) * swing
            for ch, value in enumerate((both + swing, 0.336 * green, both - swing, alpha)):
                image[ch, :, pl.ds(base, BLOCK)] = value
            return carry

        lax.fori_loop(0, W // BLOCK, columns, 0)
        for g in range(W // part):
            piece = image[:, :, g * part : (g + 1) * part].reshape(4 * TILE, part)
            high = piece.astype(jnp.bfloat16)
            low = (piece - high.astype(jnp.float32)).astype(jnp.bfloat16)
            both = jnp.dot(
                jnp.concatenate([high, low], axis=0), spread[...], preferred_element_type=jnp.float32
            )
            sorted_ = both[: 4 * TILE] + both[4 * TILE :]
            for j in range(depth):
                place = bit_reversed(j // 2, steps)
                held[0][c, place, j % 2, :, :, g * LANES : (g + 1) * LANES] = sorted_[
                    :, j * LANES : (j + 1) * LANES
                ].reshape(4, TILE, LANES)

    def combine(k, c):
        half = groups >> (k + 1)
        bit = lax.rem(z // (1 << k), 2)
        copy = part_copy(k, c)
        copy.wait_recv()

        def join(near_of, far_of):
            for i in range(half):
                for p in range(2):
                    near, far = near_of(i, p), far_of(i, p)
                    clear = 1.0 - near[3]
                    for ch in range(4):
                        held[k + 1][c, i, p, ch] = near[ch] + clear * far[ch]

        def kept(i, p):
            return held[k][c, bit * half + i, p]

        def received(i, p):
            return came[k][c, i, p]

        pl.when(bit == 0)(lambda: join(kept, received))
        pl.when(bit == 1)(lambda: join(received, kept))

    @pl.loop(0, chunks + steps + 1)
    def _(i):
        @pl.when(i < chunks)
        def _():
            pair_copy(i).wait_recv()
            pl.when(i + ahead < chunks)(lambda: pair_copy(i + ahead).start())
            pl.when(has_next)(lambda: face_copy(0, i).start())
            pl.when(has_prev)(lambda: face_copy(1, i).start())

        @pl.when(jnp.logical_and(i >= 1, i <= chunks))
        def _():
            c = i - 1
            pl.when(has_prev)(lambda: face_copy(0, c).wait_recv())
            pl.when(has_next)(lambda: face_copy(1, c).wait_recv())
            shade(c)
            part_copy(0, c).start()

        for k in range(steps):

            @pl.when(jnp.logical_and(i >= k + 2, i <= chunks + k + 1))
            def _(k=k):
                c = i - 2 - k
                combine(k, c)
                if k + 1 < steps:
                    part_copy(k + 1, c).start()
                else:
                    out_ref[:, x * chunks + c] = held[steps][c, 0, x]
                    last_copy(c).start()

    @pl.loop(0, chunks)
    def _(c):
        pair_copy(c).wait_send()
        pl.when(has_next)(lambda: face_copy(0, c).wait_send())
        pl.when(has_prev)(lambda: face_copy(1, c).wait_send())
        for k in range(steps):
            part_copy(k, c).wait_send()
        last_copy(c).wait()


def local(log_density):
    S, R, W = log_density.shape
    depth, rows = lax.axis_size("depth"), lax.axis_size("rows")
    groups = depth // 2
    fits = (
        depth >= 4
        and depth & (depth - 1) == 0
        and W % (LANES * depth) == 0
        and W % BLOCK == 0
        and R % (2 * TILE) == 0
    )
    if not fits:
        return local_general(log_density)
    steps = groups.bit_length() - 1
    tiles = R // TILE
    chunks = tiles // 2
    Cw = W // depth
    edge_rows = jnp.stack([log_density[:, r] for r in (0, R // 2 - 1, R // 2, R - 1)])
    F32 = jnp.float32
    parts = [pltpu.VMEM((chunks, groups >> k, 2, 4, TILE, Cw), F32) for k in range(steps + 1)]
    arrivals = [pltpu.VMEM((chunks, groups >> (k + 1), 2, 4, TILE, Cw), F32) for k in range(steps)]
    DMA = pltpu.SemaphoreType.DMA
    out = pl.pallas_call(
        functools.partial(kernel, depth, rows),
        out_shape=jax.ShapeDtypeStruct((4, tiles, TILE, Cw), F32),
        in_specs=[pl.BlockSpec(memory_space=pl.ANY)] * 2,
        out_specs=pl.BlockSpec(memory_space=pltpu.VMEM),
        scratch_shapes=[
            pltpu.VMEM((2 * S + 2, chunks + 2, TILE, W + 2 * LANES), F32),
            pltpu.VMEM((2, 2, S, W), F32),
            pltpu.VMEM((LANES * depth, LANES * depth), jnp.bfloat16),
            pltpu.VMEM((4, TILE, W), F32),
            *parts,
            *arrivals,
            DMA, DMA,
            DMA((chunks,)), DMA((chunks,)),
            DMA, DMA,
            DMA((2,)), DMA((2,)),
            DMA((2, chunks)), DMA((2, chunks)),
            DMA((steps, chunks)), DMA((steps, chunks)),
            DMA((chunks,)), DMA((chunks,)),
        ],
        compiler_params=pltpu.CompilerParams(
            collective_id=0, has_side_effects=True, vmem_limit_bytes=60 * 1024 * 1024
        ),
    )(log_density.reshape(S, tiles, TILE, W), edge_rows)
    return out.reshape(4, R, 1, Cw)


def solution(mesh):
    placed = (P("depth", "rows", None),)
    return jax.shard_map(
        local, mesh=mesh, in_specs=placed, out_specs=P(None, "rows", "depth", None), check_vma=False
    )
```

```python
import functools
import math

import jax
import jax.numpy as jnp
from jax import lax
from jax.experimental import pallas as pl
from jax.experimental.pallas import tpu as pltpu
from jax.sharding import PartitionSpec as P

MESH = pl.DeviceIdType.MESH
TILE = 8
LANES = 128
BLOCK = 256
AHEAD = 3
LOG2E = 1.4426950408889634


def with_halo(shard, sides, width):
    for axis, dim in sides:
        size, length = (lax.axis_size(axis), shard.shape[dim])
        up = [(i, (i + 1) % size) for i in range(size - 1)]
        down = [(j, i) for i, j in up]
        last = lax.slice_in_dim(shard, length - width, length, axis=dim)
        leading = lax.slice_in_dim(shard, 0, width, axis=dim)
        before = lax.ppermute(last, axis, up)
        after = lax.ppermute(leading, axis, down)
        shard = jnp.concatenate([before, shard, after], axis=dim)
    return shard


def shade_slab(padded, extinction, count):

    def advance(carry, index):
        accum_colour, accum_opacity = carry
        planes = lax.dynamic_slice_in_dim(padded, index, 3, 0)
        centre = planes[1, 1:-1, 1:-1]
        grad_z = 0.5 * (planes[2, 1:-1, 1:-1] - planes[0, 1:-1, 1:-1])
        grad_y = 0.5 * (planes[1, 2:, 1:-1] - planes[1, :-2, 1:-1])
        grad_x = 0.5 * (planes[1, 1:-1, 2:] - planes[1, 1:-1, :-2])
        length = jnp.sqrt(grad_z * grad_z + grad_y * grad_y + grad_x * grad_x + 1.0)
        facing = (0.6 * grad_z + 0.48 * grad_y + 0.64 * grad_x) / length
        shading = 0.3 + 0.7 * jnp.abs(facing)
        colour = (
            jnp.stack(
                [
                    jax.nn.sigmoid(2.0 * centre),
                    jnp.exp(-centre * centre),
                    jax.nn.sigmoid(-2.0 * centre),
                ]
            )
            * shading
        )
        opacity = 1.0 - jnp.exp(-extinction * jnp.exp(1.5 * centre))
        weight = (1.0 - accum_opacity) * opacity
        return ((accum_colour + weight * colour, accum_opacity + weight), None)

    height = padded.shape[1] - 2
    width = padded.shape[2] - 2
    start = (jnp.zeros((3, height, width), jnp.float32), jnp.zeros((height, width), jnp.float32))
    (colour_sum, opacity_sum), _ = lax.scan(advance, start, jnp.arange(count, dtype=jnp.int32))
    return jnp.concatenate([colour_sum, opacity_sum[None]], axis=0)


def over_pixels(nearer, farther, channel_axis):
    coverage = lax.slice_in_dim(nearer, 3, 4, axis=channel_axis)
    return nearer + (1.0 - coverage) * farther


def local_general(log_density):
    slices, row_count, width = log_density.shape
    depth_count = lax.axis_size("depth")
    classes = width // depth_count
    padded = with_halo(log_density, (("depth", 0), ("rows", 1)), 1)
    padded = jnp.pad(padded, ((0, 0), (0, 0), (1, 1)))
    image = shade_slab(padded, 0.5 / (slices * depth_count), slices)
    partial_value = image.reshape(4, row_count, classes, depth_count).transpose(0, 1, 3, 2)
    layers = lax.all_to_all(partial_value[None], "depth", split_axis=3, concat_axis=0, tiled=True)
    while layers.shape[0] > 1:
        paired = layers.reshape((layers.shape[0] // 2, 2) + layers.shape[1:])
        layers = over_pixels(paired[:, 0], paired[:, 1], 1)
    return layers[0]


def bit_reversed(value, bits):
    return sum(((value >> b) & 1) << (bits - 1 - b) for b in range(bits))


def kernel(depth, rows, vol_ref, out_ref, cells, edges, rim, cut, spread, image, final, *rest):
    S, tiles, _, W = vol_ref.shape
    chunks = tiles // 2
    groups = depth // 2
    steps = groups.bit_length() - 1
    part = LANES * depth
    parts = W // part
    pieces = parts * chunks
    ahead = min(AHEAD, pieces)
    span = pl.ds(LANES, W)
    log_extinction = math.log2(0.5 / (S * depth) * LOG2E)

    held, came = rest[: steps + 1], rest[steps + 1 : 2 * steps + 1]
    (own_sem, rim_sem, own_edge_sem, pair_send, pair_recv, edge_send, edge_recv, row_send, row_recv,
     face_send, face_recv, part_send, part_recv, last_send, last_recv) = rest[2 * steps + 1 :]

    me, row = lax.axis_index("depth"), lax.axis_index("rows")
    x, z = lax.rem(me, 2), me // 2
    first = me - x
    partner = first + 1 - x
    mine = 1 + S * x

    near = [(partner, row, None)]
    for d, there in ((-1, z >= 1), (1, z <= groups - 2)):
        near.append((me + 2 * d, row, there))
    for k in range(1, steps):
        near.append((2 * (z + (1 << k) * (1 - 2 * (lax.rem(z // (1 << k), 2)))) + x, row, None))
    for d, there in ((-1, row >= 1), (1, row <= rows - 2)):
        near.append((first, row + d, there))
        near.append((first + 1, row + d, there))
    barrier = pltpu.get_barrier_semaphore()
    count = 0
    for dd, rr, there in near:
        def greet(dd=dd, rr=rr):
            pl.semaphore_signal(barrier, inc=1, device_id=(dd, rr), device_id_type=MESH)
        if there is None:
            greet()
            count = count + 1
        else:
            pl.when(there)(greet)
            count = count + there.astype(jnp.int32)

    own = pltpu.make_async_copy(
        vol_ref.at[:, pl.ds(x * chunks, chunks)],
        cells.at[pl.ds(mine, S), pl.ds(1, chunks), :, span],
        own_sem,
    )
    own.start()
    rims = [
        pltpu.make_async_copy(vol_ref.at[:, tile], rim.at[n], rim_sem.at[n])
        for n, tile in enumerate(((1 - x) * chunks, (2 - x) * chunks - 1))
    ]
    for copy in rims:
        copy.start()
    pl.semaphore_wait(barrier, count)

    def pair_copy(q):
        def apply(act):
            for g in range(parts):
                low = g * part + (LANES if g else 0)
                high = (g + 1) * part + (LANES if g + 1 < parts else 0)

                @pl.when(q // chunks == g)
                def _(g=g, low=low, high=high):
                    c = q - g * chunks
                    act(pltpu.make_async_remote_copy(
                        src_ref=vol_ref.at[:, (1 - x) * chunks + c, :, pl.ds(low, high - low)],
                        dst_ref=cells.at[pl.ds(mine, S), 1 + c, :, pl.ds(LANES + low, high - low)],
                        send_sem=pair_send.at[q], recv_sem=pair_recv.at[q],
                        device_id=(partner, row), device_id_type=MESH,
                    ))
        return apply

    def start(copy):
        copy.start()

    def edge_copy():
        return pltpu.make_async_remote_copy(
            src_ref=cut.at[1 + x], dst_ref=edges.at[x, x],
            send_sem=edge_send, recv_sem=edge_recv,
            device_id=(partner, row), device_id_type=MESH,
        )

    def row_copy(direction):
        return pltpu.make_async_remote_copy(
            src_ref=cut.at[3 - 3 * direction], dst_ref=edges.at[direction, x],
            send_sem=row_send.at[direction], recv_sem=row_recv.at[x],
            device_id=(first + direction, row + 1 - 2 * direction), device_id_type=MESH,
        )

    def row_arrival(source):
        return pltpu.make_async_remote_copy(
            src_ref=cut.at[0], dst_ref=edges.at[x, source],
            send_sem=row_send.at[0], recv_sem=row_recv.at[source],
            device_id=(partner, row), device_id_type=MESH,
        )

    def face_copy(direction, q):
        c, at = lax.rem(q, chunks), pl.ds(pl.multiple_of(LANES + q // chunks * part, LANES), part)
        return pltpu.make_async_remote_copy(
            src_ref=cells.at[2 * S if direction == 0 else 1, 1 + c, :, at],
            dst_ref=cells.at[0 if direction == 0 else 2 * S + 1, 1 + c, :, at],
            send_sem=face_send.at[direction, q], recv_sem=face_recv.at[direction, q],
            device_id=(me + (2 if direction == 0 else -2), row), device_id_type=MESH,
        )

    def part_copy(k, q):
        half = groups >> (k + 1)
        bit = lax.rem(z // (1 << k), 2)
        return pltpu.make_async_remote_copy(
            src_ref=held[k].at[q, pl.ds((1 - bit) * half, half)], dst_ref=came[k].at[q],
            send_sem=part_send.at[k, q], recv_sem=part_recv.at[k, q],
            device_id=(me + 2 * (1 << k) * (1 - 2 * bit), row), device_id_type=MESH,
        )

    def last_copy(q):
        return pltpu.make_async_remote_copy(
            src_ref=held[steps].at[q, 0, 1 - x], dst_ref=final.at[q],
            send_sem=last_send.at[q], recv_sem=last_recv.at[q],
            device_id=(partner, row), device_id_type=MESH,
        )

    pl.loop(0, ahead)(lambda q: pair_copy(q)(start))

    has_next_row, has_prev_row = row <= rows - 2, row >= 1
    has_next, has_prev = z <= groups - 2, z >= 1
    has_edge = jnp.logical_or(jnp.logical_and(x == 0, has_prev_row), jnp.logical_and(x == 1, has_next_row))

    own.wait()
    for copy in rims:
        copy.wait()
    for s in range(S):
        cut[2 * x, s : s + 1, :] = cells[mine + s, 1, 0:1, LANES : LANES + W]
        cut[1 + 2 * x, s : s + 1, :] = cells[mine + s, chunks, TILE - 1 : TILE, LANES : LANES + W]
        cut[2 - 2 * x, s : s + 1, :] = rim[0, s, 0:1, :]
        cut[3 - 2 * x, s : s + 1, :] = rim[1, s, TILE - 1 : TILE, :]
    edge_copy().start()
    pl.when(has_next_row)(lambda: row_copy(0).start())
    pl.when(has_prev_row)(lambda: row_copy(1).start())
    own_edge = pltpu.make_async_copy(cut.at[2 - x], edges.at[1 - x, x], own_edge_sem)
    own_edge.start()

    @pl.loop(0, 2 * S + 2)
    def _(s):
        cells[s, :, :, 0:LANES] = jnp.zeros((chunks + 2, TILE, LANES), jnp.float32)
        cells[s, :, :, LANES + W :] = jnp.zeros((chunks + 2, TILE, LANES), jnp.float32)

    @pl.when(jnp.logical_not(has_prev))
    def _():
        @pl.loop(0, chunks)
        def _(c):
            cells[0, 1 + c, :, span] = jnp.zeros((TILE, W), jnp.float32)

    @pl.when(jnp.logical_not(has_next))
    def _():
        @pl.loop(0, chunks)
        def _(c):
            cells[2 * S + 1, 1 + c, :, span] = jnp.zeros((TILE, W), jnp.float32)

    @pl.loop(0, part // 16)
    def _(b):
        at = lax.broadcasted_iota(jnp.int32, (16, part), 0) + b * 16
        to = lax.broadcasted_iota(jnp.int32, (16, part), 1)
        source = (to % LANES) * depth + to // LANES
        spread[pl.ds(pl.multiple_of(b * 16, 16), 16), :] = jnp.where(at == source, 1.0, 0.0).astype(jnp.bfloat16)

    own_edge.wait()
    edge_copy().wait()
    pl.when(has_next_row)(lambda: row_copy(0).wait_send())
    pl.when(has_prev_row)(lambda: row_copy(1).wait_send())

    @pl.when(has_edge)
    def _():
        row_arrival(0).wait_recv()
        row_arrival(1).wait_recv()

    @pl.when(jnp.logical_not(has_edge))
    def _():
        edges[x] = jnp.zeros(edges.shape[1:], jnp.float32)

    for s in range(2 * S):
        cells[1 + s, 0, TILE - 1 : TILE, LANES : LANES + W] = edges[0, s // S, s % S : s % S + 1, :]
        cells[1 + s, chunks + 1, 0:1, LANES : LANES + W] = edges[1, s // S, s % S : s % S + 1, :]

    row_of = lax.broadcasted_iota(jnp.int32, (TILE, BLOCK), 0)
    is_top, is_bottom = row_of == 0, row_of == TILE - 1

    def shade(q):
        t, begin = 1 + lax.rem(q, chunks), q // chunks * part

        def columns(b, carry):
            base = pl.multiple_of(begin + b * BLOCK, BLOCK)
            mid = pl.ds(pl.multiple_of(base + LANES, LANES), BLOCK)
            both = swing = green = alpha = jnp.zeros((TILE, BLOCK), jnp.float32)
            before = cells[0, t, :, mid]
            wide = cells[1, t, :, pl.ds(base, BLOCK + 2 * LANES)]
            for s in range(1, 2 * S + 1):
                centre = wide[:, LANES : LANES + BLOCK]
                if s < 2 * S:
                    wide_after = cells[s + 1, t, :, pl.ds(base, BLOCK + 2 * LANES)]
                    after = wide_after[:, LANES : LANES + BLOCK]
                else:
                    wide_after, after = None, cells[s + 1, t, :, mid]
                left = pltpu.roll(wide, 1, 1)[:, LANES : LANES + BLOCK]
                right = pltpu.roll(wide, BLOCK + 2 * LANES - 1, 1)[:, LANES : LANES + BLOCK]
                above = jnp.where(is_top, cells[s, t - 1, TILE - 1 : TILE, mid], pltpu.roll(centre, 1, 0))
                below = jnp.where(is_bottom, cells[s, t + 1, 0:1, mid], pltpu.roll(centre, TILE - 1, 0))
                dz, dy, dx = after - before, below - above, right - left
                square = dz * dz + dy * dy + (dx * dx + 4.0)
                facing = 1.25 * dz + dy + (0.64 / 0.48) * dx
                shading = jnp.abs(facing) * lax.rsqrt(square) + 0.3 / 0.336
                opacity = 1.0 - jnp.exp2(-jnp.exp2((1.5 * LOG2E) * centre + log_extinction))
                weight = (1.0 - alpha) * opacity
                lit = weight * shading
                both = both + lit
                swing = swing + lit * jnp.tanh(centre)
                green = green + lit * jnp.exp2(centre * (centre * -LOG2E))
                alpha = alpha + weight
                before, wide = centre, wide_after
            both, swing = (0.5 * 0.336) * both, (0.5 * 0.336) * swing
            for ch, value in enumerate((both + swing, 0.336 * green, both - swing, alpha)):
                image[ch, :, pl.ds(pl.multiple_of(b * BLOCK, BLOCK), BLOCK)] = value
            return carry

        lax.fori_loop(0, part // BLOCK, columns, 0)
        piece = image[...].reshape(4 * TILE, part)
        high = piece.astype(jnp.bfloat16)
        low = (piece - high.astype(jnp.float32)).astype(jnp.bfloat16)
        two = jnp.dot(jnp.concatenate([high, low], axis=0), spread[...], preferred_element_type=jnp.float32)
        by_class = two[: 4 * TILE] + two[4 * TILE :]
        for j in range(depth):
            held[0][q, bit_reversed(j // 2, steps), j % 2] = by_class[
                :, j * LANES : (j + 1) * LANES
            ].reshape(4, TILE, LANES)

    def combine(k, q):
        half = groups >> (k + 1)
        bit = lax.rem(z // (1 << k), 2)
        part_copy(k, q).wait_recv()

        def join(near_of, far_of):
            for i in range(half):
                for p in range(2):
                    near, far = near_of(i, p), far_of(i, p)
                    clear = 1.0 - near[3]
                    for ch in range(4):
                        held[k + 1][q, i, p, ch] = near[ch] + clear * far[ch]

        def kept(i, p):
            return held[k][q, bit * half + i, p]

        def received(i, p):
            return came[k][q, i, p]

        pl.when(bit == 0)(lambda: join(kept, received))
        pl.when(bit == 1)(lambda: join(received, kept))

    def put(side, q, value):
        at = ((side * chunks + lax.rem(q, chunks)) * TILE) * parts + q // chunks
        for ch in range(4):
            out_ref[ch, pl.ds(at, TILE, stride=parts), :] = value[ch]

    @pl.loop(0, pieces + steps + 1)
    def _(i):
        @pl.when(i < pieces)
        def _():
            pair_copy(i)(lambda copy: copy.wait_recv())
            pl.when(i + ahead < pieces)(lambda: pair_copy(i + ahead)(start))
            pl.when(has_next)(lambda: face_copy(0, i).start())
            pl.when(has_prev)(lambda: face_copy(1, i).start())

        @pl.when(jnp.logical_and(i >= 1, i <= pieces))
        def _():
            q = i - 1
            pl.when(has_prev)(lambda: face_copy(0, q).wait_recv())
            pl.when(has_next)(lambda: face_copy(1, q).wait_recv())
            shade(q)
            part_copy(0, q).start()

        for k in range(steps):

            @pl.when(jnp.logical_and(i >= k + 2, i <= pieces + k + 1))
            def _(k=k):
                q = i - 2 - k
                combine(k, q)
                if k + 1 < steps:
                    part_copy(k + 1, q).start()
                else:
                    last_copy(q).start()
                    put(x, q, held[steps][q, 0, x])

    @pl.loop(0, pieces)
    def _(q):
        pair_copy(q)(lambda copy: copy.wait_send())
        pl.when(has_next)(lambda: face_copy(0, q).wait_send())
        pl.when(has_prev)(lambda: face_copy(1, q).wait_send())
        for k in range(steps):
            part_copy(k, q).wait_send()
        last_copy(q).wait()
        put(1 - x, q, final[q])


def local(log_density):
    S, R, W = log_density.shape
    depth, rows = lax.axis_size("depth"), lax.axis_size("rows")
    groups = depth // 2
    fits = (
        depth >= 4
        and depth & (depth - 1) == 0
        and W % (LANES * depth) == 0
        and R % (2 * TILE) == 0
    )
    if not fits:
        return local_general(log_density)
    steps = groups.bit_length() - 1
    tiles = R // TILE
    chunks = tiles // 2
    part = LANES * depth
    parts = W // part
    pieces = parts * chunks
    F32 = jnp.float32
    partial = [pltpu.VMEM((pieces, groups >> k, 2, 4, TILE, LANES), F32) for k in range(steps + 1)]
    arrivals = [pltpu.VMEM((pieces, groups >> (k + 1), 2, 4, TILE, LANES), F32) for k in range(steps)]
    DMA = pltpu.SemaphoreType.DMA
    out = pl.pallas_call(
        functools.partial(kernel, depth, rows),
        out_shape=jax.ShapeDtypeStruct((4, R * parts, LANES), F32),
        in_specs=[pl.BlockSpec(memory_space=pl.ANY)],
        out_specs=pl.BlockSpec(memory_space=pltpu.VMEM),
        scratch_shapes=[
            pltpu.VMEM((2 * S + 2, chunks + 2, TILE, W + 2 * LANES), F32),
            pltpu.VMEM((2, 2, S, W), F32),
            pltpu.VMEM((2, S, TILE, W), F32),
            pltpu.VMEM((4, S, W), F32),
            pltpu.VMEM((part, part), jnp.bfloat16),
            pltpu.VMEM((4, TILE, part), F32),
            pltpu.VMEM((pieces, 4, TILE, LANES), F32),
            *partial,
            *arrivals,
            DMA, DMA((2,)), DMA,
            DMA((pieces,)), DMA((pieces,)),
            DMA, DMA,
            DMA((2,)), DMA((2,)),
            DMA((2, pieces)), DMA((2, pieces)),
            DMA((steps, pieces)), DMA((steps, pieces)),
            DMA((pieces,)), DMA((pieces,)),
        ],
        compiler_params=pltpu.CompilerParams(
            collective_id=0, has_side_effects=True, vmem_limit_bytes=60 * 1024 * 1024
        ),
    )(log_density.reshape(S, tiles, TILE, W))
    return out.reshape(4, R, 1, W // depth)


def solution(mesh):
    placed = (P("depth", "rows", None),)
    return jax.shard_map(
        local, mesh=mesh, in_specs=placed, out_specs=P(None, "rows", "depth", None), check_vma=False
    )
```

```python
import functools
import math

import jax
import jax.numpy as jnp
from jax import lax
from jax.experimental import pallas as pl
from jax.experimental.pallas import tpu as pltpu
from jax.sharding import PartitionSpec as P

MESH = pl.DeviceIdType.MESH
TILE = 8
LANES = 128
BLOCK = 256
AHEAD = 6
LOG2E = 1.4426950408889634


def with_halo(shard, sides, width):
    for axis, dim in sides:
        size, length = (lax.axis_size(axis), shard.shape[dim])
        up = [(i, (i + 1) % size) for i in range(size - 1)]
        down = [(j, i) for i, j in up]
        last = lax.slice_in_dim(shard, length - width, length, axis=dim)
        leading = lax.slice_in_dim(shard, 0, width, axis=dim)
        before = lax.ppermute(last, axis, up)
        after = lax.ppermute(leading, axis, down)
        shard = jnp.concatenate([before, shard, after], axis=dim)
    return shard


def shade_slab(padded, extinction, count):

    def advance(carry, index):
        accum_colour, accum_opacity = carry
        planes = lax.dynamic_slice_in_dim(padded, index, 3, 0)
        centre = planes[1, 1:-1, 1:-1]
        grad_z = 0.5 * (planes[2, 1:-1, 1:-1] - planes[0, 1:-1, 1:-1])
        grad_y = 0.5 * (planes[1, 2:, 1:-1] - planes[1, :-2, 1:-1])
        grad_x = 0.5 * (planes[1, 1:-1, 2:] - planes[1, 1:-1, :-2])
        length = jnp.sqrt(grad_z * grad_z + grad_y * grad_y + grad_x * grad_x + 1.0)
        facing = (0.6 * grad_z + 0.48 * grad_y + 0.64 * grad_x) / length
        shading = 0.3 + 0.7 * jnp.abs(facing)
        colour = (
            jnp.stack(
                [
                    jax.nn.sigmoid(2.0 * centre),
                    jnp.exp(-centre * centre),
                    jax.nn.sigmoid(-2.0 * centre),
                ]
            )
            * shading
        )
        opacity = 1.0 - jnp.exp(-extinction * jnp.exp(1.5 * centre))
        weight = (1.0 - accum_opacity) * opacity
        return ((accum_colour + weight * colour, accum_opacity + weight), None)

    height = padded.shape[1] - 2
    width = padded.shape[2] - 2
    start = (jnp.zeros((3, height, width), jnp.float32), jnp.zeros((height, width), jnp.float32))
    (colour_sum, opacity_sum), _ = lax.scan(advance, start, jnp.arange(count, dtype=jnp.int32))
    return jnp.concatenate([colour_sum, opacity_sum[None]], axis=0)


def over_pixels(nearer, farther, channel_axis):
    coverage = lax.slice_in_dim(nearer, 3, 4, axis=channel_axis)
    return nearer + (1.0 - coverage) * farther


def local_general(log_density):
    slices, row_count, width = log_density.shape
    depth_count = lax.axis_size("depth")
    classes = width // depth_count
    padded = with_halo(log_density, (("depth", 0), ("rows", 1)), 1)
    padded = jnp.pad(padded, ((0, 0), (0, 0), (1, 1)))
    image = shade_slab(padded, 0.5 / (slices * depth_count), slices)
    partial_value = image.reshape(4, row_count, classes, depth_count).transpose(0, 1, 3, 2)
    layers = lax.all_to_all(partial_value[None], "depth", split_axis=3, concat_axis=0, tiled=True)
    while layers.shape[0] > 1:
        paired = layers.reshape((layers.shape[0] // 2, 2) + layers.shape[1:])
        layers = over_pixels(paired[:, 0], paired[:, 1], 1)
    return layers[0]


def bit_reversed(value, bits):
    return sum(((value >> b) & 1) << (bits - 1 - b) for b in range(bits))


def kernel(depth, rows, vol_ref, out_ref, cells, edges, rim, cut, spread, image, final, *rest):
    S, tiles, _, W = vol_ref.shape
    chunks = tiles // 2
    groups = depth // 2
    steps = groups.bit_length() - 1
    part = LANES * depth
    parts = W // part
    pieces = parts * chunks
    ahead = min(AHEAD, pieces)
    span = pl.ds(LANES, W)
    log_extinction = math.log2(0.5 / (S * depth) * LOG2E)

    held, came = rest[: steps + 1], rest[steps + 1 : 2 * steps + 1]
    (own_sem, rim_sem, own_edge_sem, pair_send, pair_recv, edge_send, edge_recv, row_send, row_recv,
     face_send, face_recv, part_send, part_recv, last_send, last_recv) = rest[2 * steps + 1 :]

    me, row = lax.axis_index("depth"), lax.axis_index("rows")
    x, z = lax.rem(me, 2), me // 2
    first = me - x
    partner = first + 1 - x
    mine = 1 + S * x

    near = [(partner, row, None)]
    for d, there in ((-1, z >= 1), (1, z <= groups - 2)):
        near.append((me + 2 * d, row, there))
    for k in range(1, steps):
        near.append((2 * (z + (1 << k) * (1 - 2 * (lax.rem(z // (1 << k), 2)))) + x, row, None))
    for d, there in ((-1, row >= 1), (1, row <= rows - 2)):
        near.append((first, row + d, there))
        near.append((first + 1, row + d, there))
    barrier = pltpu.get_barrier_semaphore()
    count = 0
    for dd, rr, there in near:
        def greet(dd=dd, rr=rr):
            pl.semaphore_signal(barrier, inc=1, device_id=(dd, rr), device_id_type=MESH)
        if there is None:
            greet()
            count = count + 1
        else:
            pl.when(there)(greet)
            count = count + there.astype(jnp.int32)

    own = pltpu.make_async_copy(
        vol_ref.at[:, pl.ds(x * chunks, chunks)],
        cells.at[pl.ds(mine, S), pl.ds(1, chunks), :, span],
        own_sem,
    )
    own.start()
    rims = [
        pltpu.make_async_copy(vol_ref.at[:, tile], rim.at[n], rim_sem.at[n])
        for n, tile in enumerate(((1 - x) * chunks, (2 - x) * chunks - 1))
    ]
    for copy in rims:
        copy.start()
    pl.semaphore_wait(barrier, count)

    def pair_copy(q):
        def apply(act):
            for g in range(parts):
                low = g * part + (LANES if g else 0)
                high = (g + 1) * part + (LANES if g + 1 < parts else 0)

                @pl.when(q // chunks == g)
                def _(g=g, low=low, high=high):
                    c = q - g * chunks
                    act(pltpu.make_async_remote_copy(
                        src_ref=vol_ref.at[:, (1 - x) * chunks + c, :, pl.ds(low, high - low)],
                        dst_ref=cells.at[pl.ds(mine, S), 1 + c, :, pl.ds(LANES + low, high - low)],
                        send_sem=pair_send.at[q], recv_sem=pair_recv.at[q],
                        device_id=(partner, row), device_id_type=MESH,
                    ))
        return apply

    def start(copy):
        copy.start()

    def edge_copy():
        return pltpu.make_async_remote_copy(
            src_ref=cut.at[1 + x], dst_ref=edges.at[x, x],
            send_sem=edge_send, recv_sem=edge_recv,
            device_id=(partner, row), device_id_type=MESH,
        )

    def row_copy(direction):
        return pltpu.make_async_remote_copy(
            src_ref=cut.at[3 - 3 * direction], dst_ref=edges.at[direction, x],
            send_sem=row_send.at[direction], recv_sem=row_recv.at[x],
            device_id=(first + direction, row + 1 - 2 * direction), device_id_type=MESH,
        )

    def row_arrival(source):
        return pltpu.make_async_remote_copy(
            src_ref=cut.at[0], dst_ref=edges.at[x, source],
            send_sem=row_send.at[0], recv_sem=row_recv.at[source],
            device_id=(partner, row), device_id_type=MESH,
        )

    def face_copy(direction, q):
        c, at = lax.rem(q, chunks), pl.ds(pl.multiple_of(LANES + q // chunks * part, LANES), part)
        return pltpu.make_async_remote_copy(
            src_ref=cells.at[2 * S if direction == 0 else 1, 1 + c, :, at],
            dst_ref=cells.at[0 if direction == 0 else 2 * S + 1, 1 + c, :, at],
            send_sem=face_send.at[direction, q], recv_sem=face_recv.at[direction, q],
            device_id=(me + (2 if direction == 0 else -2), row), device_id_type=MESH,
        )

    def part_copy(k, q):
        half = groups >> (k + 1)
        bit = lax.rem(z // (1 << k), 2)
        return pltpu.make_async_remote_copy(
            src_ref=held[k].at[q, pl.ds((1 - bit) * half, half)], dst_ref=came[k].at[q],
            send_sem=part_send.at[k, q], recv_sem=part_recv.at[k, q],
            device_id=(me + 2 * (1 << k) * (1 - 2 * bit), row), device_id_type=MESH,
        )

    def last_copy(q):
        return pltpu.make_async_remote_copy(
            src_ref=held[steps].at[q, 0, 1 - x], dst_ref=final.at[q],
            send_sem=last_send.at[q], recv_sem=last_recv.at[q],
            device_id=(partner, row), device_id_type=MESH,
        )

    pl.loop(0, ahead)(lambda q: pair_copy(q)(start))

    has_next_row, has_prev_row = row <= rows - 2, row >= 1
    has_next, has_prev = z <= groups - 2, z >= 1
    has_edge = jnp.logical_or(jnp.logical_and(x == 0, has_prev_row), jnp.logical_and(x == 1, has_next_row))

    own.wait()
    for copy in rims:
        copy.wait()
    for s in range(S):
        cut[2 * x, s : s + 1, :] = cells[mine + s, 1, 0:1, LANES : LANES + W]
        cut[1 + 2 * x, s : s + 1, :] = cells[mine + s, chunks, TILE - 1 : TILE, LANES : LANES + W]
        cut[2 - 2 * x, s : s + 1, :] = rim[0, s, 0:1, :]
        cut[3 - 2 * x, s : s + 1, :] = rim[1, s, TILE - 1 : TILE, :]
    edge_copy().start()
    pl.when(has_next_row)(lambda: row_copy(0).start())
    pl.when(has_prev_row)(lambda: row_copy(1).start())
    own_edge = pltpu.make_async_copy(cut.at[2 - x], edges.at[1 - x, x], own_edge_sem)
    own_edge.start()

    @pl.loop(0, 2 * S + 2)
    def _(s):
        cells[s, :, :, 0:LANES] = jnp.zeros((chunks + 2, TILE, LANES), jnp.float32)
        cells[s, :, :, LANES + W :] = jnp.zeros((chunks + 2, TILE, LANES), jnp.float32)

    @pl.when(jnp.logical_not(has_prev))
    def _():
        @pl.loop(0, chunks)
        def _(c):
            cells[0, 1 + c, :, span] = jnp.zeros((TILE, W), jnp.float32)

    @pl.when(jnp.logical_not(has_next))
    def _():
        @pl.loop(0, chunks)
        def _(c):
            cells[2 * S + 1, 1 + c, :, span] = jnp.zeros((TILE, W), jnp.float32)

    @pl.loop(0, part // 16)
    def _(b):
        at = lax.broadcasted_iota(jnp.int32, (16, part), 0) + b * 16
        to = lax.broadcasted_iota(jnp.int32, (16, part), 1)
        source = (to % LANES) * depth + to // LANES
        spread[pl.ds(pl.multiple_of(b * 16, 16), 16), :] = jnp.where(at == source, 1.0, 0.0).astype(jnp.bfloat16)

    own_edge.wait()
    edge_copy().wait()
    pl.when(has_next_row)(lambda: row_copy(0).wait_send())
    pl.when(has_prev_row)(lambda: row_copy(1).wait_send())

    @pl.when(has_edge)
    def _():
        row_arrival(0).wait_recv()
        row_arrival(1).wait_recv()

    @pl.when(jnp.logical_not(has_edge))
    def _():
        edges[x] = jnp.zeros(edges.shape[1:], jnp.float32)

    for s in range(2 * S):
        cells[1 + s, 0, TILE - 1 : TILE, LANES : LANES + W] = edges[0, s // S, s % S : s % S + 1, :]
        cells[1 + s, chunks + 1, 0:1, LANES : LANES + W] = edges[1, s // S, s % S : s % S + 1, :]

    row_of = lax.broadcasted_iota(jnp.int32, (TILE, BLOCK), 0)
    is_top, is_bottom = row_of == 0, row_of == TILE - 1

    def shade(q):
        t, begin = 1 + lax.rem(q, chunks), q // chunks * part

        def columns(b, carry):
            base = pl.multiple_of(begin + b * BLOCK, BLOCK)
            mid = pl.ds(pl.multiple_of(base + LANES, LANES), BLOCK)
            both = swing = green = alpha = jnp.zeros((TILE, BLOCK), jnp.float32)
            before = cells[0, t, :, mid]
            wide = cells[1, t, :, pl.ds(base, BLOCK + 2 * LANES)]
            for s in range(1, 2 * S + 1):
                centre = wide[:, LANES : LANES + BLOCK]
                if s < 2 * S:
                    wide_after = cells[s + 1, t, :, pl.ds(base, BLOCK + 2 * LANES)]
                    after = wide_after[:, LANES : LANES + BLOCK]
                else:
                    wide_after, after = None, cells[s + 1, t, :, mid]
                left = pltpu.roll(wide, 1, 1)[:, LANES : LANES + BLOCK]
                right = pltpu.roll(wide, BLOCK + 2 * LANES - 1, 1)[:, LANES : LANES + BLOCK]
                above = jnp.where(is_top, cells[s, t - 1, TILE - 1 : TILE, mid], pltpu.roll(centre, 1, 0))
                below = jnp.where(is_bottom, cells[s, t + 1, 0:1, mid], pltpu.roll(centre, TILE - 1, 0))
                dz, dy, dx = after - before, below - above, right - left
                square = dz * dz + dy * dy + (dx * dx + 4.0)
                facing = 1.25 * dz + dy + (0.64 / 0.48) * dx
                shading = jnp.abs(facing) * lax.rsqrt(square) + 0.3 / 0.336
                opacity = 1.0 - jnp.exp2(-jnp.exp2((1.5 * LOG2E) * centre + log_extinction))
                weight = (1.0 - alpha) * opacity
                lit = weight * shading
                both = both + lit
                swing = swing + lit * jnp.tanh(centre)
                green = green + lit * jnp.exp2(centre * (centre * -LOG2E))
                alpha = alpha + weight
                before, wide = centre, wide_after
            both, swing = (0.5 * 0.336) * both, (0.5 * 0.336) * swing
            for ch, value in enumerate((both + swing, 0.336 * green, both - swing, alpha)):
                image[ch, :, pl.ds(pl.multiple_of(b * BLOCK, BLOCK), BLOCK)] = value
            return carry

        lax.fori_loop(0, part // BLOCK, columns, 0)
        piece = image[...].reshape(4 * TILE, part)
        high = piece.astype(jnp.bfloat16)
        low = (piece - high.astype(jnp.float32)).astype(jnp.bfloat16)
        two = jnp.dot(jnp.concatenate([high, low], axis=0), spread[...], preferred_element_type=jnp.float32)
        by_class = two[: 4 * TILE] + two[4 * TILE :]
        for j in range(depth):
            held[0][q, bit_reversed(j // 2, steps), j % 2] = by_class[
                :, j * LANES : (j + 1) * LANES
            ].reshape(4, TILE, LANES)

    def combine(k, q):
        half = groups >> (k + 1)
        bit = lax.rem(z // (1 << k), 2)
        part_copy(k, q).wait_recv()

        def join(near_of, far_of):
            for i in range(half):
                for p in range(2):
                    near, far = near_of(i, p), far_of(i, p)
                    clear = 1.0 - near[3]
                    for ch in range(4):
                        held[k + 1][q, i, p, ch] = near[ch] + clear * far[ch]

        def kept(i, p):
            return held[k][q, bit * half + i, p]

        def received(i, p):
            return came[k][q, i, p]

        pl.when(bit == 0)(lambda: join(kept, received))
        pl.when(bit == 1)(lambda: join(received, kept))

    def put(side, q, value):
        at = ((side * chunks + lax.rem(q, chunks)) * TILE) * parts + q // chunks
        for ch in range(4):
            out_ref[ch, pl.ds(at, TILE, stride=parts), :] = value[ch]

    @pl.loop(0, pieces + steps + 1)
    def _(i):
        @pl.when(i < pieces)
        def _():
            pair_copy(i)(lambda copy: copy.wait_recv())
            pl.when(i + ahead < pieces)(lambda: pair_copy(i + ahead)(start))
            pl.when(has_next)(lambda: face_copy(0, i).start())
            pl.when(has_prev)(lambda: face_copy(1, i).start())

        @pl.when(jnp.logical_and(i >= 1, i <= pieces))
        def _():
            q = i - 1
            pl.when(has_prev)(lambda: face_copy(0, q).wait_recv())
            pl.when(has_next)(lambda: face_copy(1, q).wait_recv())
            shade(q)
            part_copy(0, q).start()

        for k in range(steps):

            @pl.when(jnp.logical_and(i >= k + 2, i <= pieces + k + 1))
            def _(k=k):
                q = i - 2 - k
                combine(k, q)
                if k + 1 < steps:
                    part_copy(k + 1, q).start()
                else:
                    last_copy(q).start()
                    put(x, q, held[steps][q, 0, x])

    @pl.loop(0, pieces)
    def _(q):
        pair_copy(q)(lambda copy: copy.wait_send())
        pl.when(has_next)(lambda: face_copy(0, q).wait_send())
        pl.when(has_prev)(lambda: face_copy(1, q).wait_send())
        for k in range(steps):
            part_copy(k, q).wait_send()
        last_copy(q).wait()
        put(1 - x, q, final[q])


def local(log_density):
    S, R, W = log_density.shape
    depth, rows = lax.axis_size("depth"), lax.axis_size("rows")
    groups = depth // 2
    fits = (
        depth >= 4
        and depth & (depth - 1) == 0
        and W % (LANES * depth) == 0
        and R % (2 * TILE) == 0
    )
    if not fits:
        return local_general(log_density)
    steps = groups.bit_length() - 1
    tiles = R // TILE
    chunks = tiles // 2
    part = LANES * depth
    parts = W // part
    pieces = parts * chunks
    F32 = jnp.float32
    partial = [pltpu.VMEM((pieces, groups >> k, 2, 4, TILE, LANES), F32) for k in range(steps + 1)]
    arrivals = [pltpu.VMEM((pieces, groups >> (k + 1), 2, 4, TILE, LANES), F32) for k in range(steps)]
    DMA = pltpu.SemaphoreType.DMA
    out = pl.pallas_call(
        functools.partial(kernel, depth, rows),
        out_shape=jax.ShapeDtypeStruct((4, R * parts, LANES), F32),
        in_specs=[pl.BlockSpec(memory_space=pl.ANY)],
        out_specs=pl.BlockSpec(memory_space=pltpu.VMEM),
        scratch_shapes=[
            pltpu.VMEM((2 * S + 2, chunks + 2, TILE, W + 2 * LANES), F32),
            pltpu.VMEM((2, 2, S, W), F32),
            pltpu.VMEM((2, S, TILE, W), F32),
            pltpu.VMEM((4, S, W), F32),
            pltpu.VMEM((part, part), jnp.bfloat16),
            pltpu.VMEM((4, TILE, part), F32),
            pltpu.VMEM((pieces, 4, TILE, LANES), F32),
            *partial,
            *arrivals,
            DMA, DMA((2,)), DMA,
            DMA((pieces,)), DMA((pieces,)),
            DMA, DMA,
            DMA((2,)), DMA((2,)),
            DMA((2, pieces)), DMA((2, pieces)),
            DMA((steps, pieces)), DMA((steps, pieces)),
            DMA((pieces,)), DMA((pieces,)),
        ],
        compiler_params=pltpu.CompilerParams(
            collective_id=0, has_side_effects=True, vmem_limit_bytes=60 * 1024 * 1024
        ),
    )(log_density.reshape(S, tiles, TILE, W))
    return out.reshape(4, R, 1, W // depth)


def solution(mesh):
    placed = (P("depth", "rows", None),)
    return jax.shard_map(
        local, mesh=mesh, in_specs=placed, out_specs=P(None, "rows", "depth", None), check_vma=False
    )
```

```python
import functools
import math

import jax
import jax.numpy as jnp
from jax import lax
from jax.experimental import pallas as pl
from jax.experimental.pallas import tpu as pltpu
from jax.sharding import PartitionSpec as P

MESH = pl.DeviceIdType.MESH
TILE = 8
LANES = 128
BLOCK = 256
AHEAD = 2
LOG2E = 1.4426950408889634


def with_halo(shard, sides, width):
    for axis, dim in sides:
        size, length = (lax.axis_size(axis), shard.shape[dim])
        up = [(i, (i + 1) % size) for i in range(size - 1)]
        down = [(j, i) for i, j in up]
        last = lax.slice_in_dim(shard, length - width, length, axis=dim)
        leading = lax.slice_in_dim(shard, 0, width, axis=dim)
        before = lax.ppermute(last, axis, up)
        after = lax.ppermute(leading, axis, down)
        shard = jnp.concatenate([before, shard, after], axis=dim)
    return shard


def shade_slab(padded, extinction, count):

    def advance(carry, index):
        accum_colour, accum_opacity = carry
        planes = lax.dynamic_slice_in_dim(padded, index, 3, 0)
        centre = planes[1, 1:-1, 1:-1]
        grad_z = 0.5 * (planes[2, 1:-1, 1:-1] - planes[0, 1:-1, 1:-1])
        grad_y = 0.5 * (planes[1, 2:, 1:-1] - planes[1, :-2, 1:-1])
        grad_x = 0.5 * (planes[1, 1:-1, 2:] - planes[1, 1:-1, :-2])
        length = jnp.sqrt(grad_z * grad_z + grad_y * grad_y + grad_x * grad_x + 1.0)
        facing = (0.6 * grad_z + 0.48 * grad_y + 0.64 * grad_x) / length
        shading = 0.3 + 0.7 * jnp.abs(facing)
        colour = (
            jnp.stack(
                [
                    jax.nn.sigmoid(2.0 * centre),
                    jnp.exp(-centre * centre),
                    jax.nn.sigmoid(-2.0 * centre),
                ]
            )
            * shading
        )
        opacity = 1.0 - jnp.exp(-extinction * jnp.exp(1.5 * centre))
        weight = (1.0 - accum_opacity) * opacity
        return ((accum_colour + weight * colour, accum_opacity + weight), None)

    height = padded.shape[1] - 2
    width = padded.shape[2] - 2
    start = (jnp.zeros((3, height, width), jnp.float32), jnp.zeros((height, width), jnp.float32))
    (colour_sum, opacity_sum), _ = lax.scan(advance, start, jnp.arange(count, dtype=jnp.int32))
    return jnp.concatenate([colour_sum, opacity_sum[None]], axis=0)


def over_pixels(nearer, farther, channel_axis):
    coverage = lax.slice_in_dim(nearer, 3, 4, axis=channel_axis)
    return nearer + (1.0 - coverage) * farther


def local_general(log_density):
    slices, row_count, width = log_density.shape
    depth_count = lax.axis_size("depth")
    classes = width // depth_count
    padded = with_halo(log_density, (("depth", 0), ("rows", 1)), 1)
    padded = jnp.pad(padded, ((0, 0), (0, 0), (1, 1)))
    image = shade_slab(padded, 0.5 / (slices * depth_count), slices)
    partial_value = image.reshape(4, row_count, classes, depth_count).transpose(0, 1, 3, 2)
    layers = lax.all_to_all(partial_value[None], "depth", split_axis=3, concat_axis=0, tiled=True)
    while layers.shape[0] > 1:
        paired = layers.reshape((layers.shape[0] // 2, 2) + layers.shape[1:])
        layers = over_pixels(paired[:, 0], paired[:, 1], 1)
    return layers[0]


def bit_reversed(value, bits):
    return sum(((value >> b) & 1) << (bits - 1 - b) for b in range(bits))


def kernel(depth, rows, vol_ref, out_ref, cells, edges, rim, cut, spread, image, final, *rest):
    S, tiles, _, W = vol_ref.shape
    chunks = tiles // 2
    groups = depth // 2
    steps = groups.bit_length() - 1
    part = LANES * depth
    parts = W // part
    pieces = parts * chunks
    ahead = min(AHEAD, pieces)
    span = pl.ds(LANES, W)
    log_extinction = math.log2(0.5 / (S * depth) * LOG2E)

    held, came = rest[: steps + 1], rest[steps + 1 : 2 * steps + 1]
    (own_sem, rim_sem, own_edge_sem, pair_send, pair_recv, edge_send, edge_recv, row_send, row_recv,
     face_send, face_recv, part_send, part_recv, last_send, last_recv) = rest[2 * steps + 1 :]

    me, row = lax.axis_index("depth"), lax.axis_index("rows")
    x, z = lax.rem(me, 2), me // 2
    first = me - x
    partner = first + 1 - x
    mine = 1 + S * x

    near = [(partner, row, None)]
    for d, there in ((-1, z >= 1), (1, z <= groups - 2)):
        near.append((me + 2 * d, row, there))
    for k in range(1, steps):
        near.append((2 * (z + (1 << k) * (1 - 2 * (lax.rem(z // (1 << k), 2)))) + x, row, None))
    for d, there in ((-1, row >= 1), (1, row <= rows - 2)):
        near.append((first, row + d, there))
        near.append((first + 1, row + d, there))
    barrier = pltpu.get_barrier_semaphore()
    count = 0
    for dd, rr, there in near:
        def greet(dd=dd, rr=rr):
            pl.semaphore_signal(barrier, inc=1, device_id=(dd, rr), device_id_type=MESH)
        if there is None:
            greet()
            count = count + 1
        else:
            pl.when(there)(greet)
            count = count + there.astype(jnp.int32)

    own = pltpu.make_async_copy(
        vol_ref.at[:, pl.ds(x * chunks, chunks)],
        cells.at[pl.ds(mine, S), pl.ds(1, chunks), :, span],
        own_sem,
    )
    own.start()
    rims = [
        pltpu.make_async_copy(vol_ref.at[:, tile], rim.at[n], rim_sem.at[n])
        for n, tile in enumerate(((1 - x) * chunks, (2 - x) * chunks - 1))
    ]
    for copy in rims:
        copy.start()
    pl.semaphore_wait(barrier, count)

    def pair_copy(q):
        def apply(act):
            for g in range(parts):
                low = g * part + (LANES if g else 0)
                high = (g + 1) * part + (LANES if g + 1 < parts else 0)

                @pl.when(q // chunks == g)
                def _(g=g, low=low, high=high):
                    c = q - g * chunks
                    act(pltpu.make_async_remote_copy(
                        src_ref=vol_ref.at[:, (1 - x) * chunks + c, :, pl.ds(low, high - low)],
                        dst_ref=cells.at[pl.ds(mine, S), 1 + c, :, pl.ds(LANES + low, high - low)],
                        send_sem=pair_send.at[q], recv_sem=pair_recv.at[q],
                        device_id=(partner, row), device_id_type=MESH,
                    ))
        return apply

    def start(copy):
        copy.start()

    def edge_copy():
        return pltpu.make_async_remote_copy(
            src_ref=cut.at[1 + x], dst_ref=edges.at[x, x],
            send_sem=edge_send, recv_sem=edge_recv,
            device_id=(partner, row), device_id_type=MESH,
        )

    def row_copy(direction):
        return pltpu.make_async_remote_copy(
            src_ref=cut.at[3 - 3 * direction], dst_ref=edges.at[direction, x],
            send_sem=row_send.at[direction], recv_sem=row_recv.at[x],
            device_id=(first + direction, row + 1 - 2 * direction), device_id_type=MESH,
        )

    def row_arrival(source):
        return pltpu.make_async_remote_copy(
            src_ref=cut.at[0], dst_ref=edges.at[x, source],
            send_sem=row_send.at[0], recv_sem=row_recv.at[source],
            device_id=(partner, row), device_id_type=MESH,
        )

    def face_copy(direction, q):
        c, at = lax.rem(q, chunks), pl.ds(pl.multiple_of(LANES + q // chunks * part, LANES), part)
        return pltpu.make_async_remote_copy(
            src_ref=cells.at[2 * S if direction == 0 else 1, 1 + c, :, at],
            dst_ref=cells.at[0 if direction == 0 else 2 * S + 1, 1 + c, :, at],
            send_sem=face_send.at[direction, q], recv_sem=face_recv.at[direction, q],
            device_id=(me + (2 if direction == 0 else -2), row), device_id_type=MESH,
        )

    def part_copy(k, q):
        half = groups >> (k + 1)
        bit = lax.rem(z // (1 << k), 2)
        return pltpu.make_async_remote_copy(
            src_ref=held[k].at[q, pl.ds((1 - bit) * half, half)], dst_ref=came[k].at[q],
            send_sem=part_send.at[k, q], recv_sem=part_recv.at[k, q],
            device_id=(me + 2 * (1 << k) * (1 - 2 * bit), row), device_id_type=MESH,
        )

    def last_copy(q):
        return pltpu.make_async_remote_copy(
            src_ref=held[steps].at[q, 0, 1 - x], dst_ref=final.at[q],
            send_sem=last_send.at[q], recv_sem=last_recv.at[q],
            device_id=(partner, row), device_id_type=MESH,
        )

    pl.loop(0, ahead)(lambda q: pair_copy(q)(start))

    has_next_row, has_prev_row = row <= rows - 2, row >= 1
    has_next, has_prev = z <= groups - 2, z >= 1
    has_edge = jnp.logical_or(jnp.logical_and(x == 0, has_prev_row), jnp.logical_and(x == 1, has_next_row))

    own.wait()
    for copy in rims:
        copy.wait()
    for s in range(S):
        cut[2 * x, s : s + 1, :] = cells[mine + s, 1, 0:1, LANES : LANES + W]
        cut[1 + 2 * x, s : s + 1, :] = cells[mine + s, chunks, TILE - 1 : TILE, LANES : LANES + W]
        cut[2 - 2 * x, s : s + 1, :] = rim[0, s, 0:1, :]
        cut[3 - 2 * x, s : s + 1, :] = rim[1, s, TILE - 1 : TILE, :]
    edge_copy().start()
    pl.when(has_next_row)(lambda: row_copy(0).start())
    pl.when(has_prev_row)(lambda: row_copy(1).start())
    own_edge = pltpu.make_async_copy(cut.at[2 - x], edges.at[1 - x, x], own_edge_sem)
    own_edge.start()

    @pl.loop(0, 2 * S + 2)
    def _(s):
        cells[s, :, :, 0:LANES] = jnp.zeros((chunks + 2, TILE, LANES), jnp.float32)
        cells[s, :, :, LANES + W :] = jnp.zeros((chunks + 2, TILE, LANES), jnp.float32)

    @pl.when(jnp.logical_not(has_prev))
    def _():
        @pl.loop(0, chunks)
        def _(c):
            cells[0, 1 + c, :, span] = jnp.zeros((TILE, W), jnp.float32)

    @pl.when(jnp.logical_not(has_next))
    def _():
        @pl.loop(0, chunks)
        def _(c):
            cells[2 * S + 1, 1 + c, :, span] = jnp.zeros((TILE, W), jnp.float32)

    blocks, group = part // BLOCK, BLOCK // depth

    @pl.loop(0, blocks)
    def _(b):
        at = lax.broadcasted_iota(jnp.int32, (BLOCK, BLOCK), 0)
        to = lax.broadcasted_iota(jnp.int32, (BLOCK, BLOCK), 1)
        klass = to // LANES * blocks + (to % LANES // group + blocks - b) % blocks
        source = to % group * depth + klass
        spread[b] = jnp.where(at == source, 1.0, 0.0).astype(jnp.bfloat16)

    own_edge.wait()
    edge_copy().wait()
    pl.when(has_next_row)(lambda: row_copy(0).wait_send())
    pl.when(has_prev_row)(lambda: row_copy(1).wait_send())

    @pl.when(has_edge)
    def _():
        row_arrival(0).wait_recv()
        row_arrival(1).wait_recv()

    @pl.when(jnp.logical_not(has_edge))
    def _():
        edges[x] = jnp.zeros(edges.shape[1:], jnp.float32)

    for s in range(2 * S):
        cells[1 + s, 0, TILE - 1 : TILE, LANES : LANES + W] = edges[0, s // S, s % S : s % S + 1, :]
        cells[1 + s, chunks + 1, 0:1, LANES : LANES + W] = edges[1, s // S, s % S : s % S + 1, :]

    row_of = lax.broadcasted_iota(jnp.int32, (TILE, LANES), 0)
    lane_of = lax.broadcasted_iota(jnp.int32, (TILE, LANES), 1)
    is_top, is_bottom = row_of == 0, row_of == TILE - 1
    is_left, is_right = lane_of == 0, lane_of == LANES - 1
    group_of = lax.broadcasted_iota(jnp.int32, (4 * TILE, LANES), 1) // group

    def shade(q):
        t, begin = 1 + lax.rem(q, chunks), q // chunks * part

        def columns(b, carry):
            base = pl.multiple_of(begin + b * BLOCK, BLOCK)

            def lanes(v):
                return pl.ds(pl.multiple_of(base + v * LANES, LANES), LANES)

            def load(s):
                return [cells[s, t, :, lanes(v)] for v in range(BLOCK // LANES + 2)]

            zero = jnp.zeros((TILE, LANES), jnp.float32)
            sums = [[zero] * 4 for _ in range(BLOCK // LANES)]
            before, here = load(0), load(1)
            for s in range(1, 2 * S + 1):
                after = load(s + 1)
                for v in range(BLOCK // LANES):
                    both, swing, green, alpha = sums[v]
                    centre = here[v + 1]
                    left = pltpu.roll(jnp.where(is_right, here[v], centre), 1, 1)
                    right = pltpu.roll(jnp.where(is_left, here[v + 2], centre), LANES - 1, 1)
                    above = pltpu.roll(jnp.where(is_bottom, cells[s, t - 1, :, lanes(v + 1)], centre), 1, 0)
                    below = pltpu.roll(jnp.where(is_top, cells[s, t + 1, :, lanes(v + 1)], centre), TILE - 1, 0)
                    dz, dy, dx = after[v + 1] - before[v + 1], below - above, right - left
                    square = dz * dz + dy * dy + (dx * dx + 4.0)
                    facing = 1.25 * dz + dy + (0.64 / 0.48) * dx
                    shading = jnp.abs(facing) * lax.rsqrt(square) + 0.3 / 0.336
                    opacity = 1.0 - jnp.exp2(-jnp.exp2((1.5 * LOG2E) * centre + log_extinction))
                    weight = (1.0 - alpha) * opacity
                    lit = weight * shading
                    sums[v] = [
                        both + lit,
                        swing + lit * jnp.tanh(centre),
                        green + lit * jnp.exp2(centre * (centre * -LOG2E)),
                        alpha + weight,
                    ]
                before, here = here, after
            for v in range(BLOCK // LANES):
                both, swing, green, alpha = sums[v]
                both, swing = (0.5 * 0.336) * both, (0.5 * 0.336) * swing
                to = pl.ds(pl.multiple_of(b * BLOCK + v * LANES, LANES), LANES)
                for ch, value in enumerate((both + swing, 0.336 * green, both - swing, alpha)):
                    image[ch, :, to] = value
            return carry

        lax.fori_loop(0, blocks, columns, 0)
        turned = []
        for b in range(blocks):
            piece = image[:, :, b * BLOCK : (b + 1) * BLOCK].reshape(4 * TILE, BLOCK)
            high = piece.astype(jnp.bfloat16)
            low = (piece - high.astype(jnp.float32)).astype(jnp.bfloat16)
            two = jnp.dot(jnp.concatenate([high, low], axis=0), spread[b], preferred_element_type=jnp.float32)
            turned.append(two[: 4 * TILE] + two[4 * TILE :])
        for j in range(depth):
            h, r = j // blocks, j % blocks
            mixed = turned[-r % blocks][:, h * LANES : (h + 1) * LANES]
            for g in range(1, blocks):
                other = turned[(g - r) % blocks][:, h * LANES : (h + 1) * LANES]
                mixed = jnp.where(group_of == g, other, mixed)
            if r:
                mixed = pltpu.roll(mixed, LANES - group * r, 1)
            held[0][q, bit_reversed(j // 2, steps), j % 2] = mixed.reshape(4, TILE, LANES)

    def combine(k, q):
        half = groups >> (k + 1)
        bit = lax.rem(z // (1 << k), 2)
        part_copy(k, q).wait_recv()

        def join(near_of, far_of):
            for i in range(half):
                for p in range(2):
                    near, far = near_of(i, p), far_of(i, p)
                    clear = 1.0 - near[3]
                    for ch in range(4):
                        held[k + 1][q, i, p, ch] = near[ch] + clear * far[ch]

        def kept(i, p):
            return held[k][q, bit * half + i, p]

        def received(i, p):
            return came[k][q, i, p]

        pl.when(bit == 0)(lambda: join(kept, received))
        pl.when(bit == 1)(lambda: join(received, kept))

    def put(side, q, value):
        at = ((side * chunks + lax.rem(q, chunks)) * TILE) * parts + q // chunks
        for ch in range(4):
            out_ref[ch, pl.ds(at, TILE, stride=parts), :] = value[ch]

    @pl.loop(0, pieces + steps + 1)
    def _(i):
        @pl.when(i < pieces)
        def _():
            pair_copy(i)(lambda copy: copy.wait_recv())
            pl.when(i + ahead < pieces)(lambda: pair_copy(i + ahead)(start))
            pl.when(has_next)(lambda: face_copy(0, i).start())
            pl.when(has_prev)(lambda: face_copy(1, i).start())

        @pl.when(jnp.logical_and(i >= 1, i <= pieces))
        def _():
            q = i - 1
            pl.when(has_prev)(lambda: face_copy(0, q).wait_recv())
            pl.when(has_next)(lambda: face_copy(1, q).wait_recv())
            shade(q)
            part_copy(0, q).start()

        for k in range(steps):

            @pl.when(jnp.logical_and(i >= k + 2, i <= pieces + k + 1))
            def _(k=k):
                q = i - 2 - k
                combine(k, q)
                if k + 1 < steps:
                    part_copy(k + 1, q).start()
                else:
                    last_copy(q).start()
                    put(x, q, held[steps][q, 0, x])

    @pl.loop(0, pieces)
    def _(q):
        pair_copy(q)(lambda copy: copy.wait_send())
        pl.when(has_next)(lambda: face_copy(0, q).wait_send())
        pl.when(has_prev)(lambda: face_copy(1, q).wait_send())
        for k in range(steps):
            part_copy(k, q).wait_send()
        last_copy(q).wait()
        put(1 - x, q, final[q])


def local(log_density):
    S, R, W = log_density.shape
    depth, rows = lax.axis_size("depth"), lax.axis_size("rows")
    groups = depth // 2
    fits = (
        4 <= depth <= LANES
        and depth & (depth - 1) == 0
        and W % (LANES * depth) == 0
        and R % (2 * TILE) == 0
    )
    if not fits:
        return local_general(log_density)
    steps = groups.bit_length() - 1
    tiles = R // TILE
    chunks = tiles // 2
    part = LANES * depth
    parts = W // part
    pieces = parts * chunks
    F32 = jnp.float32
    partial = [pltpu.VMEM((pieces, groups >> k, 2, 4, TILE, LANES), F32) for k in range(steps + 1)]
    arrivals = [pltpu.VMEM((pieces, groups >> (k + 1), 2, 4, TILE, LANES), F32) for k in range(steps)]
    DMA = pltpu.SemaphoreType.DMA
    out = pl.pallas_call(
        functools.partial(kernel, depth, rows),
        out_shape=jax.ShapeDtypeStruct((4, R * parts, LANES), F32),
        in_specs=[pl.BlockSpec(memory_space=pl.ANY)],
        out_specs=pl.BlockSpec(memory_space=pltpu.VMEM),
        scratch_shapes=[
            pltpu.VMEM((2 * S + 2, chunks + 2, TILE, W + 2 * LANES), F32),
            pltpu.VMEM((2, 2, S, W), F32),
            pltpu.VMEM((2, S, TILE, W), F32),
            pltpu.VMEM((4, S, W), F32),
            pltpu.VMEM((part // BLOCK, BLOCK, BLOCK), jnp.bfloat16),
            pltpu.VMEM((4, TILE, part), F32),
            pltpu.VMEM((pieces, 4, TILE, LANES), F32),
            *partial,
            *arrivals,
            DMA, DMA((2,)), DMA,
            DMA((pieces,)), DMA((pieces,)),
            DMA, DMA,
            DMA((2,)), DMA((2,)),
            DMA((2, pieces)), DMA((2, pieces)),
            DMA((steps, pieces)), DMA((steps, pieces)),
            DMA((pieces,)), DMA((pieces,)),
        ],
        compiler_params=pltpu.CompilerParams(
            collective_id=0, has_side_effects=True, vmem_limit_bytes=52 * 1024 * 1024
        ),
    )(log_density.reshape(S, tiles, TILE, W))
    return out.reshape(4, R, 1, W // depth)


def solution(mesh):
    placed = (P("depth", "rows", None),)
    return jax.shard_map(
        local, mesh=mesh, in_specs=placed, out_specs=P(None, "rows", "depth", None), check_vma=False
    )
```

```python
import functools
import math

import jax
import jax.numpy as jnp
from jax import lax
from jax.experimental import pallas as pl
from jax.experimental.pallas import tpu as pltpu
from jax.sharding import PartitionSpec as P

MESH = pl.DeviceIdType.MESH
TILE = 8
LANES = 128
BLOCK = 256
AHEAD = 2
LOG2E = 1.4426950408889634


def with_halo(shard, sides, width):
    for axis, dim in sides:
        size, length = (lax.axis_size(axis), shard.shape[dim])
        up = [(i, (i + 1) % size) for i in range(size - 1)]
        down = [(j, i) for i, j in up]
        last = lax.slice_in_dim(shard, length - width, length, axis=dim)
        leading = lax.slice_in_dim(shard, 0, width, axis=dim)
        before = lax.ppermute(last, axis, up)
        after = lax.ppermute(leading, axis, down)
        shard = jnp.concatenate([before, shard, after], axis=dim)
    return shard


def shade_slab(padded, extinction, count):

    def advance(carry, index):
        accum_colour, accum_opacity = carry
        planes = lax.dynamic_slice_in_dim(padded, index, 3, 0)
        centre = planes[1, 1:-1, 1:-1]
        grad_z = 0.5 * (planes[2, 1:-1, 1:-1] - planes[0, 1:-1, 1:-1])
        grad_y = 0.5 * (planes[1, 2:, 1:-1] - planes[1, :-2, 1:-1])
        grad_x = 0.5 * (planes[1, 1:-1, 2:] - planes[1, 1:-1, :-2])
        length = jnp.sqrt(grad_z * grad_z + grad_y * grad_y + grad_x * grad_x + 1.0)
        facing = (0.6 * grad_z + 0.48 * grad_y + 0.64 * grad_x) / length
        shading = 0.3 + 0.7 * jnp.abs(facing)
        colour = (
            jnp.stack(
                [
                    jax.nn.sigmoid(2.0 * centre),
                    jnp.exp(-centre * centre),
                    jax.nn.sigmoid(-2.0 * centre),
                ]
            )
            * shading
        )
        opacity = 1.0 - jnp.exp(-extinction * jnp.exp(1.5 * centre))
        weight = (1.0 - accum_opacity) * opacity
        return ((accum_colour + weight * colour, accum_opacity + weight), None)

    height = padded.shape[1] - 2
    width = padded.shape[2] - 2
    start = (jnp.zeros((3, height, width), jnp.float32), jnp.zeros((height, width), jnp.float32))
    (colour_sum, opacity_sum), _ = lax.scan(advance, start, jnp.arange(count, dtype=jnp.int32))
    return jnp.concatenate([colour_sum, opacity_sum[None]], axis=0)


def over_pixels(nearer, farther, channel_axis):
    coverage = lax.slice_in_dim(nearer, 3, 4, axis=channel_axis)
    return nearer + (1.0 - coverage) * farther


def local_general(log_density):
    slices, row_count, width = log_density.shape
    depth_count = lax.axis_size("depth")
    classes = width // depth_count
    padded = with_halo(log_density, (("depth", 0), ("rows", 1)), 1)
    padded = jnp.pad(padded, ((0, 0), (0, 0), (1, 1)))
    image = shade_slab(padded, 0.5 / (slices * depth_count), slices)
    partial_value = image.reshape(4, row_count, classes, depth_count).transpose(0, 1, 3, 2)
    layers = lax.all_to_all(partial_value[None], "depth", split_axis=3, concat_axis=0, tiled=True)
    while layers.shape[0] > 1:
        paired = layers.reshape((layers.shape[0] // 2, 2) + layers.shape[1:])
        layers = over_pixels(paired[:, 0], paired[:, 1], 1)
    return layers[0]


def bit_reversed(value, bits):
    return sum(((value >> b) & 1) << (bits - 1 - b) for b in range(bits))


def kernel(depth, rows, vol_ref, out_ref, cells, edges, rim, cut, spread, image, final, *rest):
    S, tiles, _, W = vol_ref.shape
    chunks = tiles // 2
    groups = depth // 2
    steps = groups.bit_length() - 1
    part = LANES * depth
    parts = W // part
    pieces = parts * chunks
    ahead = min(AHEAD, pieces)
    span = pl.ds(LANES, W)
    log_extinction = math.log2(0.5 / (S * depth) * LOG2E)

    held, came = rest[: steps + 1], rest[steps + 1 : 2 * steps + 1]
    (own_sem, rim_sem, own_edge_sem, pair_send, pair_recv, edge_send, edge_recv, row_send, row_recv,
     face_send, face_recv, part_send, part_recv, last_send, last_recv) = rest[2 * steps + 1 :]

    me, row = lax.axis_index("depth"), lax.axis_index("rows")
    x, z = lax.rem(me, 2), me // 2
    first = me - x
    partner = first + 1 - x
    mine = 1 + S * x

    near = [(partner, row, None)]
    for d, there in ((-1, z >= 1), (1, z <= groups - 2)):
        near.append((me + 2 * d, row, there))
    for k in range(1, steps):
        near.append((2 * (z + (1 << k) * (1 - 2 * (lax.rem(z // (1 << k), 2)))) + x, row, None))
    for d, there in ((-1, row >= 1), (1, row <= rows - 2)):
        near.append((first, row + d, there))
        near.append((first + 1, row + d, there))
    barrier = pltpu.get_barrier_semaphore()
    count = 0
    for dd, rr, there in near:
        def greet(dd=dd, rr=rr):
            pl.semaphore_signal(barrier, inc=1, device_id=(dd, rr), device_id_type=MESH)
        if there is None:
            greet()
            count = count + 1
        else:
            pl.when(there)(greet)
            count = count + there.astype(jnp.int32)

    own = pltpu.make_async_copy(
        vol_ref.at[:, pl.ds(x * chunks, chunks)],
        cells.at[pl.ds(mine, S), pl.ds(1, chunks), :, span],
        own_sem,
    )
    own.start()
    rims = [
        pltpu.make_async_copy(vol_ref.at[:, tile], rim.at[n], rim_sem.at[n])
        for n, tile in enumerate(((1 - x) * chunks, (2 - x) * chunks - 1))
    ]
    for copy in rims:
        copy.start()
    pl.semaphore_wait(barrier, count)

    def pair_copy(q):
        def apply(act):
            for g in range(parts):
                low = g * part + (LANES if g else 0)
                high = (g + 1) * part + (LANES if g + 1 < parts else 0)

                @pl.when(q // chunks == g)
                def _(g=g, low=low, high=high):
                    c = q - g * chunks
                    act(pltpu.make_async_remote_copy(
                        src_ref=vol_ref.at[:, (1 - x) * chunks + c, :, pl.ds(low, high - low)],
                        dst_ref=cells.at[pl.ds(mine, S), 1 + c, :, pl.ds(LANES + low, high - low)],
                        send_sem=pair_send.at[q], recv_sem=pair_recv.at[q],
                        device_id=(partner, row), device_id_type=MESH,
                    ))
        return apply

    def start(copy):
        copy.start()

    def edge_copy():
        return pltpu.make_async_remote_copy(
            src_ref=cut.at[1 + x], dst_ref=edges.at[x, x],
            send_sem=edge_send, recv_sem=edge_recv,
            device_id=(partner, row), device_id_type=MESH,
        )

    def row_copy(direction):
        return pltpu.make_async_remote_copy(
            src_ref=cut.at[3 - 3 * direction], dst_ref=edges.at[direction, x],
            send_sem=row_send.at[direction], recv_sem=row_recv.at[x],
            device_id=(first + direction, row + 1 - 2 * direction), device_id_type=MESH,
        )

    def row_arrival(source):
        return pltpu.make_async_remote_copy(
            src_ref=cut.at[0], dst_ref=edges.at[x, source],
            send_sem=row_send.at[0], recv_sem=row_recv.at[source],
            device_id=(partner, row), device_id_type=MESH,
        )

    def face_copy(direction, q):
        c, at = lax.rem(q, chunks), pl.ds(pl.multiple_of(LANES + q // chunks * part, LANES), part)
        return pltpu.make_async_remote_copy(
            src_ref=cells.at[2 * S if direction == 0 else 1, 1 + c, :, at],
            dst_ref=cells.at[0 if direction == 0 else 2 * S + 1, 1 + c, :, at],
            send_sem=face_send.at[direction, q], recv_sem=face_recv.at[direction, q],
            device_id=(me + (2 if direction == 0 else -2), row), device_id_type=MESH,
        )

    def part_copy(k, q):
        half = groups >> (k + 1)
        bit = lax.rem(z // (1 << k), 2)
        return pltpu.make_async_remote_copy(
            src_ref=held[k].at[q, pl.ds((1 - bit) * half, half)], dst_ref=came[k].at[q],
            send_sem=part_send.at[k, q], recv_sem=part_recv.at[k, q],
            device_id=(me + 2 * (1 << k) * (1 - 2 * bit), row), device_id_type=MESH,
        )

    def last_copy(q):
        return pltpu.make_async_remote_copy(
            src_ref=held[steps].at[q, 0, 1 - x], dst_ref=final.at[q],
            send_sem=last_send.at[q], recv_sem=last_recv.at[q],
            device_id=(partner, row), device_id_type=MESH,
        )

    pl.loop(0, ahead)(lambda q: pair_copy(q)(start))

    has_next_row, has_prev_row = row <= rows - 2, row >= 1
    has_next, has_prev = z <= groups - 2, z >= 1
    has_edge = jnp.logical_or(jnp.logical_and(x == 0, has_prev_row), jnp.logical_and(x == 1, has_next_row))

    own.wait()
    for copy in rims:
        copy.wait()
    for s in range(S):
        cut[2 * x, s : s + 1, :] = cells[mine + s, 1, 0:1, LANES : LANES + W]
        cut[1 + 2 * x, s : s + 1, :] = cells[mine + s, chunks, TILE - 1 : TILE, LANES : LANES + W]
        cut[2 - 2 * x, s : s + 1, :] = rim[0, s, 0:1, :]
        cut[3 - 2 * x, s : s + 1, :] = rim[1, s, TILE - 1 : TILE, :]
    edge_copy().start()
    pl.when(has_next_row)(lambda: row_copy(0).start())
    pl.when(has_prev_row)(lambda: row_copy(1).start())
    own_edge = pltpu.make_async_copy(cut.at[2 - x], edges.at[1 - x, x], own_edge_sem)
    own_edge.start()

    @pl.loop(0, 2 * S + 2)
    def _(s):
        cells[s, :, :, 0:LANES] = jnp.zeros((chunks + 2, TILE, LANES), jnp.float32)
        cells[s, :, :, LANES + W :] = jnp.zeros((chunks + 2, TILE, LANES), jnp.float32)

    @pl.when(jnp.logical_not(has_prev))
    def _():
        @pl.loop(0, chunks)
        def _(c):
            cells[0, 1 + c, :, span] = jnp.zeros((TILE, W), jnp.float32)

    @pl.when(jnp.logical_not(has_next))
    def _():
        @pl.loop(0, chunks)
        def _(c):
            cells[2 * S + 1, 1 + c, :, span] = jnp.zeros((TILE, W), jnp.float32)

    blocks, group = part // BLOCK, BLOCK // depth

    @pl.loop(0, blocks)
    def _(b):
        at = lax.broadcasted_iota(jnp.int32, (BLOCK, BLOCK), 0)
        to = lax.broadcasted_iota(jnp.int32, (BLOCK, BLOCK), 1)
        klass = to // LANES * blocks + (to % LANES // group + blocks - b) % blocks
        source = to % group * depth + klass
        spread[b] = jnp.where(at == source, 1.0, 0.0).astype(jnp.bfloat16)

    own_edge.wait()
    edge_copy().wait()
    pl.when(has_next_row)(lambda: row_copy(0).wait_send())
    pl.when(has_prev_row)(lambda: row_copy(1).wait_send())

    @pl.when(has_edge)
    def _():
        row_arrival(0).wait_recv()
        row_arrival(1).wait_recv()

    @pl.when(jnp.logical_not(has_edge))
    def _():
        edges[x] = jnp.zeros(edges.shape[1:], jnp.float32)

    for s in range(2 * S):
        cells[1 + s, 0, TILE - 1 : TILE, LANES : LANES + W] = edges[0, s // S, s % S : s % S + 1, :]
        cells[1 + s, chunks + 1, 0:1, LANES : LANES + W] = edges[1, s // S, s % S : s % S + 1, :]

    row_of = lax.broadcasted_iota(jnp.int32, (TILE, LANES), 0)
    lane_of = lax.broadcasted_iota(jnp.int32, (TILE, LANES), 1)
    is_top, is_bottom = row_of == 0, row_of == TILE - 1
    is_left, is_right = lane_of == 0, lane_of == LANES - 1
    group_of = lax.broadcasted_iota(jnp.int32, (4 * TILE, LANES), 1) // group

    def shade(q):
        t, begin = 1 + lax.rem(q, chunks), q // chunks * part

        def columns(b, carry):
            base = pl.multiple_of(begin + b * BLOCK, BLOCK)

            def lanes(v):
                return pl.ds(pl.multiple_of(base + v * LANES, LANES), LANES)

            def load(s):
                return [cells[s, t, :, lanes(v)] for v in range(BLOCK // LANES + 2)]

            zero = jnp.zeros((TILE, LANES), jnp.float32)
            sums = [[zero] * 4 for _ in range(BLOCK // LANES)]
            before, here = load(0), load(1)
            for s in range(1, 2 * S + 1):
                after = load(s + 1)
                for v in range(BLOCK // LANES):
                    both, swing, green, alpha = sums[v]
                    centre = here[v + 1]
                    left = pltpu.roll(jnp.where(is_right, here[v], centre), 1, 1)
                    right = pltpu.roll(jnp.where(is_left, here[v + 2], centre), LANES - 1, 1)
                    above = pltpu.roll(jnp.where(is_bottom, cells[s, t - 1, :, lanes(v + 1)], centre), 1, 0)
                    below = pltpu.roll(jnp.where(is_top, cells[s, t + 1, :, lanes(v + 1)], centre), TILE - 1, 0)
                    dz, dy, dx = after[v + 1] - before[v + 1], below - above, right - left
                    square = dz * dz + dy * dy + (dx * dx + 4.0)
                    facing = 1.25 * dz + dy + (0.64 / 0.48) * dx
                    shading = jnp.abs(facing) * lax.rsqrt(square) + 0.3 / 0.336
                    opacity = 1.0 - jnp.exp2(-jnp.exp2((1.5 * LOG2E) * centre + log_extinction))
                    weight = (1.0 - alpha) * opacity
                    lit = weight * shading
                    sums[v] = [
                        both + lit,
                        swing + lit * jnp.tanh(centre),
                        green + lit * jnp.exp2(centre * (centre * -LOG2E)),
                        alpha + weight,
                    ]
                before, here = here, after
            for v in range(BLOCK // LANES):
                both, swing, green, alpha = sums[v]
                both, swing = (0.5 * 0.336) * both, (0.5 * 0.336) * swing
                to = pl.ds(pl.multiple_of(b * BLOCK + v * LANES, LANES), LANES)
                for ch, value in enumerate((both + swing, 0.336 * green, both - swing, alpha)):
                    image[ch, :, to] = value
            return carry

        lax.fori_loop(0, blocks, columns, 0)
        turned = []
        for b in range(blocks):
            piece = image[:, :, b * BLOCK : (b + 1) * BLOCK].reshape(4 * TILE, BLOCK)
            high = piece.astype(jnp.bfloat16)
            low = (piece - high.astype(jnp.float32)).astype(jnp.bfloat16)
            two = jnp.dot(jnp.concatenate([high, low], axis=0), spread[b], preferred_element_type=jnp.float32)
            turned.append(two[: 4 * TILE] + two[4 * TILE :])
        for j in range(depth):
            h, r = j // blocks, j % blocks
            mixed = turned[-r % blocks][:, h * LANES : (h + 1) * LANES]
            for g in range(1, blocks):
                other = turned[(g - r) % blocks][:, h * LANES : (h + 1) * LANES]
                mixed = jnp.where(group_of == g, other, mixed)
            if r:
                mixed = pltpu.roll(mixed, LANES - group * r, 1)
            held[0][q, bit_reversed(j // 2, steps), j % 2] = mixed.reshape(4, TILE, LANES)

    def combine(k, q):
        half = groups >> (k + 1)
        bit = lax.rem(z // (1 << k), 2)
        part_copy(k, q).wait_recv()

        def join(near_of, far_of):
            for i in range(half):
                for p in range(2):
                    near, far = near_of(i, p), far_of(i, p)
                    clear = 1.0 - near[3]
                    for ch in range(4):
                        held[k + 1][q, i, p, ch] = near[ch] + clear * far[ch]

        def kept(i, p):
            return held[k][q, bit * half + i, p]

        def received(i, p):
            return came[k][q, i, p]

        pl.when(bit == 0)(lambda: join(kept, received))
        pl.when(bit == 1)(lambda: join(received, kept))

    def put(side, q, value):
        at = ((side * chunks + lax.rem(q, chunks)) * TILE) * parts + q // chunks
        for ch in range(4):
            out_ref[ch, pl.ds(at, TILE, stride=parts), :] = value[ch]

    @pl.loop(0, pieces + steps + 2)
    def _(i):
        @pl.when(i < pieces)
        def _():
            pair_copy(i)(lambda copy: copy.wait_recv())
            pl.when(i + ahead < pieces)(lambda: pair_copy(i + ahead)(start))
            pl.when(has_next)(lambda: face_copy(0, i).start())
            pl.when(has_prev)(lambda: face_copy(1, i).start())

        @pl.when(jnp.logical_and(i >= 1, i <= pieces))
        def _():
            q = i - 1
            pl.when(has_prev)(lambda: face_copy(0, q).wait_recv())
            pl.when(has_next)(lambda: face_copy(1, q).wait_recv())
            shade(q)
            part_copy(0, q).start()

        for k in range(steps):

            @pl.when(jnp.logical_and(i >= k + 2, i <= pieces + k + 1))
            def _(k=k):
                q = i - 2 - k
                combine(k, q)
                if k + 1 < steps:
                    part_copy(k + 1, q).start()
                else:
                    last_copy(q).start()
                    put(x, q, held[steps][q, 0, x])

        @pl.when(i >= steps + 2)
        def _():
            q = i - steps - 2
            pair_copy(q)(lambda copy: copy.wait_send())
            pl.when(has_next)(lambda: face_copy(0, q).wait_send())
            pl.when(has_prev)(lambda: face_copy(1, q).wait_send())
            for k in range(steps):
                part_copy(k, q).wait_send()
            last_copy(q).wait()
            put(1 - x, q, final[q])


def local(log_density):
    S, R, W = log_density.shape
    depth, rows = lax.axis_size("depth"), lax.axis_size("rows")
    groups = depth // 2
    fits = (
        4 <= depth <= LANES
        and depth & (depth - 1) == 0
        and W % (LANES * depth) == 0
        and R % (2 * TILE) == 0
    )
    if not fits:
        return local_general(log_density)
    steps = groups.bit_length() - 1
    tiles = R // TILE
    chunks = tiles // 2
    part = LANES * depth
    parts = W // part
    pieces = parts * chunks
    F32 = jnp.float32
    partial = [pltpu.VMEM((pieces, groups >> k, 2, 4, TILE, LANES), F32) for k in range(steps + 1)]
    arrivals = [pltpu.VMEM((pieces, groups >> (k + 1), 2, 4, TILE, LANES), F32) for k in range(steps)]
    DMA = pltpu.SemaphoreType.DMA
    out = pl.pallas_call(
        functools.partial(kernel, depth, rows),
        out_shape=jax.ShapeDtypeStruct((4, R * parts, LANES), F32),
        in_specs=[pl.BlockSpec(memory_space=pl.ANY)],
        out_specs=pl.BlockSpec(memory_space=pltpu.VMEM),
        scratch_shapes=[
            pltpu.VMEM((2 * S + 2, chunks + 2, TILE, W + 2 * LANES), F32),
            pltpu.VMEM((2, 2, S, W), F32),
            pltpu.VMEM((2, S, TILE, W), F32),
            pltpu.VMEM((4, S, W), F32),
            pltpu.VMEM((part // BLOCK, BLOCK, BLOCK), jnp.bfloat16),
            pltpu.VMEM((4, TILE, part), F32),
            pltpu.VMEM((pieces, 4, TILE, LANES), F32),
            *partial,
            *arrivals,
            DMA, DMA((2,)), DMA,
            DMA((pieces,)), DMA((pieces,)),
            DMA, DMA,
            DMA((2,)), DMA((2,)),
            DMA((2, pieces)), DMA((2, pieces)),
            DMA((steps, pieces)), DMA((steps, pieces)),
            DMA((pieces,)), DMA((pieces,)),
        ],
        compiler_params=pltpu.CompilerParams(
            collective_id=0, has_side_effects=True, vmem_limit_bytes=52 * 1024 * 1024
        ),
    )(log_density.reshape(S, tiles, TILE, W))
    return out.reshape(4, R, 1, W // depth)


def solution(mesh):
    placed = (P("depth", "rows", None),)
    return jax.shard_map(
        local, mesh=mesh, in_specs=placed, out_specs=P(None, "rows", "depth", None), check_vma=False
    )
```

```python
import functools
import math

import jax
import jax.numpy as jnp
from jax import lax
from jax.experimental import pallas as pl
from jax.experimental.pallas import tpu as pltpu
from jax.sharding import PartitionSpec as P

MESH = pl.DeviceIdType.MESH
TILE = 8
LANES = 128
BLOCK = 256
SPAN = 512
AHEAD = 2
LOG2E = 1.4426950408889634


def with_halo(shard, sides, width):
    for axis, dim in sides:
        size, length = (lax.axis_size(axis), shard.shape[dim])
        up = [(i, (i + 1) % size) for i in range(size - 1)]
        down = [(j, i) for i, j in up]
        last = lax.slice_in_dim(shard, length - width, length, axis=dim)
        leading = lax.slice_in_dim(shard, 0, width, axis=dim)
        before = lax.ppermute(last, axis, up)
        after = lax.ppermute(leading, axis, down)
        shard = jnp.concatenate([before, shard, after], axis=dim)
    return shard


def shade_slab(padded, extinction, count):

    def advance(carry, index):
        accum_colour, accum_opacity = carry
        planes = lax.dynamic_slice_in_dim(padded, index, 3, 0)
        centre = planes[1, 1:-1, 1:-1]
        grad_z = 0.5 * (planes[2, 1:-1, 1:-1] - planes[0, 1:-1, 1:-1])
        grad_y = 0.5 * (planes[1, 2:, 1:-1] - planes[1, :-2, 1:-1])
        grad_x = 0.5 * (planes[1, 1:-1, 2:] - planes[1, 1:-1, :-2])
        length = jnp.sqrt(grad_z * grad_z + grad_y * grad_y + grad_x * grad_x + 1.0)
        facing = (0.6 * grad_z + 0.48 * grad_y + 0.64 * grad_x) / length
        shading = 0.3 + 0.7 * jnp.abs(facing)
        colour = (
            jnp.stack(
                [
                    jax.nn.sigmoid(2.0 * centre),
                    jnp.exp(-centre * centre),
                    jax.nn.sigmoid(-2.0 * centre),
                ]
            )
            * shading
        )
        opacity = 1.0 - jnp.exp(-extinction * jnp.exp(1.5 * centre))
        weight = (1.0 - accum_opacity) * opacity
        return ((accum_colour + weight * colour, accum_opacity + weight), None)

    height = padded.shape[1] - 2
    width = padded.shape[2] - 2
    start = (jnp.zeros((3, height, width), jnp.float32), jnp.zeros((height, width), jnp.float32))
    (colour_sum, opacity_sum), _ = lax.scan(advance, start, jnp.arange(count, dtype=jnp.int32))
    return jnp.concatenate([colour_sum, opacity_sum[None]], axis=0)


def over_pixels(nearer, farther, channel_axis):
    coverage = lax.slice_in_dim(nearer, 3, 4, axis=channel_axis)
    return nearer + (1.0 - coverage) * farther


def local_general(log_density):
    slices, row_count, width = log_density.shape
    depth_count = lax.axis_size("depth")
    classes = width // depth_count
    padded = with_halo(log_density, (("depth", 0), ("rows", 1)), 1)
    padded = jnp.pad(padded, ((0, 0), (0, 0), (1, 1)))
    image = shade_slab(padded, 0.5 / (slices * depth_count), slices)
    partial_value = image.reshape(4, row_count, classes, depth_count).transpose(0, 1, 3, 2)
    layers = lax.all_to_all(partial_value[None], "depth", split_axis=3, concat_axis=0, tiled=True)
    while layers.shape[0] > 1:
        paired = layers.reshape((layers.shape[0] // 2, 2) + layers.shape[1:])
        layers = over_pixels(paired[:, 0], paired[:, 1], 1)
    return layers[0]


def bit_reversed(value, bits):
    return sum(((value >> b) & 1) << (bits - 1 - b) for b in range(bits))


def kernel(depth, rows, vol_ref, out_ref, cells, edges, rim, cut, spread, image, final, *rest):
    S, tiles, _, W = vol_ref.shape
    chunks = tiles // 2
    groups = depth // 2
    steps = groups.bit_length() - 1
    part = LANES * depth
    parts = W // part
    pieces = parts * chunks
    ahead = min(AHEAD, pieces)
    span = pl.ds(LANES, W)
    log_extinction = math.log2(0.5 / (S * depth) * LOG2E)

    held, came = rest[: steps + 1], rest[steps + 1 : 2 * steps + 1]
    (own_sem, rim_sem, own_edge_sem, pair_send, pair_recv, edge_send, edge_recv, row_send, row_recv,
     face_send, face_recv, part_send, part_recv, last_send, last_recv) = rest[2 * steps + 1 :]

    me, row = lax.axis_index("depth"), lax.axis_index("rows")
    x, z = lax.rem(me, 2), me // 2
    first = me - x
    partner = first + 1 - x
    mine = 1 + S * x

    near = [(partner, row, None)]
    for d, there in ((-1, z >= 1), (1, z <= groups - 2)):
        near.append((me + 2 * d, row, there))
    for k in range(1, steps):
        near.append((2 * (z + (1 << k) * (1 - 2 * (lax.rem(z // (1 << k), 2)))) + x, row, None))
    for d, there in ((-1, row >= 1), (1, row <= rows - 2)):
        near.append((first, row + d, there))
        near.append((first + 1, row + d, there))
    barrier = pltpu.get_barrier_semaphore()
    count = 0
    for dd, rr, there in near:
        def greet(dd=dd, rr=rr):
            pl.semaphore_signal(barrier, inc=1, device_id=(dd, rr), device_id_type=MESH)
        if there is None:
            greet()
            count = count + 1
        else:
            pl.when(there)(greet)
            count = count + there.astype(jnp.int32)

    own = pltpu.make_async_copy(
        vol_ref.at[:, pl.ds(x * chunks, chunks)],
        cells.at[pl.ds(mine, S), pl.ds(1, chunks), :, span],
        own_sem,
    )
    own.start()
    rims = [
        pltpu.make_async_copy(vol_ref.at[:, tile], rim.at[n], rim_sem.at[n])
        for n, tile in enumerate(((1 - x) * chunks, (2 - x) * chunks - 1))
    ]
    for copy in rims:
        copy.start()
    pl.semaphore_wait(barrier, count)

    def pair_copy(q):
        def apply(act):
            for g in range(parts):
                low = g * part + (LANES if g else 0)
                high = (g + 1) * part + (LANES if g + 1 < parts else 0)

                @pl.when(q // chunks == g)
                def _(g=g, low=low, high=high):
                    c = q - g * chunks
                    act(pltpu.make_async_remote_copy(
                        src_ref=vol_ref.at[:, (1 - x) * chunks + c, :, pl.ds(low, high - low)],
                        dst_ref=cells.at[pl.ds(mine, S), 1 + c, :, pl.ds(LANES + low, high - low)],
                        send_sem=pair_send.at[q], recv_sem=pair_recv.at[q],
                        device_id=(partner, row), device_id_type=MESH,
                    ))
        return apply

    def start(copy):
        copy.start()

    def edge_copy():
        return pltpu.make_async_remote_copy(
            src_ref=cut.at[1 + x], dst_ref=edges.at[x, x],
            send_sem=edge_send, recv_sem=edge_recv,
            device_id=(partner, row), device_id_type=MESH,
        )

    def row_copy(direction):
        return pltpu.make_async_remote_copy(
            src_ref=cut.at[3 - 3 * direction], dst_ref=edges.at[direction, x],
            send_sem=row_send.at[direction], recv_sem=row_recv.at[x],
            device_id=(first + direction, row + 1 - 2 * direction), device_id_type=MESH,
        )

    def row_arrival(source):
        return pltpu.make_async_remote_copy(
            src_ref=cut.at[0], dst_ref=edges.at[x, source],
            send_sem=row_send.at[0], recv_sem=row_recv.at[source],
            device_id=(partner, row), device_id_type=MESH,
        )

    def face_copy(direction, q):
        c, at = lax.rem(q, chunks), pl.ds(pl.multiple_of(LANES + q // chunks * part, LANES), part)
        return pltpu.make_async_remote_copy(
            src_ref=cells.at[2 * S if direction == 0 else 1, 1 + c, :, at],
            dst_ref=cells.at[0 if direction == 0 else 2 * S + 1, 1 + c, :, at],
            send_sem=face_send.at[direction, q], recv_sem=face_recv.at[direction, q],
            device_id=(me + (2 if direction == 0 else -2), row), device_id_type=MESH,
        )

    def part_copy(k, q):
        half = groups >> (k + 1)
        bit = lax.rem(z // (1 << k), 2)
        return pltpu.make_async_remote_copy(
            src_ref=held[k].at[q, pl.ds((1 - bit) * half, half)], dst_ref=came[k].at[q],
            send_sem=part_send.at[k, q], recv_sem=part_recv.at[k, q],
            device_id=(me + 2 * (1 << k) * (1 - 2 * bit), row), device_id_type=MESH,
        )

    def last_copy(q):
        return pltpu.make_async_remote_copy(
            src_ref=held[steps].at[q, 0, 1 - x], dst_ref=final.at[q],
            send_sem=last_send.at[q], recv_sem=last_recv.at[q],
            device_id=(partner, row), device_id_type=MESH,
        )

    pl.loop(0, ahead)(lambda q: pair_copy(q)(start))

    has_next_row, has_prev_row = row <= rows - 2, row >= 1
    has_next, has_prev = z <= groups - 2, z >= 1
    has_edge = jnp.logical_or(jnp.logical_and(x == 0, has_prev_row), jnp.logical_and(x == 1, has_next_row))

    own.wait()
    for copy in rims:
        copy.wait()
    for s in range(S):
        cut[2 * x, s : s + 1, :] = cells[mine + s, 1, 0:1, LANES : LANES + W]
        cut[1 + 2 * x, s : s + 1, :] = cells[mine + s, chunks, TILE - 1 : TILE, LANES : LANES + W]
        cut[2 - 2 * x, s : s + 1, :] = rim[0, s, 0:1, :]
        cut[3 - 2 * x, s : s + 1, :] = rim[1, s, TILE - 1 : TILE, :]
    edge_copy().start()
    pl.when(has_next_row)(lambda: row_copy(0).start())
    pl.when(has_prev_row)(lambda: row_copy(1).start())
    own_edge = pltpu.make_async_copy(cut.at[2 - x], edges.at[1 - x, x], own_edge_sem)
    own_edge.start()

    @pl.loop(0, 2 * S + 2)
    def _(s):
        cells[s, :, :, 0:LANES] = jnp.zeros((chunks + 2, TILE, LANES), jnp.float32)
        cells[s, :, :, LANES + W :] = jnp.zeros((chunks + 2, TILE, LANES), jnp.float32)

    @pl.when(jnp.logical_not(has_prev))
    def _():
        @pl.loop(0, chunks)
        def _(c):
            cells[0, 1 + c, :, span] = jnp.zeros((TILE, W), jnp.float32)

    @pl.when(jnp.logical_not(has_next))
    def _():
        @pl.loop(0, chunks)
        def _(c):
            cells[2 * S + 1, 1 + c, :, span] = jnp.zeros((TILE, W), jnp.float32)

    blocks, group = part // BLOCK, BLOCK // depth

    @pl.loop(0, blocks)
    def _(b):
        at = lax.broadcasted_iota(jnp.int32, (BLOCK, BLOCK), 0)
        to = lax.broadcasted_iota(jnp.int32, (BLOCK, BLOCK), 1)
        klass = to // LANES * blocks + (to % LANES // group + blocks - b) % blocks
        source = to % group * depth + klass
        spread[b] = jnp.where(at == source, 1.0, 0.0).astype(jnp.bfloat16)

    own_edge.wait()
    edge_copy().wait()
    pl.when(has_next_row)(lambda: row_copy(0).wait_send())
    pl.when(has_prev_row)(lambda: row_copy(1).wait_send())

    @pl.when(has_edge)
    def _():
        row_arrival(0).wait_recv()
        row_arrival(1).wait_recv()

    @pl.when(jnp.logical_not(has_edge))
    def _():
        edges[x] = jnp.zeros(edges.shape[1:], jnp.float32)

    for s in range(2 * S):
        cells[1 + s, 0, TILE - 1 : TILE, LANES : LANES + W] = edges[0, s // S, s % S : s % S + 1, :]
        cells[1 + s, chunks + 1, 0:1, LANES : LANES + W] = edges[1, s // S, s % S : s % S + 1, :]

    row_of = lax.broadcasted_iota(jnp.int32, (TILE, LANES), 0)
    lane_of = lax.broadcasted_iota(jnp.int32, (TILE, LANES), 1)
    is_top, is_bottom = row_of == 0, row_of == TILE - 1
    is_left, is_right = lane_of == 0, lane_of == LANES - 1
    group_of = lax.broadcasted_iota(jnp.int32, (4 * TILE, LANES), 1) // group

    def shade(q):
        t, begin = 1 + lax.rem(q, chunks), q // chunks * part

        def columns(b, carry):
            base = pl.multiple_of(begin + b * SPAN, SPAN)

            def lanes(v):
                return pl.ds(pl.multiple_of(base + v * LANES, LANES), LANES)

            def load(s):
                return [cells[s, t, :, lanes(v)] for v in range(SPAN // LANES + 2)]

            zero = jnp.zeros((TILE, LANES), jnp.float32)
            sums = [[zero] * 4 for _ in range(SPAN // LANES)]
            before, here = load(0), load(1)
            for s in range(1, 2 * S + 1):
                after = load(s + 1)
                for v in range(SPAN // LANES):
                    both, swing, green, alpha = sums[v]
                    centre = here[v + 1]
                    left = pltpu.roll(jnp.where(is_right, here[v], centre), 1, 1)
                    right = pltpu.roll(jnp.where(is_left, here[v + 2], centre), LANES - 1, 1)
                    above = pltpu.roll(jnp.where(is_bottom, cells[s, t - 1, :, lanes(v + 1)], centre), 1, 0)
                    below = pltpu.roll(jnp.where(is_top, cells[s, t + 1, :, lanes(v + 1)], centre), TILE - 1, 0)
                    dz, dy, dx = after[v + 1] - before[v + 1], below - above, right - left
                    square = dz * dz + dy * dy + (dx * dx + 4.0)
                    facing = 1.25 * dz + dy + (0.64 / 0.48) * dx
                    shading = jnp.abs(facing) * lax.rsqrt(square) + 0.3 / 0.336
                    opacity = 1.0 - jnp.exp2(-jnp.exp2((1.5 * LOG2E) * centre + log_extinction))
                    weight = (1.0 - alpha) * opacity
                    lit = weight * shading
                    sums[v] = [
                        both + lit,
                        swing + lit * jnp.tanh(centre),
                        green + lit * jnp.exp2(centre * (centre * -LOG2E)),
                        alpha + weight,
                    ]
                before, here = here, after
            for v in range(SPAN // LANES):
                both, swing, green, alpha = sums[v]
                both, swing = (0.5 * 0.336) * both, (0.5 * 0.336) * swing
                to = pl.ds(pl.multiple_of(b * SPAN + v * LANES, LANES), LANES)
                for ch, value in enumerate((both + swing, 0.336 * green, both - swing, alpha)):
                    image[ch, :, to] = value
            return carry

        lax.fori_loop(0, part // SPAN, columns, 0)
        turned = []
        for b in range(blocks):
            piece = image[:, :, b * BLOCK : (b + 1) * BLOCK].reshape(4 * TILE, BLOCK)
            high = piece.astype(jnp.bfloat16)
            low = (piece - high.astype(jnp.float32)).astype(jnp.bfloat16)
            two = jnp.dot(jnp.concatenate([high, low], axis=0), spread[b], preferred_element_type=jnp.float32)
            turned.append(two[: 4 * TILE] + two[4 * TILE :])
        for j in range(depth):
            h, r = j // blocks, j % blocks
            mixed = turned[-r % blocks][:, h * LANES : (h + 1) * LANES]
            for g in range(1, blocks):
                other = turned[(g - r) % blocks][:, h * LANES : (h + 1) * LANES]
                mixed = jnp.where(group_of == g, other, mixed)
            if r:
                mixed = pltpu.roll(mixed, LANES - group * r, 1)
            held[0][q, bit_reversed(j // 2, steps), j % 2] = mixed.reshape(4, TILE, LANES)

    def combine(k, q):
        half = groups >> (k + 1)
        bit = lax.rem(z // (1 << k), 2)
        part_copy(k, q).wait_recv()

        def join(near_of, far_of):
            for i in range(half):
                for p in range(2):
                    near, far = near_of(i, p), far_of(i, p)
                    clear = 1.0 - near[3]
                    for ch in range(4):
                        held[k + 1][q, i, p, ch] = near[ch] + clear * far[ch]

        def kept(i, p):
            return held[k][q, bit * half + i, p]

        def received(i, p):
            return came[k][q, i, p]

        pl.when(bit == 0)(lambda: join(kept, received))
        pl.when(bit == 1)(lambda: join(received, kept))

    def put(side, q, value):
        at = ((side * chunks + lax.rem(q, chunks)) * TILE) * parts + q // chunks
        for ch in range(4):
            out_ref[ch, pl.ds(at, TILE, stride=parts), :] = value[ch]

    @pl.loop(0, pieces + steps + 1)
    def _(i):
        @pl.when(i < pieces)
        def _():
            pair_copy(i)(lambda copy: copy.wait_recv())
            pl.when(i + ahead < pieces)(lambda: pair_copy(i + ahead)(start))
            pl.when(has_next)(lambda: face_copy(0, i).start())
            pl.when(has_prev)(lambda: face_copy(1, i).start())

        @pl.when(jnp.logical_and(i >= 1, i <= pieces))
        def _():
            q = i - 1
            pl.when(has_prev)(lambda: face_copy(0, q).wait_recv())
            pl.when(has_next)(lambda: face_copy(1, q).wait_recv())
            shade(q)
            part_copy(0, q).start()

        for k in range(steps):

            @pl.when(jnp.logical_and(i >= k + 2, i <= pieces + k + 1))
            def _(k=k):
                q = i - 2 - k
                combine(k, q)
                if k + 1 < steps:
                    part_copy(k + 1, q).start()
                else:
                    last_copy(q).start()
                    put(x, q, held[steps][q, 0, x])

    @pl.loop(0, pieces)
    def _(q):
        pair_copy(q)(lambda copy: copy.wait_send())
        pl.when(has_next)(lambda: face_copy(0, q).wait_send())
        pl.when(has_prev)(lambda: face_copy(1, q).wait_send())
        for k in range(steps):
            part_copy(k, q).wait_send()
        last_copy(q).wait()
        put(1 - x, q, final[q])


def local(log_density):
    S, R, W = log_density.shape
    depth, rows = lax.axis_size("depth"), lax.axis_size("rows")
    groups = depth // 2
    fits = (
        4 <= depth <= LANES
        and (LANES * depth) % SPAN == 0
        and depth & (depth - 1) == 0
        and W % (LANES * depth) == 0
        and R % (2 * TILE) == 0
    )
    if not fits:
        return local_general(log_density)
    steps = groups.bit_length() - 1
    tiles = R // TILE
    chunks = tiles // 2
    part = LANES * depth
    parts = W // part
    pieces = parts * chunks
    F32 = jnp.float32
    partial = [pltpu.VMEM((pieces, groups >> k, 2, 4, TILE, LANES), F32) for k in range(steps + 1)]
    arrivals = [pltpu.VMEM((pieces, groups >> (k + 1), 2, 4, TILE, LANES), F32) for k in range(steps)]
    DMA = pltpu.SemaphoreType.DMA
    out = pl.pallas_call(
        functools.partial(kernel, depth, rows),
        out_shape=jax.ShapeDtypeStruct((4, R * parts, LANES), F32),
        in_specs=[pl.BlockSpec(memory_space=pl.ANY)],
        out_specs=pl.BlockSpec(memory_space=pltpu.VMEM),
        scratch_shapes=[
            pltpu.VMEM((2 * S + 2, chunks + 2, TILE, W + 2 * LANES), F32),
            pltpu.VMEM((2, 2, S, W), F32),
            pltpu.VMEM((2, S, TILE, W), F32),
            pltpu.VMEM((4, S, W), F32),
            pltpu.VMEM((part // BLOCK, BLOCK, BLOCK), jnp.bfloat16),
            pltpu.VMEM((4, TILE, part), F32),
            pltpu.VMEM((pieces, 4, TILE, LANES), F32),
            *partial,
            *arrivals,
            DMA, DMA((2,)), DMA,
            DMA((pieces,)), DMA((pieces,)),
            DMA, DMA,
            DMA((2,)), DMA((2,)),
            DMA((2, pieces)), DMA((2, pieces)),
            DMA((steps, pieces)), DMA((steps, pieces)),
            DMA((pieces,)), DMA((pieces,)),
        ],
        compiler_params=pltpu.CompilerParams(
            collective_id=0, has_side_effects=True, vmem_limit_bytes=52 * 1024 * 1024
        ),
    )(log_density.reshape(S, tiles, TILE, W))
    return out.reshape(4, R, 1, W // depth)


def solution(mesh):
    placed = (P("depth", "rows", None),)
    return jax.shard_map(
        local, mesh=mesh, in_specs=placed, out_specs=P(None, "rows", "depth", None), check_vma=False
    )
```

```python
import functools
import math

import jax
import jax.numpy as jnp
from jax import lax
from jax.experimental import pallas as pl
from jax.experimental.pallas import tpu as pltpu
from jax.sharding import PartitionSpec as P

MESH = pl.DeviceIdType.MESH
TILE = 8
LANES = 128
BLOCK = 256
SPAN = 512
AHEAD = 2
LOG2E = 1.4426950408889634


def with_halo(shard, sides, width):
    for axis, dim in sides:
        size, length = (lax.axis_size(axis), shard.shape[dim])
        up = [(i, (i + 1) % size) for i in range(size - 1)]
        down = [(j, i) for i, j in up]
        last = lax.slice_in_dim(shard, length - width, length, axis=dim)
        leading = lax.slice_in_dim(shard, 0, width, axis=dim)
        before = lax.ppermute(last, axis, up)
        after = lax.ppermute(leading, axis, down)
        shard = jnp.concatenate([before, shard, after], axis=dim)
    return shard


def shade_slab(padded, extinction, count):

    def advance(carry, index):
        accum_colour, accum_opacity = carry
        planes = lax.dynamic_slice_in_dim(padded, index, 3, 0)
        centre = planes[1, 1:-1, 1:-1]
        grad_z = 0.5 * (planes[2, 1:-1, 1:-1] - planes[0, 1:-1, 1:-1])
        grad_y = 0.5 * (planes[1, 2:, 1:-1] - planes[1, :-2, 1:-1])
        grad_x = 0.5 * (planes[1, 1:-1, 2:] - planes[1, 1:-1, :-2])
        length = jnp.sqrt(grad_z * grad_z + grad_y * grad_y + grad_x * grad_x + 1.0)
        facing = (0.6 * grad_z + 0.48 * grad_y + 0.64 * grad_x) / length
        shading = 0.3 + 0.7 * jnp.abs(facing)
        colour = (
            jnp.stack(
                [
                    jax.nn.sigmoid(2.0 * centre),
                    jnp.exp(-centre * centre),
                    jax.nn.sigmoid(-2.0 * centre),
                ]
            )
            * shading
        )
        opacity = 1.0 - jnp.exp(-extinction * jnp.exp(1.5 * centre))
        weight = (1.0 - accum_opacity) * opacity
        return ((accum_colour + weight * colour, accum_opacity + weight), None)

    height = padded.shape[1] - 2
    width = padded.shape[2] - 2
    start = (jnp.zeros((3, height, width), jnp.float32), jnp.zeros((height, width), jnp.float32))
    (colour_sum, opacity_sum), _ = lax.scan(advance, start, jnp.arange(count, dtype=jnp.int32))
    return jnp.concatenate([colour_sum, opacity_sum[None]], axis=0)


def over_pixels(nearer, farther, channel_axis):
    coverage = lax.slice_in_dim(nearer, 3, 4, axis=channel_axis)
    return nearer + (1.0 - coverage) * farther


def local_general(log_density):
    slices, row_count, width = log_density.shape
    depth_count = lax.axis_size("depth")
    classes = width // depth_count
    padded = with_halo(log_density, (("depth", 0), ("rows", 1)), 1)
    padded = jnp.pad(padded, ((0, 0), (0, 0), (1, 1)))
    image = shade_slab(padded, 0.5 / (slices * depth_count), slices)
    partial_value = image.reshape(4, row_count, classes, depth_count).transpose(0, 1, 3, 2)
    layers = lax.all_to_all(partial_value[None], "depth", split_axis=3, concat_axis=0, tiled=True)
    while layers.shape[0] > 1:
        paired = layers.reshape((layers.shape[0] // 2, 2) + layers.shape[1:])
        layers = over_pixels(paired[:, 0], paired[:, 1], 1)
    return layers[0]


def bit_reversed(value, bits):
    return sum(((value >> b) & 1) << (bits - 1 - b) for b in range(bits))


def kernel(depth, rows, vol_ref, out_ref, cells, edges, rim, cut, spread, image, final, *rest):
    S, tiles, _, W = vol_ref.shape
    chunks = tiles // 2
    groups = depth // 2
    steps = groups.bit_length() - 1
    part = LANES * depth
    parts = W // part
    pieces = parts * chunks
    ahead = min(AHEAD, pieces)
    span = pl.ds(LANES, W)
    log_extinction = math.log2(0.5 / (S * depth) * LOG2E)

    held, came = rest[: steps + 1], rest[steps + 1 : 2 * steps + 1]
    (own_sem, rim_sem, own_edge_sem, pair_send, pair_recv, edge_send, edge_recv, row_send, row_recv,
     face_send, face_recv, part_send, part_recv, last_send, last_recv) = rest[2 * steps + 1 :]

    me, row = lax.axis_index("depth"), lax.axis_index("rows")
    x, z = lax.rem(me, 2), me // 2
    first = me - x
    partner = first + 1 - x
    mine = 1 + S * x

    near = [(partner, row, None)]
    for d, there in ((-1, z >= 1), (1, z <= groups - 2)):
        near.append((me + 2 * d, row, there))
    for k in range(1, steps):
        near.append((2 * (z + (1 << k) * (1 - 2 * (lax.rem(z // (1 << k), 2)))) + x, row, None))
    for d, there in ((-1, row >= 1), (1, row <= rows - 2)):
        near.append((first, row + d, there))
        near.append((first + 1, row + d, there))
    barrier = pltpu.get_barrier_semaphore()
    count = 0
    for dd, rr, there in near:
        def greet(dd=dd, rr=rr):
            pl.semaphore_signal(barrier, inc=1, device_id=(dd, rr), device_id_type=MESH)
        if there is None:
            greet()
            count = count + 1
        else:
            pl.when(there)(greet)
            count = count + there.astype(jnp.int32)

    own = pltpu.make_async_copy(
        vol_ref.at[:, pl.ds(x * chunks, chunks)],
        cells.at[pl.ds(mine, S), pl.ds(1, chunks), :, span],
        own_sem,
    )
    own.start()
    rims = [
        pltpu.make_async_copy(vol_ref.at[:, tile], rim.at[n], rim_sem.at[n])
        for n, tile in enumerate(((1 - x) * chunks, (2 - x) * chunks - 1))
    ]
    for copy in rims:
        copy.start()
    pl.semaphore_wait(barrier, count)

    def pair_copy(q, h):
        def apply(act):
            for g in range(parts):
                low = g * part + (LANES if g else 0)
                high = (g + 1) * part + (LANES if g + 1 < parts else 0)

                @pl.when(q // chunks == g)
                def _(g=g, low=low, high=high):
                    c = q - g * chunks
                    act(pltpu.make_async_remote_copy(
                        src_ref=vol_ref.at[pl.ds(h * (S // 2), S // 2), (1 - x) * chunks + c, :, pl.ds(low, high - low)],
                        dst_ref=cells.at[pl.ds(mine + h * (S // 2), S // 2), 1 + c, :, pl.ds(LANES + low, high - low)],
                        send_sem=pair_send.at[h, q], recv_sem=pair_recv.at[h, q],
                        device_id=(partner, row), device_id_type=MESH,
                    ))
        return apply

    def start(copy):
        copy.start()

    def edge_copy():
        return pltpu.make_async_remote_copy(
            src_ref=cut.at[1 + x], dst_ref=edges.at[x, x],
            send_sem=edge_send, recv_sem=edge_recv,
            device_id=(partner, row), device_id_type=MESH,
        )

    def row_copy(direction):
        return pltpu.make_async_remote_copy(
            src_ref=cut.at[3 - 3 * direction], dst_ref=edges.at[direction, x],
            send_sem=row_send.at[direction], recv_sem=row_recv.at[x],
            device_id=(first + direction, row + 1 - 2 * direction), device_id_type=MESH,
        )

    def row_arrival(source):
        return pltpu.make_async_remote_copy(
            src_ref=cut.at[0], dst_ref=edges.at[x, source],
            send_sem=row_send.at[0], recv_sem=row_recv.at[source],
            device_id=(partner, row), device_id_type=MESH,
        )

    def face_copy(direction, q):
        c, at = lax.rem(q, chunks), pl.ds(pl.multiple_of(LANES + q // chunks * part, LANES), part)
        return pltpu.make_async_remote_copy(
            src_ref=cells.at[2 * S if direction == 0 else 1, 1 + c, :, at],
            dst_ref=cells.at[0 if direction == 0 else 2 * S + 1, 1 + c, :, at],
            send_sem=face_send.at[direction, q], recv_sem=face_recv.at[direction, q],
            device_id=(me + (2 if direction == 0 else -2), row), device_id_type=MESH,
        )

    def part_copy(k, q):
        half = groups >> (k + 1)
        bit = lax.rem(z // (1 << k), 2)
        return pltpu.make_async_remote_copy(
            src_ref=held[k].at[q, pl.ds((1 - bit) * half, half)], dst_ref=came[k].at[q],
            send_sem=part_send.at[k, q], recv_sem=part_recv.at[k, q],
            device_id=(me + 2 * (1 << k) * (1 - 2 * bit), row), device_id_type=MESH,
        )

    def last_copy(q):
        return pltpu.make_async_remote_copy(
            src_ref=held[steps].at[q, 0, 1 - x], dst_ref=final.at[q],
            send_sem=last_send.at[q], recv_sem=last_recv.at[q],
            device_id=(partner, row), device_id_type=MESH,
        )

    @pl.loop(0, ahead)
    def _(q):
        for h in range(2):
            pair_copy(q, h)(start)

    has_next_row, has_prev_row = row <= rows - 2, row >= 1
    has_next, has_prev = z <= groups - 2, z >= 1
    has_edge = jnp.logical_or(jnp.logical_and(x == 0, has_prev_row), jnp.logical_and(x == 1, has_next_row))

    own.wait()
    for copy in rims:
        copy.wait()
    for s in range(S):
        cut[2 * x, s : s + 1, :] = cells[mine + s, 1, 0:1, LANES : LANES + W]
        cut[1 + 2 * x, s : s + 1, :] = cells[mine + s, chunks, TILE - 1 : TILE, LANES : LANES + W]
        cut[2 - 2 * x, s : s + 1, :] = rim[0, s, 0:1, :]
        cut[3 - 2 * x, s : s + 1, :] = rim[1, s, TILE - 1 : TILE, :]
    edge_copy().start()
    pl.when(has_next_row)(lambda: row_copy(0).start())
    pl.when(has_prev_row)(lambda: row_copy(1).start())
    own_edge = pltpu.make_async_copy(cut.at[2 - x], edges.at[1 - x, x], own_edge_sem)
    own_edge.start()

    @pl.loop(0, 2 * S + 2)
    def _(s):
        cells[s, :, :, 0:LANES] = jnp.zeros((chunks + 2, TILE, LANES), jnp.float32)
        cells[s, :, :, LANES + W :] = jnp.zeros((chunks + 2, TILE, LANES), jnp.float32)

    @pl.when(jnp.logical_not(has_prev))
    def _():
        @pl.loop(0, chunks)
        def _(c):
            cells[0, 1 + c, :, span] = jnp.zeros((TILE, W), jnp.float32)

    @pl.when(jnp.logical_not(has_next))
    def _():
        @pl.loop(0, chunks)
        def _(c):
            cells[2 * S + 1, 1 + c, :, span] = jnp.zeros((TILE, W), jnp.float32)

    blocks, group = part // BLOCK, BLOCK // depth

    @pl.loop(0, blocks)
    def _(b):
        at = lax.broadcasted_iota(jnp.int32, (BLOCK, BLOCK), 0)
        to = lax.broadcasted_iota(jnp.int32, (BLOCK, BLOCK), 1)
        klass = to // LANES * blocks + (to % LANES // group + blocks - b) % blocks
        source = to % group * depth + klass
        spread[b] = jnp.where(at == source, 1.0, 0.0).astype(jnp.bfloat16)

    own_edge.wait()
    edge_copy().wait()
    pl.when(has_next_row)(lambda: row_copy(0).wait_send())
    pl.when(has_prev_row)(lambda: row_copy(1).wait_send())

    @pl.when(has_edge)
    def _():
        row_arrival(0).wait_recv()
        row_arrival(1).wait_recv()

    @pl.when(jnp.logical_not(has_edge))
    def _():
        edges[x] = jnp.zeros(edges.shape[1:], jnp.float32)

    for s in range(2 * S):
        cells[1 + s, 0, TILE - 1 : TILE, LANES : LANES + W] = edges[0, s // S, s % S : s % S + 1, :]
        cells[1 + s, chunks + 1, 0:1, LANES : LANES + W] = edges[1, s // S, s % S : s % S + 1, :]

    row_of = lax.broadcasted_iota(jnp.int32, (TILE, LANES), 0)
    lane_of = lax.broadcasted_iota(jnp.int32, (TILE, LANES), 1)
    is_top, is_bottom = row_of == 0, row_of == TILE - 1
    is_left, is_right = lane_of == 0, lane_of == LANES - 1
    group_of = lax.broadcasted_iota(jnp.int32, (4 * TILE, LANES), 1) // group

    def shade(q):
        t, begin = 1 + lax.rem(q, chunks), q // chunks * part

        def columns(b, carry):
            base = pl.multiple_of(begin + b * SPAN, SPAN)

            def lanes(v):
                return pl.ds(pl.multiple_of(base + v * LANES, LANES), LANES)

            def load(s):
                return [cells[s, t, :, lanes(v)] for v in range(SPAN // LANES + 2)]

            zero = jnp.zeros((TILE, LANES), jnp.float32)
            sums = [[zero] * 4 for _ in range(SPAN // LANES)]
            before, here = load(0), load(1)
            for s in range(1, 2 * S + 1):
                after = load(s + 1)
                for v in range(SPAN // LANES):
                    both, swing, green, alpha = sums[v]
                    centre = here[v + 1]
                    left = pltpu.roll(jnp.where(is_right, here[v], centre), 1, 1)
                    right = pltpu.roll(jnp.where(is_left, here[v + 2], centre), LANES - 1, 1)
                    above = pltpu.roll(jnp.where(is_bottom, cells[s, t - 1, :, lanes(v + 1)], centre), 1, 0)
                    below = pltpu.roll(jnp.where(is_top, cells[s, t + 1, :, lanes(v + 1)], centre), TILE - 1, 0)
                    dz, dy, dx = after[v + 1] - before[v + 1], below - above, right - left
                    square = dz * dz + dy * dy + (dx * dx + 4.0)
                    facing = 1.25 * dz + dy + (0.64 / 0.48) * dx
                    shading = jnp.abs(facing) * lax.rsqrt(square) + 0.3 / 0.336
                    opacity = 1.0 - jnp.exp2(-jnp.exp2((1.5 * LOG2E) * centre + log_extinction))
                    weight = (1.0 - alpha) * opacity
                    lit = weight * shading
                    sums[v] = [
                        both + lit,
                        swing + lit * jnp.tanh(centre),
                        green + lit * jnp.exp2(centre * (centre * -LOG2E)),
                        alpha + weight,
                    ]
                before, here = here, after
            for v in range(SPAN // LANES):
                both, swing, green, alpha = sums[v]
                both, swing = (0.5 * 0.336) * both, (0.5 * 0.336) * swing
                to = pl.ds(pl.multiple_of(b * SPAN + v * LANES, LANES), LANES)
                for ch, value in enumerate((both + swing, 0.336 * green, both - swing, alpha)):
                    image[ch, :, to] = value
            return carry

        lax.fori_loop(0, part // SPAN, columns, 0)
        turned = []
        for b in range(blocks):
            piece = image[:, :, b * BLOCK : (b + 1) * BLOCK].reshape(4 * TILE, BLOCK)
            high = piece.astype(jnp.bfloat16)
            low = (piece - high.astype(jnp.float32)).astype(jnp.bfloat16)
            two = jnp.dot(jnp.concatenate([high, low], axis=0), spread[b], preferred_element_type=jnp.float32)
            turned.append(two[: 4 * TILE] + two[4 * TILE :])
        for j in range(depth):
            h, r = j // blocks, j % blocks
            mixed = turned[-r % blocks][:, h * LANES : (h + 1) * LANES]
            for g in range(1, blocks):
                other = turned[(g - r) % blocks][:, h * LANES : (h + 1) * LANES]
                mixed = jnp.where(group_of == g, other, mixed)
            if r:
                mixed = pltpu.roll(mixed, LANES - group * r, 1)
            held[0][q, bit_reversed(j // 2, steps), j % 2] = mixed.reshape(4, TILE, LANES)

    def combine(k, q):
        half = groups >> (k + 1)
        bit = lax.rem(z // (1 << k), 2)
        part_copy(k, q).wait_recv()

        def join(near_of, far_of):
            for i in range(half):
                for p in range(2):
                    near, far = near_of(i, p), far_of(i, p)
                    clear = 1.0 - near[3]
                    for ch in range(4):
                        held[k + 1][q, i, p, ch] = near[ch] + clear * far[ch]

        def kept(i, p):
            return held[k][q, bit * half + i, p]

        def received(i, p):
            return came[k][q, i, p]

        pl.when(bit == 0)(lambda: join(kept, received))
        pl.when(bit == 1)(lambda: join(received, kept))

    def put(side, q, value):
        at = ((side * chunks + lax.rem(q, chunks)) * TILE) * parts + q // chunks
        for ch in range(4):
            out_ref[ch, pl.ds(at, TILE, stride=parts), :] = value[ch]

    @pl.loop(0, pieces + steps + 1)
    def _(i):
        @pl.when(i < pieces)
        def _():
            for h in range(2):
                pair_copy(i, h)(lambda copy: copy.wait_recv())
            pl.when(has_next)(lambda: face_copy(0, i).start())
            pl.when(has_prev)(lambda: face_copy(1, i).start())
            pl.when(i + ahead < pieces)(lambda: pair_copy(i + ahead, 0)(start))

        @pl.when(jnp.logical_and(i >= 1, i <= pieces))
        def _():
            q = i - 1
            pl.when(has_prev)(lambda: face_copy(0, q).wait_recv())
            pl.when(has_next)(lambda: face_copy(1, q).wait_recv())
            shade(q)
            part_copy(0, q).start()

        pl.when(i + ahead < pieces)(lambda: pair_copy(i + ahead, 1)(start))
        for k in range(steps):

            @pl.when(jnp.logical_and(i >= k + 2, i <= pieces + k + 1))
            def _(k=k):
                q = i - 2 - k
                combine(k, q)
                if k + 1 < steps:
                    part_copy(k + 1, q).start()
                else:
                    last_copy(q).start()
                    put(x, q, held[steps][q, 0, x])

    @pl.loop(0, pieces)
    def _(q):
        for h in range(2):
            pair_copy(q, h)(lambda copy: copy.wait_send())
        pl.when(has_next)(lambda: face_copy(0, q).wait_send())
        pl.when(has_prev)(lambda: face_copy(1, q).wait_send())
        for k in range(steps):
            part_copy(k, q).wait_send()
        last_copy(q).wait()
        put(1 - x, q, final[q])


def local(log_density):
    S, R, W = log_density.shape
    depth, rows = lax.axis_size("depth"), lax.axis_size("rows")
    groups = depth // 2
    fits = (
        4 <= depth <= LANES
        and (LANES * depth) % SPAN == 0
        and depth & (depth - 1) == 0
        and W % (LANES * depth) == 0
        and R % (2 * TILE) == 0
        and S % 2 == 0
    )
    if not fits:
        return local_general(log_density)
    steps = groups.bit_length() - 1
    tiles = R // TILE
    chunks = tiles // 2
    part = LANES * depth
    parts = W // part
    pieces = parts * chunks
    F32 = jnp.float32
    partial = [pltpu.VMEM((pieces, groups >> k, 2, 4, TILE, LANES), F32) for k in range(steps + 1)]
    arrivals = [pltpu.VMEM((pieces, groups >> (k + 1), 2, 4, TILE, LANES), F32) for k in range(steps)]
    DMA = pltpu.SemaphoreType.DMA
    out = pl.pallas_call(
        functools.partial(kernel, depth, rows),
        out_shape=jax.ShapeDtypeStruct((4, R * parts, LANES), F32),
        in_specs=[pl.BlockSpec(memory_space=pl.ANY)],
        out_specs=pl.BlockSpec(memory_space=pltpu.VMEM),
        scratch_shapes=[
            pltpu.VMEM((2 * S + 2, chunks + 2, TILE, W + 2 * LANES), F32),
            pltpu.VMEM((2, 2, S, W), F32),
            pltpu.VMEM((2, S, TILE, W), F32),
            pltpu.VMEM((4, S, W), F32),
            pltpu.VMEM((part // BLOCK, BLOCK, BLOCK), jnp.bfloat16),
            pltpu.VMEM((4, TILE, part), F32),
            pltpu.VMEM((pieces, 4, TILE, LANES), F32),
            *partial,
            *arrivals,
            DMA, DMA((2,)), DMA,
            DMA((2, pieces)), DMA((2, pieces)),
            DMA, DMA,
            DMA((2,)), DMA((2,)),
            DMA((2, pieces)), DMA((2, pieces)),
            DMA((steps, pieces)), DMA((steps, pieces)),
            DMA((pieces,)), DMA((pieces,)),
        ],
        compiler_params=pltpu.CompilerParams(
            collective_id=0, has_side_effects=True, vmem_limit_bytes=52 * 1024 * 1024
        ),
    )(log_density.reshape(S, tiles, TILE, W))
    return out.reshape(4, R, 1, W // depth)


def solution(mesh):
    placed = (P("depth", "rows", None),)
    return jax.shard_map(
        local, mesh=mesh, in_specs=placed, out_specs=P(None, "rows", "depth", None), check_vma=False
    )
```

```python
import functools
import math

import jax
import jax.numpy as jnp
from jax import lax
from jax.experimental import pallas as pl
from jax.experimental.pallas import tpu as pltpu
from jax.sharding import PartitionSpec as P

MESH = pl.DeviceIdType.MESH
TILE = 8
LANES = 128
BLOCK = 256
SPAN = 512
AHEAD = 2
LOG2E = 1.4426950408889634


def with_halo(shard, sides, width):
    for axis, dim in sides:
        size, length = (lax.axis_size(axis), shard.shape[dim])
        up = [(i, (i + 1) % size) for i in range(size - 1)]
        down = [(j, i) for i, j in up]
        last = lax.slice_in_dim(shard, length - width, length, axis=dim)
        leading = lax.slice_in_dim(shard, 0, width, axis=dim)
        before = lax.ppermute(last, axis, up)
        after = lax.ppermute(leading, axis, down)
        shard = jnp.concatenate([before, shard, after], axis=dim)
    return shard


def shade_slab(padded, extinction, count):

    def advance(carry, index):
        accum_colour, accum_opacity = carry
        planes = lax.dynamic_slice_in_dim(padded, index, 3, 0)
        centre = planes[1, 1:-1, 1:-1]
        grad_z = 0.5 * (planes[2, 1:-1, 1:-1] - planes[0, 1:-1, 1:-1])
        grad_y = 0.5 * (planes[1, 2:, 1:-1] - planes[1, :-2, 1:-1])
        grad_x = 0.5 * (planes[1, 1:-1, 2:] - planes[1, 1:-1, :-2])
        length = jnp.sqrt(grad_z * grad_z + grad_y * grad_y + grad_x * grad_x + 1.0)
        facing = (0.6 * grad_z + 0.48 * grad_y + 0.64 * grad_x) / length
        shading = 0.3 + 0.7 * jnp.abs(facing)
        colour = (
            jnp.stack(
                [
                    jax.nn.sigmoid(2.0 * centre),
                    jnp.exp(-centre * centre),
                    jax.nn.sigmoid(-2.0 * centre),
                ]
            )
            * shading
        )
        opacity = 1.0 - jnp.exp(-extinction * jnp.exp(1.5 * centre))
        weight = (1.0 - accum_opacity) * opacity
        return ((accum_colour + weight * colour, accum_opacity + weight), None)

    height = padded.shape[1] - 2
    width = padded.shape[2] - 2
    start = (jnp.zeros((3, height, width), jnp.float32), jnp.zeros((height, width), jnp.float32))
    (colour_sum, opacity_sum), _ = lax.scan(advance, start, jnp.arange(count, dtype=jnp.int32))
    return jnp.concatenate([colour_sum, opacity_sum[None]], axis=0)


def over_pixels(nearer, farther, channel_axis):
    coverage = lax.slice_in_dim(nearer, 3, 4, axis=channel_axis)
    return nearer + (1.0 - coverage) * farther


def local_general(log_density):
    slices, row_count, width = log_density.shape
    depth_count = lax.axis_size("depth")
    classes = width // depth_count
    padded = with_halo(log_density, (("depth", 0), ("rows", 1)), 1)
    padded = jnp.pad(padded, ((0, 0), (0, 0), (1, 1)))
    image = shade_slab(padded, 0.5 / (slices * depth_count), slices)
    partial_value = image.reshape(4, row_count, classes, depth_count).transpose(0, 1, 3, 2)
    layers = lax.all_to_all(partial_value[None], "depth", split_axis=3, concat_axis=0, tiled=True)
    while layers.shape[0] > 1:
        paired = layers.reshape((layers.shape[0] // 2, 2) + layers.shape[1:])
        layers = over_pixels(paired[:, 0], paired[:, 1], 1)
    return layers[0]


def bit_reversed(value, bits):
    return sum(((value >> b) & 1) << (bits - 1 - b) for b in range(bits))


def kernel(depth, rows, vol_ref, out_ref, cells, edges, rim, cut, spread, image, final, *rest):
    S, tiles, _, W = vol_ref.shape
    chunks = tiles // 2
    groups = depth // 2
    steps = groups.bit_length() - 1
    part = LANES * depth
    parts = W // part
    pieces = parts * chunks
    span = pl.ds(LANES, W)
    log_extinction = math.log2(0.5 / (S * depth) * LOG2E)

    held, came = rest[: steps + 1], rest[steps + 1 : 2 * steps + 1]
    (own_sem, rim_sem, own_edge_sem, pair_send, pair_recv, edge_send, edge_recv, row_send, row_recv,
     face_send, face_recv, part_send, part_recv, last_send, last_recv) = rest[2 * steps + 1 :]

    me, row = lax.axis_index("depth"), lax.axis_index("rows")
    x, z = lax.rem(me, 2), me // 2
    first = me - x
    ahead = jnp.minimum(AHEAD + 1 - lax.rem(row, 2), pieces)
    partner = first + 1 - x
    mine = 1 + S * x

    near = [(partner, row, None)]
    for d, there in ((-1, z >= 1), (1, z <= groups - 2)):
        near.append((me + 2 * d, row, there))
    for k in range(1, steps):
        near.append((2 * (z + (1 << k) * (1 - 2 * (lax.rem(z // (1 << k), 2)))) + x, row, None))
    for d, there in ((-1, row >= 1), (1, row <= rows - 2)):
        near.append((first, row + d, there))
        near.append((first + 1, row + d, there))
    barrier = pltpu.get_barrier_semaphore()
    count = 0
    for dd, rr, there in near:
        def greet(dd=dd, rr=rr):
            pl.semaphore_signal(barrier, inc=1, device_id=(dd, rr), device_id_type=MESH)
        if there is None:
            greet()
            count = count + 1
        else:
            pl.when(there)(greet)
            count = count + there.astype(jnp.int32)

    own = pltpu.make_async_copy(
        vol_ref.at[:, pl.ds(x * chunks, chunks)],
        cells.at[pl.ds(mine, S), pl.ds(1, chunks), :, span],
        own_sem,
    )
    own.start()
    rims = [
        pltpu.make_async_copy(vol_ref.at[:, tile], rim.at[n], rim_sem.at[n])
        for n, tile in enumerate(((1 - x) * chunks, (2 - x) * chunks - 1))
    ]
    for copy in rims:
        copy.start()
    pl.semaphore_wait(barrier, count)

    def pair_copy(q):
        def apply(act):
            for g in range(parts):
                low = g * part + (LANES if g else 0)
                high = (g + 1) * part + (LANES if g + 1 < parts else 0)

                @pl.when(q // chunks == g)
                def _(g=g, low=low, high=high):
                    c = q - g * chunks
                    act(pltpu.make_async_remote_copy(
                        src_ref=vol_ref.at[:, (1 - x) * chunks + c, :, pl.ds(low, high - low)],
                        dst_ref=cells.at[pl.ds(mine, S), 1 + c, :, pl.ds(LANES + low, high - low)],
                        send_sem=pair_send.at[q], recv_sem=pair_recv.at[q],
                        device_id=(partner, row), device_id_type=MESH,
                    ))
        return apply

    def start(copy):
        copy.start()

    def edge_copy():
        return pltpu.make_async_remote_copy(
            src_ref=cut.at[1 + x], dst_ref=edges.at[x, x],
            send_sem=edge_send, recv_sem=edge_recv,
            device_id=(partner, row), device_id_type=MESH,
        )

    def row_copy(direction):
        return pltpu.make_async_remote_copy(
            src_ref=cut.at[3 - 3 * direction], dst_ref=edges.at[direction, x],
            send_sem=row_send.at[direction], recv_sem=row_recv.at[x],
            device_id=(first + direction, row + 1 - 2 * direction), device_id_type=MESH,
        )

    def row_arrival(source):
        return pltpu.make_async_remote_copy(
            src_ref=cut.at[0], dst_ref=edges.at[x, source],
            send_sem=row_send.at[0], recv_sem=row_recv.at[source],
            device_id=(partner, row), device_id_type=MESH,
        )

    def face_copy(direction, q):
        c, at = lax.rem(q, chunks), pl.ds(pl.multiple_of(LANES + q // chunks * part, LANES), part)
        return pltpu.make_async_remote_copy(
            src_ref=cells.at[2 * S if direction == 0 else 1, 1 + c, :, at],
            dst_ref=cells.at[0 if direction == 0 else 2 * S + 1, 1 + c, :, at],
            send_sem=face_send.at[direction, q], recv_sem=face_recv.at[direction, q],
            device_id=(me + (2 if direction == 0 else -2), row), device_id_type=MESH,
        )

    def part_copy(k, q):
        half = groups >> (k + 1)
        bit = lax.rem(z // (1 << k), 2)
        return pltpu.make_async_remote_copy(
            src_ref=held[k].at[q, pl.ds((1 - bit) * half, half)], dst_ref=came[k].at[q],
            send_sem=part_send.at[k, q], recv_sem=part_recv.at[k, q],
            device_id=(me + 2 * (1 << k) * (1 - 2 * bit), row), device_id_type=MESH,
        )

    def last_copy(q):
        return pltpu.make_async_remote_copy(
            src_ref=held[steps].at[q, 0, 1 - x], dst_ref=final.at[q],
            send_sem=last_send.at[q], recv_sem=last_recv.at[q],
            device_id=(partner, row), device_id_type=MESH,
        )

    pl.loop(0, ahead)(lambda q: pair_copy(q)(start))

    has_next_row, has_prev_row = row <= rows - 2, row >= 1
    has_next, has_prev = z <= groups - 2, z >= 1
    has_edge = jnp.logical_or(jnp.logical_and(x == 0, has_prev_row), jnp.logical_and(x == 1, has_next_row))

    own.wait()
    for copy in rims:
        copy.wait()
    for s in range(S):
        cut[2 * x, s : s + 1, :] = cells[mine + s, 1, 0:1, LANES : LANES + W]
        cut[1 + 2 * x, s : s + 1, :] = cells[mine + s, chunks, TILE - 1 : TILE, LANES : LANES + W]
        cut[2 - 2 * x, s : s + 1, :] = rim[0, s, 0:1, :]
        cut[3 - 2 * x, s : s + 1, :] = rim[1, s, TILE - 1 : TILE, :]
    edge_copy().start()
    pl.when(has_next_row)(lambda: row_copy(0).start())
    pl.when(has_prev_row)(lambda: row_copy(1).start())
    own_edge = pltpu.make_async_copy(cut.at[2 - x], edges.at[1 - x, x], own_edge_sem)
    own_edge.start()

    @pl.loop(0, 2 * S + 2)
    def _(s):
        cells[s, :, :, 0:LANES] = jnp.zeros((chunks + 2, TILE, LANES), jnp.float32)
        cells[s, :, :, LANES + W :] = jnp.zeros((chunks + 2, TILE, LANES), jnp.float32)

    @pl.when(jnp.logical_not(has_prev))
    def _():
        @pl.loop(0, chunks)
        def _(c):
            cells[0, 1 + c, :, span] = jnp.zeros((TILE, W), jnp.float32)

    @pl.when(jnp.logical_not(has_next))
    def _():
        @pl.loop(0, chunks)
        def _(c):
            cells[2 * S + 1, 1 + c, :, span] = jnp.zeros((TILE, W), jnp.float32)

    blocks, group = part // BLOCK, BLOCK // depth

    @pl.loop(0, blocks)
    def _(b):
        at = lax.broadcasted_iota(jnp.int32, (BLOCK, BLOCK), 0)
        to = lax.broadcasted_iota(jnp.int32, (BLOCK, BLOCK), 1)
        klass = to // LANES * blocks + (to % LANES // group + blocks - b) % blocks
        source = to % group * depth + klass
        spread[b] = jnp.where(at == source, 1.0, 0.0).astype(jnp.bfloat16)

    own_edge.wait()
    edge_copy().wait()
    pl.when(has_next_row)(lambda: row_copy(0).wait_send())
    pl.when(has_prev_row)(lambda: row_copy(1).wait_send())

    @pl.when(has_edge)
    def _():
        row_arrival(0).wait_recv()
        row_arrival(1).wait_recv()

    @pl.when(jnp.logical_not(has_edge))
    def _():
        edges[x] = jnp.zeros(edges.shape[1:], jnp.float32)

    for s in range(2 * S):
        cells[1 + s, 0, TILE - 1 : TILE, LANES : LANES + W] = edges[0, s // S, s % S : s % S + 1, :]
        cells[1 + s, chunks + 1, 0:1, LANES : LANES + W] = edges[1, s // S, s % S : s % S + 1, :]

    row_of = lax.broadcasted_iota(jnp.int32, (TILE, LANES), 0)
    lane_of = lax.broadcasted_iota(jnp.int32, (TILE, LANES), 1)
    is_top, is_bottom = row_of == 0, row_of == TILE - 1
    is_left, is_right = lane_of == 0, lane_of == LANES - 1
    group_of = lax.broadcasted_iota(jnp.int32, (4 * TILE, LANES), 1) // group

    def shade(q):
        t, begin = 1 + lax.rem(q, chunks), q // chunks * part

        def columns(b, carry):
            base = pl.multiple_of(begin + b * SPAN, SPAN)

            def lanes(v):
                return pl.ds(pl.multiple_of(base + v * LANES, LANES), LANES)

            def load(s):
                return [cells[s, t, :, lanes(v)] for v in range(SPAN // LANES + 2)]

            zero = jnp.zeros((TILE, LANES), jnp.float32)
            sums = [[zero] * 4 for _ in range(SPAN // LANES)]
            before, here = load(0), load(1)
            for s in range(1, 2 * S + 1):
                after = load(s + 1)
                for v in range(SPAN // LANES):
                    both, swing, green, alpha = sums[v]
                    centre = here[v + 1]
                    left = pltpu.roll(jnp.where(is_right, here[v], centre), 1, 1)
                    right = pltpu.roll(jnp.where(is_left, here[v + 2], centre), LANES - 1, 1)
                    above = pltpu.roll(jnp.where(is_bottom, cells[s, t - 1, :, lanes(v + 1)], centre), 1, 0)
                    below = pltpu.roll(jnp.where(is_top, cells[s, t + 1, :, lanes(v + 1)], centre), TILE - 1, 0)
                    dz, dy, dx = after[v + 1] - before[v + 1], below - above, right - left
                    square = dz * dz + dy * dy + (dx * dx + 4.0)
                    facing = 1.25 * dz + dy + (0.64 / 0.48) * dx
                    shading = jnp.abs(facing) * lax.rsqrt(square) + 0.3 / 0.336
                    opacity = 1.0 - jnp.exp2(-jnp.exp2((1.5 * LOG2E) * centre + log_extinction))
                    weight = (1.0 - alpha) * opacity
                    lit = weight * shading
                    sums[v] = [
                        both + lit,
                        swing + lit * jnp.tanh(centre),
                        green + lit * jnp.exp2(centre * (centre * -LOG2E)),
                        alpha + weight,
                    ]
                before, here = here, after
            for v in range(SPAN // LANES):
                both, swing, green, alpha = sums[v]
                both, swing = (0.5 * 0.336) * both, (0.5 * 0.336) * swing
                to = pl.ds(pl.multiple_of(b * SPAN + v * LANES, LANES), LANES)
                for ch, value in enumerate((both + swing, 0.336 * green, both - swing, alpha)):
                    image[ch, :, to] = value
            return carry

        lax.fori_loop(0, part // SPAN, columns, 0)
        turned = []
        for b in range(blocks):
            piece = image[:, :, b * BLOCK : (b + 1) * BLOCK].reshape(4 * TILE, BLOCK)
            high = piece.astype(jnp.bfloat16)
            low = (piece - high.astype(jnp.float32)).astype(jnp.bfloat16)
            two = jnp.dot(jnp.concatenate([high, low], axis=0), spread[b], preferred_element_type=jnp.float32)
            turned.append(two[: 4 * TILE] + two[4 * TILE :])
        for j in range(depth):
            h, r = j // blocks, j % blocks
            mixed = turned[-r % blocks][:, h * LANES : (h + 1) * LANES]
            for g in range(1, blocks):
                other = turned[(g - r) % blocks][:, h * LANES : (h + 1) * LANES]
                mixed = jnp.where(group_of == g, other, mixed)
            if r:
                mixed = pltpu.roll(mixed, LANES - group * r, 1)
            held[0][q, bit_reversed(j // 2, steps), j % 2] = mixed.reshape(4, TILE, LANES)

    def combine(k, q):
        half = groups >> (k + 1)
        bit = lax.rem(z // (1 << k), 2)
        part_copy(k, q).wait_recv()

        def join(near_of, far_of):
            for i in range(half):
                for p in range(2):
                    near, far = near_of(i, p), far_of(i, p)
                    clear = 1.0 - near[3]
                    for ch in range(4):
                        held[k + 1][q, i, p, ch] = near[ch] + clear * far[ch]

        def kept(i, p):
            return held[k][q, bit * half + i, p]

        def received(i, p):
            return came[k][q, i, p]

        pl.when(bit == 0)(lambda: join(kept, received))
        pl.when(bit == 1)(lambda: join(received, kept))

    def put(side, q, value):
        at = ((side * chunks + lax.rem(q, chunks)) * TILE) * parts + q // chunks
        for ch in range(4):
            out_ref[ch, pl.ds(at, TILE, stride=parts), :] = value[ch]

    @pl.loop(0, pieces + steps + 1)
    def _(i):
        @pl.when(i < pieces)
        def _():
            pair_copy(i)(lambda copy: copy.wait_recv())
            pl.when(i + ahead < pieces)(lambda: pair_copy(i + ahead)(start))
            pl.when(has_next)(lambda: face_copy(0, i).start())
            pl.when(has_prev)(lambda: face_copy(1, i).start())

        @pl.when(jnp.logical_and(i >= 1, i <= pieces))
        def _():
            q = i - 1
            pl.when(has_prev)(lambda: face_copy(0, q).wait_recv())
            pl.when(has_next)(lambda: face_copy(1, q).wait_recv())
            shade(q)
            part_copy(0, q).start()

        for k in range(steps):

            @pl.when(jnp.logical_and(i >= k + 2, i <= pieces + k + 1))
            def _(k=k):
                q = i - 2 - k
                combine(k, q)
                if k + 1 < steps:
                    part_copy(k + 1, q).start()
                else:
                    last_copy(q).start()
                    put(x, q, held[steps][q, 0, x])

    @pl.loop(0, pieces)
    def _(q):
        pair_copy(q)(lambda copy: copy.wait_send())
        pl.when(has_next)(lambda: face_copy(0, q).wait_send())
        pl.when(has_prev)(lambda: face_copy(1, q).wait_send())
        for k in range(steps):
            part_copy(k, q).wait_send()
        last_copy(q).wait()
        put(1 - x, q, final[q])


def local(log_density):
    S, R, W = log_density.shape
    depth, rows = lax.axis_size("depth"), lax.axis_size("rows")
    groups = depth // 2
    fits = (
        4 <= depth <= LANES
        and (LANES * depth) % SPAN == 0
        and depth & (depth - 1) == 0
        and W % (LANES * depth) == 0
        and R % (2 * TILE) == 0
    )
    if not fits:
        return local_general(log_density)
    steps = groups.bit_length() - 1
    tiles = R // TILE
    chunks = tiles // 2
    part = LANES * depth
    parts = W // part
    pieces = parts * chunks
    F32 = jnp.float32
    partial = [pltpu.VMEM((pieces, groups >> k, 2, 4, TILE, LANES), F32) for k in range(steps + 1)]
    arrivals = [pltpu.VMEM((pieces, groups >> (k + 1), 2, 4, TILE, LANES), F32) for k in range(steps)]
    DMA = pltpu.SemaphoreType.DMA
    out = pl.pallas_call(
        functools.partial(kernel, depth, rows),
        out_shape=jax.ShapeDtypeStruct((4, R * parts, LANES), F32),
        in_specs=[pl.BlockSpec(memory_space=pl.ANY)],
        out_specs=pl.BlockSpec(memory_space=pltpu.VMEM),
        scratch_shapes=[
            pltpu.VMEM((2 * S + 2, chunks + 2, TILE, W + 2 * LANES), F32),
            pltpu.VMEM((2, 2, S, W), F32),
            pltpu.VMEM((2, S, TILE, W), F32),
            pltpu.VMEM((4, S, W), F32),
            pltpu.VMEM((part // BLOCK, BLOCK, BLOCK), jnp.bfloat16),
            pltpu.VMEM((4, TILE, part), F32),
            pltpu.VMEM((pieces, 4, TILE, LANES), F32),
            *partial,
            *arrivals,
            DMA, DMA((2,)), DMA,
            DMA((pieces,)), DMA((pieces,)),
            DMA, DMA,
            DMA((2,)), DMA((2,)),
            DMA((2, pieces)), DMA((2, pieces)),
            DMA((steps, pieces)), DMA((steps, pieces)),
            DMA((pieces,)), DMA((pieces,)),
        ],
        compiler_params=pltpu.CompilerParams(
            collective_id=0, has_side_effects=True, vmem_limit_bytes=52 * 1024 * 1024
        ),
    )(log_density.reshape(S, tiles, TILE, W))
    return out.reshape(4, R, 1, W // depth)


def solution(mesh):
    placed = (P("depth", "rows", None),)
    return jax.shard_map(
        local, mesh=mesh, in_specs=placed, out_specs=P(None, "rows", "depth", None), check_vma=False
    )
```

```python
import functools
import math

import jax
import jax.numpy as jnp
from jax import lax
from jax.experimental import pallas as pl
from jax.experimental.pallas import tpu as pltpu
from jax.sharding import PartitionSpec as P

MESH = pl.DeviceIdType.MESH
TILE = 8
LANES = 128
BLOCK = 256
SPAN = 512
AHEAD = 2
LAG = 2
LOG2E = 1.4426950408889634


def with_halo(shard, sides, width):
    for axis, dim in sides:
        size, length = (lax.axis_size(axis), shard.shape[dim])
        up = [(i, (i + 1) % size) for i in range(size - 1)]
        down = [(j, i) for i, j in up]
        last = lax.slice_in_dim(shard, length - width, length, axis=dim)
        leading = lax.slice_in_dim(shard, 0, width, axis=dim)
        before = lax.ppermute(last, axis, up)
        after = lax.ppermute(leading, axis, down)
        shard = jnp.concatenate([before, shard, after], axis=dim)
    return shard


def shade_slab(padded, extinction, count):

    def advance(carry, index):
        accum_colour, accum_opacity = carry
        planes = lax.dynamic_slice_in_dim(padded, index, 3, 0)
        centre = planes[1, 1:-1, 1:-1]
        grad_z = 0.5 * (planes[2, 1:-1, 1:-1] - planes[0, 1:-1, 1:-1])
        grad_y = 0.5 * (planes[1, 2:, 1:-1] - planes[1, :-2, 1:-1])
        grad_x = 0.5 * (planes[1, 1:-1, 2:] - planes[1, 1:-1, :-2])
        length = jnp.sqrt(grad_z * grad_z + grad_y * grad_y + grad_x * grad_x + 1.0)
        facing = (0.6 * grad_z + 0.48 * grad_y + 0.64 * grad_x) / length
        shading = 0.3 + 0.7 * jnp.abs(facing)
        colour = (
            jnp.stack(
                [
                    jax.nn.sigmoid(2.0 * centre),
                    jnp.exp(-centre * centre),
                    jax.nn.sigmoid(-2.0 * centre),
                ]
            )
            * shading
        )
        opacity = 1.0 - jnp.exp(-extinction * jnp.exp(1.5 * centre))
        weight = (1.0 - accum_opacity) * opacity
        return ((accum_colour + weight * colour, accum_opacity + weight), None)

    height = padded.shape[1] - 2
    width = padded.shape[2] - 2
    start = (jnp.zeros((3, height, width), jnp.float32), jnp.zeros((height, width), jnp.float32))
    (colour_sum, opacity_sum), _ = lax.scan(advance, start, jnp.arange(count, dtype=jnp.int32))
    return jnp.concatenate([colour_sum, opacity_sum[None]], axis=0)


def over_pixels(nearer, farther, channel_axis):
    coverage = lax.slice_in_dim(nearer, 3, 4, axis=channel_axis)
    return nearer + (1.0 - coverage) * farther


def local_general(log_density):
    slices, row_count, width = log_density.shape
    depth_count = lax.axis_size("depth")
    classes = width // depth_count
    padded = with_halo(log_density, (("depth", 0), ("rows", 1)), 1)
    padded = jnp.pad(padded, ((0, 0), (0, 0), (1, 1)))
    image = shade_slab(padded, 0.5 / (slices * depth_count), slices)
    partial_value = image.reshape(4, row_count, classes, depth_count).transpose(0, 1, 3, 2)
    layers = lax.all_to_all(partial_value[None], "depth", split_axis=3, concat_axis=0, tiled=True)
    while layers.shape[0] > 1:
        paired = layers.reshape((layers.shape[0] // 2, 2) + layers.shape[1:])
        layers = over_pixels(paired[:, 0], paired[:, 1], 1)
    return layers[0]


def bit_reversed(value, bits):
    return sum(((value >> b) & 1) << (bits - 1 - b) for b in range(bits))


def kernel(depth, rows, vol_ref, out_ref, cells, edges, rim, cut, spread, image, final, *rest):
    S, tiles, _, W = vol_ref.shape
    chunks = tiles // 2
    groups = depth // 2
    steps = groups.bit_length() - 1
    part = LANES * depth
    parts = W // part
    pieces = parts * chunks
    ahead = min(AHEAD, pieces)
    span = pl.ds(LANES, W)
    log_extinction = math.log2(0.5 / (S * depth) * LOG2E)

    held, came = rest[: steps + 1], rest[steps + 1 : 2 * steps + 1]
    (own_sem, rim_sem, own_edge_sem, pair_send, pair_recv, edge_send, edge_recv, row_send, row_recv,
     face_send, face_recv, part_send, part_recv, last_send, last_recv) = rest[2 * steps + 1 :]

    me, row = lax.axis_index("depth"), lax.axis_index("rows")
    x, z = lax.rem(me, 2), me // 2
    first = me - x
    partner = first + 1 - x
    mine = 1 + S * x

    near = [(partner, row, None)]
    for d, there in ((-1, z >= 1), (1, z <= groups - 2)):
        near.append((me + 2 * d, row, there))
    for k in range(1, steps):
        near.append((2 * (z + (1 << k) * (1 - 2 * (lax.rem(z // (1 << k), 2)))) + x, row, None))
    for d, there in ((-1, row >= 1), (1, row <= rows - 2)):
        near.append((first, row + d, there))
        near.append((first + 1, row + d, there))
    barrier = pltpu.get_barrier_semaphore()
    count = 0
    for dd, rr, there in near:
        def greet(dd=dd, rr=rr):
            pl.semaphore_signal(barrier, inc=1, device_id=(dd, rr), device_id_type=MESH)
        if there is None:
            greet()
            count = count + 1
        else:
            pl.when(there)(greet)
            count = count + there.astype(jnp.int32)

    own = pltpu.make_async_copy(
        vol_ref.at[:, pl.ds(x * chunks, chunks)],
        cells.at[pl.ds(mine, S), pl.ds(1, chunks), :, span],
        own_sem,
    )
    own.start()
    rims = [
        pltpu.make_async_copy(vol_ref.at[:, tile], rim.at[n], rim_sem.at[n])
        for n, tile in enumerate(((1 - x) * chunks, (2 - x) * chunks - 1))
    ]
    for copy in rims:
        copy.start()
    pl.semaphore_wait(barrier, count)

    def pair_copy(q):
        def apply(act):
            for g in range(parts):
                low = g * part + (LANES if g else 0)
                high = (g + 1) * part + (LANES if g + 1 < parts else 0)

                @pl.when(q // chunks == g)
                def _(g=g, low=low, high=high):
                    c = q - g * chunks
                    act(pltpu.make_async_remote_copy(
                        src_ref=vol_ref.at[:, (1 - x) * chunks + c, :, pl.ds(low, high - low)],
                        dst_ref=cells.at[pl.ds(mine, S), 1 + c, :, pl.ds(LANES + low, high - low)],
                        send_sem=pair_send.at[q], recv_sem=pair_recv.at[q],
                        device_id=(partner, row), device_id_type=MESH,
                    ))
        return apply

    def start(copy):
        copy.start()

    def edge_copy():
        return pltpu.make_async_remote_copy(
            src_ref=cut.at[1 + x], dst_ref=edges.at[x, x],
            send_sem=edge_send, recv_sem=edge_recv,
            device_id=(partner, row), device_id_type=MESH,
        )

    def row_copy(direction):
        return pltpu.make_async_remote_copy(
            src_ref=cut.at[3 - 3 * direction], dst_ref=edges.at[direction, x],
            send_sem=row_send.at[direction], recv_sem=row_recv.at[x],
            device_id=(first + direction, row + 1 - 2 * direction), device_id_type=MESH,
        )

    def row_arrival(source):
        return pltpu.make_async_remote_copy(
            src_ref=cut.at[0], dst_ref=edges.at[x, source],
            send_sem=row_send.at[0], recv_sem=row_recv.at[source],
            device_id=(partner, row), device_id_type=MESH,
        )

    def face_copy(direction, q):
        c, at = lax.rem(q, chunks), pl.ds(pl.multiple_of(LANES + q // chunks * part, LANES), part)
        return pltpu.make_async_remote_copy(
            src_ref=cells.at[2 * S if direction == 0 else 1, 1 + c, :, at],
            dst_ref=cells.at[0 if direction == 0 else 2 * S + 1, 1 + c, :, at],
            send_sem=face_send.at[direction, q], recv_sem=face_recv.at[direction, q],
            device_id=(me + (2 if direction == 0 else -2), row), device_id_type=MESH,
        )

    def part_copy(k, q):
        half = groups >> (k + 1)
        bit = lax.rem(z // (1 << k), 2)
        return pltpu.make_async_remote_copy(
            src_ref=held[k].at[q, pl.ds((1 - bit) * half, half)], dst_ref=came[k].at[q],
            send_sem=part_send.at[k, q], recv_sem=part_recv.at[k, q],
            device_id=(me + 2 * (1 << k) * (1 - 2 * bit), row), device_id_type=MESH,
        )

    def last_copy(q):
        return pltpu.make_async_remote_copy(
            src_ref=held[steps].at[q, 0, 1 - x], dst_ref=final.at[q],
            send_sem=last_send.at[q], recv_sem=last_recv.at[q],
            device_id=(partner, row), device_id_type=MESH,
        )

    pl.loop(0, ahead)(lambda q: pair_copy(q)(start))

    has_next_row, has_prev_row = row <= rows - 2, row >= 1
    has_next, has_prev = z <= groups - 2, z >= 1
    has_edge = jnp.logical_or(jnp.logical_and(x == 0, has_prev_row), jnp.logical_and(x == 1, has_next_row))

    own.wait()
    for copy in rims:
        copy.wait()
    for s in range(S):
        cut[2 * x, s : s + 1, :] = cells[mine + s, 1, 0:1, LANES : LANES + W]
        cut[1 + 2 * x, s : s + 1, :] = cells[mine + s, chunks, TILE - 1 : TILE, LANES : LANES + W]
        cut[2 - 2 * x, s : s + 1, :] = rim[0, s, 0:1, :]
        cut[3 - 2 * x, s : s + 1, :] = rim[1, s, TILE - 1 : TILE, :]
    edge_copy().start()
    pl.when(has_next_row)(lambda: row_copy(0).start())
    pl.when(has_prev_row)(lambda: row_copy(1).start())
    own_edge = pltpu.make_async_copy(cut.at[2 - x], edges.at[1 - x, x], own_edge_sem)
    own_edge.start()

    @pl.loop(0, 2 * S + 2)
    def _(s):
        cells[s, :, :, 0:LANES] = jnp.zeros((chunks + 2, TILE, LANES), jnp.float32)
        cells[s, :, :, LANES + W :] = jnp.zeros((chunks + 2, TILE, LANES), jnp.float32)

    @pl.when(jnp.logical_not(has_prev))
    def _():
        @pl.loop(0, chunks)
        def _(c):
            cells[0, 1 + c, :, span] = jnp.zeros((TILE, W), jnp.float32)

    @pl.when(jnp.logical_not(has_next))
    def _():
        @pl.loop(0, chunks)
        def _(c):
            cells[2 * S + 1, 1 + c, :, span] = jnp.zeros((TILE, W), jnp.float32)

    blocks, group = part // BLOCK, BLOCK // depth

    @pl.loop(0, blocks)
    def _(b):
        at = lax.broadcasted_iota(jnp.int32, (BLOCK, BLOCK), 0)
        to = lax.broadcasted_iota(jnp.int32, (BLOCK, BLOCK), 1)
        klass = to // LANES * blocks + (to % LANES // group + blocks - b) % blocks
        source = to % group * depth + klass
        spread[b] = jnp.where(at == source, 1.0, 0.0).astype(jnp.bfloat16)

    own_edge.wait()
    edge_copy().wait()
    pl.when(has_next_row)(lambda: row_copy(0).wait_send())
    pl.when(has_prev_row)(lambda: row_copy(1).wait_send())

    @pl.when(has_edge)
    def _():
        row_arrival(0).wait_recv()
        row_arrival(1).wait_recv()

    @pl.when(jnp.logical_not(has_edge))
    def _():
        edges[x] = jnp.zeros(edges.shape[1:], jnp.float32)

    for s in range(2 * S):
        cells[1 + s, 0, TILE - 1 : TILE, LANES : LANES + W] = edges[0, s // S, s % S : s % S + 1, :]
        cells[1 + s, chunks + 1, 0:1, LANES : LANES + W] = edges[1, s // S, s % S : s % S + 1, :]

    row_of = lax.broadcasted_iota(jnp.int32, (TILE, LANES), 0)
    lane_of = lax.broadcasted_iota(jnp.int32, (TILE, LANES), 1)
    is_top, is_bottom = row_of == 0, row_of == TILE - 1
    is_left, is_right = lane_of == 0, lane_of == LANES - 1
    group_of = lax.broadcasted_iota(jnp.int32, (4 * TILE, LANES), 1) // group

    def shade(q):
        t, begin = 1 + lax.rem(q, chunks), q // chunks * part

        def columns(b, carry):
            base = pl.multiple_of(begin + b * SPAN, SPAN)

            def lanes(v):
                return pl.ds(pl.multiple_of(base + v * LANES, LANES), LANES)

            def load(s):
                return [cells[s, t, :, lanes(v)] for v in range(SPAN // LANES + 2)]

            zero = jnp.zeros((TILE, LANES), jnp.float32)
            sums = [[zero] * 4 for _ in range(SPAN // LANES)]
            before, here = load(0), load(1)
            for s in range(1, 2 * S + 1):
                after = load(s + 1)
                for v in range(SPAN // LANES):
                    both, swing, green, alpha = sums[v]
                    centre = here[v + 1]
                    left = pltpu.roll(jnp.where(is_right, here[v], centre), 1, 1)
                    right = pltpu.roll(jnp.where(is_left, here[v + 2], centre), LANES - 1, 1)
                    above = pltpu.roll(jnp.where(is_bottom, cells[s, t - 1, :, lanes(v + 1)], centre), 1, 0)
                    below = pltpu.roll(jnp.where(is_top, cells[s, t + 1, :, lanes(v + 1)], centre), TILE - 1, 0)
                    dz, dy, dx = after[v + 1] - before[v + 1], below - above, right - left
                    square = dz * dz + dy * dy + (dx * dx + 4.0)
                    facing = 1.25 * dz + dy + (0.64 / 0.48) * dx
                    shading = jnp.abs(facing) * lax.rsqrt(square) + 0.3 / 0.336
                    opacity = 1.0 - jnp.exp2(-jnp.exp2((1.5 * LOG2E) * centre + log_extinction))
                    weight = (1.0 - alpha) * opacity
                    lit = weight * shading
                    sums[v] = [
                        both + lit,
                        swing + lit * jnp.tanh(centre),
                        green + lit * jnp.exp2(centre * (centre * -LOG2E)),
                        alpha + weight,
                    ]
                before, here = here, after
            for v in range(SPAN // LANES):
                both, swing, green, alpha = sums[v]
                both, swing = (0.5 * 0.336) * both, (0.5 * 0.336) * swing
                to = pl.ds(pl.multiple_of(b * SPAN + v * LANES, LANES), LANES)
                for ch, value in enumerate((both + swing, 0.336 * green, both - swing, alpha)):
                    image[ch, :, to] = value
            return carry

        lax.fori_loop(0, part // SPAN, columns, 0)
        turned = []
        for b in range(blocks):
            piece = image[:, :, b * BLOCK : (b + 1) * BLOCK].reshape(4 * TILE, BLOCK)
            high = piece.astype(jnp.bfloat16)
            low = (piece - high.astype(jnp.float32)).astype(jnp.bfloat16)
            two = jnp.dot(jnp.concatenate([high, low], axis=0), spread[b], preferred_element_type=jnp.float32)
            turned.append(two[: 4 * TILE] + two[4 * TILE :])
        for j in range(depth):
            h, r = j // blocks, j % blocks
            mixed = turned[-r % blocks][:, h * LANES : (h + 1) * LANES]
            for g in range(1, blocks):
                other = turned[(g - r) % blocks][:, h * LANES : (h + 1) * LANES]
                mixed = jnp.where(group_of == g, other, mixed)
            if r:
                mixed = pltpu.roll(mixed, LANES - group * r, 1)
            held[0][q, bit_reversed(j // 2, steps), j % 2] = mixed.reshape(4, TILE, LANES)

    def combine(k, q):
        half = groups >> (k + 1)
        bit = lax.rem(z // (1 << k), 2)
        part_copy(k, q).wait_recv()

        def join(near_of, far_of):
            for i in range(half):
                for p in range(2):
                    near, far = near_of(i, p), far_of(i, p)
                    clear = 1.0 - near[3]
                    for ch in range(4):
                        held[k + 1][q, i, p, ch] = near[ch] + clear * far[ch]

        def kept(i, p):
            return held[k][q, bit * half + i, p]

        def received(i, p):
            return came[k][q, i, p]

        pl.when(bit == 0)(lambda: join(kept, received))
        pl.when(bit == 1)(lambda: join(received, kept))

    def put(side, q, value):
        at = ((side * chunks + lax.rem(q, chunks)) * TILE) * parts + q // chunks
        for ch in range(4):
            out_ref[ch, pl.ds(at, TILE, stride=parts), :] = value[ch]

    @pl.loop(0, pieces + LAG * steps + 1)
    def _(i):
        @pl.when(i < pieces)
        def _():
            pair_copy(i)(lambda copy: copy.wait_recv())
            pl.when(i + ahead < pieces)(lambda: pair_copy(i + ahead)(start))
            pl.when(has_next)(lambda: face_copy(0, i).start())
            pl.when(has_prev)(lambda: face_copy(1, i).start())

        @pl.when(jnp.logical_and(i >= 1, i <= pieces))
        def _():
            q = i - 1
            pl.when(has_prev)(lambda: face_copy(0, q).wait_recv())
            pl.when(has_next)(lambda: face_copy(1, q).wait_recv())
            shade(q)
            part_copy(0, q).start()

        for k in range(steps):

            @pl.when(jnp.logical_and(i >= 1 + LAG * (k + 1), i <= pieces + LAG * (k + 1)))
            def _(k=k):
                q = i - 1 - LAG * (k + 1)
                combine(k, q)
                if k + 1 < steps:
                    part_copy(k + 1, q).start()
                else:
                    last_copy(q).start()
                    put(x, q, held[steps][q, 0, x])

    @pl.loop(0, pieces)
    def _(q):
        pair_copy(q)(lambda copy: copy.wait_send())
        pl.when(has_next)(lambda: face_copy(0, q).wait_send())
        pl.when(has_prev)(lambda: face_copy(1, q).wait_send())
        for k in range(steps):
            part_copy(k, q).wait_send()
        last_copy(q).wait()
        put(1 - x, q, final[q])


def local(log_density):
    S, R, W = log_density.shape
    depth, rows = lax.axis_size("depth"), lax.axis_size("rows")
    groups = depth // 2
    fits = (
        4 <= depth <= LANES
        and (LANES * depth) % SPAN == 0
        and depth & (depth - 1) == 0
        and W % (LANES * depth) == 0
        and R % (2 * TILE) == 0
    )
    if not fits:
        return local_general(log_density)
    steps = groups.bit_length() - 1
    tiles = R // TILE
    chunks = tiles // 2
    part = LANES * depth
    parts = W // part
    pieces = parts * chunks
    F32 = jnp.float32
    partial = [pltpu.VMEM((pieces, groups >> k, 2, 4, TILE, LANES), F32) for k in range(steps + 1)]
    arrivals = [pltpu.VMEM((pieces, groups >> (k + 1), 2, 4, TILE, LANES), F32) for k in range(steps)]
    DMA = pltpu.SemaphoreType.DMA
    out = pl.pallas_call(
        functools.partial(kernel, depth, rows),
        out_shape=jax.ShapeDtypeStruct((4, R * parts, LANES), F32),
        in_specs=[pl.BlockSpec(memory_space=pl.ANY)],
        out_specs=pl.BlockSpec(memory_space=pltpu.VMEM),
        scratch_shapes=[
            pltpu.VMEM((2 * S + 2, chunks + 2, TILE, W + 2 * LANES), F32),
            pltpu.VMEM((2, 2, S, W), F32),
            pltpu.VMEM((2, S, TILE, W), F32),
            pltpu.VMEM((4, S, W), F32),
            pltpu.VMEM((part // BLOCK, BLOCK, BLOCK), jnp.bfloat16),
            pltpu.VMEM((4, TILE, part), F32),
            pltpu.VMEM((pieces, 4, TILE, LANES), F32),
            *partial,
            *arrivals,
            DMA, DMA((2,)), DMA,
            DMA((pieces,)), DMA((pieces,)),
            DMA, DMA,
            DMA((2,)), DMA((2,)),
            DMA((2, pieces)), DMA((2, pieces)),
            DMA((steps, pieces)), DMA((steps, pieces)),
            DMA((pieces,)), DMA((pieces,)),
        ],
        compiler_params=pltpu.CompilerParams(
            collective_id=0, has_side_effects=True, vmem_limit_bytes=52 * 1024 * 1024
        ),
    )(log_density.reshape(S, tiles, TILE, W))
    return out.reshape(4, R, 1, W // depth)


def solution(mesh):
    placed = (P("depth", "rows", None),)
    return jax.shard_map(
        local, mesh=mesh, in_specs=placed, out_specs=P(None, "rows", "depth", None), check_vma=False
    )
```

```python
import functools
import math

import jax
import jax.numpy as jnp
from jax import lax
from jax.experimental import pallas as pl
from jax.experimental.pallas import tpu as pltpu
from jax.sharding import PartitionSpec as P

MESH = pl.DeviceIdType.MESH
TILE = 8
LANES = 128
BLOCK = 256
SPAN = 512
AHEAD = 1
LAG = 2
LOG2E = 1.4426950408889634


def with_halo(shard, sides, width):
    for axis, dim in sides:
        size, length = (lax.axis_size(axis), shard.shape[dim])
        up = [(i, (i + 1) % size) for i in range(size - 1)]
        down = [(j, i) for i, j in up]
        last = lax.slice_in_dim(shard, length - width, length, axis=dim)
        leading = lax.slice_in_dim(shard, 0, width, axis=dim)
        before = lax.ppermute(last, axis, up)
        after = lax.ppermute(leading, axis, down)
        shard = jnp.concatenate([before, shard, after], axis=dim)
    return shard


def shade_slab(padded, extinction, count):

    def advance(carry, index):
        accum_colour, accum_opacity = carry
        planes = lax.dynamic_slice_in_dim(padded, index, 3, 0)
        centre = planes[1, 1:-1, 1:-1]
        grad_z = 0.5 * (planes[2, 1:-1, 1:-1] - planes[0, 1:-1, 1:-1])
        grad_y = 0.5 * (planes[1, 2:, 1:-1] - planes[1, :-2, 1:-1])
        grad_x = 0.5 * (planes[1, 1:-1, 2:] - planes[1, 1:-1, :-2])
        length = jnp.sqrt(grad_z * grad_z + grad_y * grad_y + grad_x * grad_x + 1.0)
        facing = (0.6 * grad_z + 0.48 * grad_y + 0.64 * grad_x) / length
        shading = 0.3 + 0.7 * jnp.abs(facing)
        colour = (
            jnp.stack(
                [
                    jax.nn.sigmoid(2.0 * centre),
                    jnp.exp(-centre * centre),
                    jax.nn.sigmoid(-2.0 * centre),
                ]
            )
            * shading
        )
        opacity = 1.0 - jnp.exp(-extinction * jnp.exp(1.5 * centre))
        weight = (1.0 - accum_opacity) * opacity
        return ((accum_colour + weight * colour, accum_opacity + weight), None)

    height = padded.shape[1] - 2
    width = padded.shape[2] - 2
    start = (jnp.zeros((3, height, width), jnp.float32), jnp.zeros((height, width), jnp.float32))
    (colour_sum, opacity_sum), _ = lax.scan(advance, start, jnp.arange(count, dtype=jnp.int32))
    return jnp.concatenate([colour_sum, opacity_sum[None]], axis=0)


def over_pixels(nearer, farther, channel_axis):
    coverage = lax.slice_in_dim(nearer, 3, 4, axis=channel_axis)
    return nearer + (1.0 - coverage) * farther


def local_general(log_density):
    slices, row_count, width = log_density.shape
    depth_count = lax.axis_size("depth")
    classes = width // depth_count
    padded = with_halo(log_density, (("depth", 0), ("rows", 1)), 1)
    padded = jnp.pad(padded, ((0, 0), (0, 0), (1, 1)))
    image = shade_slab(padded, 0.5 / (slices * depth_count), slices)
    partial_value = image.reshape(4, row_count, classes, depth_count).transpose(0, 1, 3, 2)
    layers = lax.all_to_all(partial_value[None], "depth", split_axis=3, concat_axis=0, tiled=True)
    while layers.shape[0] > 1:
        paired = layers.reshape((layers.shape[0] // 2, 2) + layers.shape[1:])
        layers = over_pixels(paired[:, 0], paired[:, 1], 1)
    return layers[0]


def bit_reversed(value, bits):
    return sum(((value >> b) & 1) << (bits - 1 - b) for b in range(bits))


def kernel(depth, rows, vol_ref, out_ref, cells, edges, rim, cut, spread, image, final, *rest):
    S, tiles, _, W = vol_ref.shape
    chunks = tiles // 2
    groups = depth // 2
    steps = groups.bit_length() - 1
    part = LANES * depth
    parts = W // part
    pieces = parts * chunks
    ahead = min(AHEAD, pieces)
    span = pl.ds(LANES, W)
    log_extinction = math.log2(0.5 / (S * depth) * LOG2E)

    held, came = rest[: steps + 1], rest[steps + 1 : 2 * steps + 1]
    (own_sem, rim_sem, own_edge_sem, pair_send, pair_recv, edge_send, edge_recv, row_send, row_recv,
     face_send, face_recv, part_send, part_recv, last_send, last_recv) = rest[2 * steps + 1 :]

    me, row = lax.axis_index("depth"), lax.axis_index("rows")
    x, z = lax.rem(me, 2), me // 2
    first = me - x
    partner = first + 1 - x
    mine = 1 + S * x

    near = [(partner, row, None)]
    for d, there in ((-1, z >= 1), (1, z <= groups - 2)):
        near.append((me + 2 * d, row, there))
    for k in range(1, steps):
        near.append((2 * (z + (1 << k) * (1 - 2 * (lax.rem(z // (1 << k), 2)))) + x, row, None))
    for d, there in ((-1, row >= 1), (1, row <= rows - 2)):
        near.append((first, row + d, there))
        near.append((first + 1, row + d, there))
    barrier = pltpu.get_barrier_semaphore()
    count = 0
    for dd, rr, there in near:
        def greet(dd=dd, rr=rr):
            pl.semaphore_signal(barrier, inc=1, device_id=(dd, rr), device_id_type=MESH)
        if there is None:
            greet()
            count = count + 1
        else:
            pl.when(there)(greet)
            count = count + there.astype(jnp.int32)

    own = pltpu.make_async_copy(
        vol_ref.at[:, pl.ds(x * chunks, chunks)],
        cells.at[pl.ds(mine, S), pl.ds(1, chunks), :, span],
        own_sem,
    )
    own.start()
    rims = [
        pltpu.make_async_copy(vol_ref.at[:, tile], rim.at[n], rim_sem.at[n])
        for n, tile in enumerate(((1 - x) * chunks, (2 - x) * chunks - 1))
    ]
    for copy in rims:
        copy.start()
    pl.semaphore_wait(barrier, count)

    def pair_copy(q):
        def apply(act):
            for g in range(parts):
                low = g * part + (LANES if g else 0)
                high = (g + 1) * part + (LANES if g + 1 < parts else 0)

                @pl.when(q // chunks == g)
                def _(g=g, low=low, high=high):
                    c = q - g * chunks
                    act(pltpu.make_async_remote_copy(
                        src_ref=vol_ref.at[:, (1 - x) * chunks + c, :, pl.ds(low, high - low)],
                        dst_ref=cells.at[pl.ds(mine, S), 1 + c, :, pl.ds(LANES + low, high - low)],
                        send_sem=pair_send.at[q], recv_sem=pair_recv.at[q],
                        device_id=(partner, row), device_id_type=MESH,
                    ))
        return apply

    def start(copy):
        copy.start()

    def edge_copy():
        return pltpu.make_async_remote_copy(
            src_ref=cut.at[1 + x], dst_ref=edges.at[x, x],
            send_sem=edge_send, recv_sem=edge_recv,
            device_id=(partner, row), device_id_type=MESH,
        )

    def row_copy(direction):
        return pltpu.make_async_remote_copy(
            src_ref=cut.at[3 - 3 * direction], dst_ref=edges.at[direction, x],
            send_sem=row_send.at[direction], recv_sem=row_recv.at[x],
            device_id=(first + direction, row + 1 - 2 * direction), device_id_type=MESH,
        )

    def row_arrival(source):
        return pltpu.make_async_remote_copy(
            src_ref=cut.at[0], dst_ref=edges.at[x, source],
            send_sem=row_send.at[0], recv_sem=row_recv.at[source],
            device_id=(partner, row), device_id_type=MESH,
        )

    def face_copy(direction, q):
        c, at = lax.rem(q, chunks), pl.ds(pl.multiple_of(LANES + q // chunks * part, LANES), part)
        return pltpu.make_async_remote_copy(
            src_ref=cells.at[2 * S if direction == 0 else 1, 1 + c, :, at],
            dst_ref=cells.at[0 if direction == 0 else 2 * S + 1, 1 + c, :, at],
            send_sem=face_send.at[direction, q], recv_sem=face_recv.at[direction, q],
            device_id=(me + (2 if direction == 0 else -2), row), device_id_type=MESH,
        )

    def part_copy(k, q):
        half = groups >> (k + 1)
        bit = lax.rem(z // (1 << k), 2)
        return pltpu.make_async_remote_copy(
            src_ref=held[k].at[q, pl.ds((1 - bit) * half, half)], dst_ref=came[k].at[q],
            send_sem=part_send.at[k, q], recv_sem=part_recv.at[k, q],
            device_id=(me + 2 * (1 << k) * (1 - 2 * bit), row), device_id_type=MESH,
        )

    def last_copy(q):
        return pltpu.make_async_remote_copy(
            src_ref=held[steps].at[q, 0, 1 - x], dst_ref=final.at[q],
            send_sem=last_send.at[q], recv_sem=last_recv.at[q],
            device_id=(partner, row), device_id_type=MESH,
        )

    pl.loop(0, ahead)(lambda q: pair_copy(q)(start))

    has_next_row, has_prev_row = row <= rows - 2, row >= 1
    has_next, has_prev = z <= groups - 2, z >= 1
    has_edge = jnp.logical_or(jnp.logical_and(x == 0, has_prev_row), jnp.logical_and(x == 1, has_next_row))

    own.wait()
    for copy in rims:
        copy.wait()
    for s in range(S):
        cut[2 * x, s : s + 1, :] = cells[mine + s, 1, 0:1, LANES : LANES + W]
        cut[1 + 2 * x, s : s + 1, :] = cells[mine + s, chunks, TILE - 1 : TILE, LANES : LANES + W]
        cut[2 - 2 * x, s : s + 1, :] = rim[0, s, 0:1, :]
        cut[3 - 2 * x, s : s + 1, :] = rim[1, s, TILE - 1 : TILE, :]
    edge_copy().start()
    pl.when(has_next_row)(lambda: row_copy(0).start())
    pl.when(has_prev_row)(lambda: row_copy(1).start())
    own_edge = pltpu.make_async_copy(cut.at[2 - x], edges.at[1 - x, x], own_edge_sem)
    own_edge.start()

    @pl.loop(0, 2 * S + 2)
    def _(s):
        cells[s, :, :, 0:LANES] = jnp.zeros((chunks + 2, TILE, LANES), jnp.float32)
        cells[s, :, :, LANES + W :] = jnp.zeros((chunks + 2, TILE, LANES), jnp.float32)

    @pl.when(jnp.logical_not(has_prev))
    def _():
        @pl.loop(0, chunks)
        def _(c):
            cells[0, 1 + c, :, span] = jnp.zeros((TILE, W), jnp.float32)

    @pl.when(jnp.logical_not(has_next))
    def _():
        @pl.loop(0, chunks)
        def _(c):
            cells[2 * S + 1, 1 + c, :, span] = jnp.zeros((TILE, W), jnp.float32)

    blocks, group = part // BLOCK, BLOCK // depth

    @pl.loop(0, blocks)
    def _(b):
        at = lax.broadcasted_iota(jnp.int32, (BLOCK, BLOCK), 0)
        to = lax.broadcasted_iota(jnp.int32, (BLOCK, BLOCK), 1)
        klass = to // LANES * blocks + (to % LANES // group + blocks - b) % blocks
        source = to % group * depth + klass
        spread[b] = jnp.where(at == source, 1.0, 0.0).astype(jnp.bfloat16)

    own_edge.wait()
    edge_copy().wait()
    pl.when(has_next_row)(lambda: row_copy(0).wait_send())
    pl.when(has_prev_row)(lambda: row_copy(1).wait_send())

    @pl.when(has_edge)
    def _():
        row_arrival(0).wait_recv()
        row_arrival(1).wait_recv()

    @pl.when(jnp.logical_not(has_edge))
    def _():
        edges[x] = jnp.zeros(edges.shape[1:], jnp.float32)

    for s in range(2 * S):
        cells[1 + s, 0, TILE - 1 : TILE, LANES : LANES + W] = edges[0, s // S, s % S : s % S + 1, :]
        cells[1 + s, chunks + 1, 0:1, LANES : LANES + W] = edges[1, s // S, s % S : s % S + 1, :]

    row_of = lax.broadcasted_iota(jnp.int32, (TILE, LANES), 0)
    lane_of = lax.broadcasted_iota(jnp.int32, (TILE, LANES), 1)
    is_top, is_bottom = row_of == 0, row_of == TILE - 1
    is_left, is_right = lane_of == 0, lane_of == LANES - 1
    group_of = lax.broadcasted_iota(jnp.int32, (4 * TILE, LANES), 1) // group

    def shade(q):
        t, begin = 1 + lax.rem(q, chunks), q // chunks * part

        def columns(b, carry):
            base = pl.multiple_of(begin + b * SPAN, SPAN)

            def lanes(v):
                return pl.ds(pl.multiple_of(base + v * LANES, LANES), LANES)

            def load(s):
                return [cells[s, t, :, lanes(v)] for v in range(SPAN // LANES + 2)]

            zero = jnp.zeros((TILE, LANES), jnp.float32)
            sums = [[zero] * 4 for _ in range(SPAN // LANES)]
            before, here = load(0), load(1)
            for s in range(1, 2 * S + 1):
                after = load(s + 1)
                for v in range(SPAN // LANES):
                    both, swing, green, alpha = sums[v]
                    centre = here[v + 1]
                    left = pltpu.roll(jnp.where(is_right, here[v], centre), 1, 1)
                    right = pltpu.roll(jnp.where(is_left, here[v + 2], centre), LANES - 1, 1)
                    above = pltpu.roll(jnp.where(is_bottom, cells[s, t - 1, :, lanes(v + 1)], centre), 1, 0)
                    below = pltpu.roll(jnp.where(is_top, cells[s, t + 1, :, lanes(v + 1)], centre), TILE - 1, 0)
                    dz, dy, dx = after[v + 1] - before[v + 1], below - above, right - left
                    square = dz * dz + dy * dy + (dx * dx + 4.0)
                    facing = 1.25 * dz + dy + (0.64 / 0.48) * dx
                    shading = jnp.abs(facing) * lax.rsqrt(square) + 0.3 / 0.336
                    opacity = 1.0 - jnp.exp2(-jnp.exp2((1.5 * LOG2E) * centre + log_extinction))
                    weight = (1.0 - alpha) * opacity
                    lit = weight * shading
                    sums[v] = [
                        both + lit,
                        swing + lit * jnp.tanh(centre),
                        green + lit * jnp.exp2(centre * (centre * -LOG2E)),
                        alpha + weight,
                    ]
                before, here = here, after
            for v in range(SPAN // LANES):
                both, swing, green, alpha = sums[v]
                both, swing = (0.5 * 0.336) * both, (0.5 * 0.336) * swing
                to = pl.ds(pl.multiple_of(b * SPAN + v * LANES, LANES), LANES)
                for ch, value in enumerate((both + swing, 0.336 * green, both - swing, alpha)):
                    image[ch, :, to] = value
            return carry

        lax.fori_loop(0, part // SPAN, columns, 0)
        turned = []
        for b in range(blocks):
            piece = image[:, :, b * BLOCK : (b + 1) * BLOCK].reshape(4 * TILE, BLOCK)
            high = piece.astype(jnp.bfloat16)
            low = (piece - high.astype(jnp.float32)).astype(jnp.bfloat16)
            two = jnp.dot(jnp.concatenate([high, low], axis=0), spread[b], preferred_element_type=jnp.float32)
            turned.append(two[: 4 * TILE] + two[4 * TILE :])
        for j in range(depth):
            h, r = j // blocks, j % blocks
            mixed = turned[-r % blocks][:, h * LANES : (h + 1) * LANES]
            for g in range(1, blocks):
                other = turned[(g - r) % blocks][:, h * LANES : (h + 1) * LANES]
                mixed = jnp.where(group_of == g, other, mixed)
            if r:
                mixed = pltpu.roll(mixed, LANES - group * r, 1)
            held[0][q, bit_reversed(j // 2, steps), j % 2] = mixed.reshape(4, TILE, LANES)

    def combine(k, q):
        half = groups >> (k + 1)
        bit = lax.rem(z // (1 << k), 2)
        part_copy(k, q).wait_recv()

        def join(near_of, far_of):
            for i in range(half):
                for p in range(2):
                    near, far = near_of(i, p), far_of(i, p)
                    clear = 1.0 - near[3]
                    for ch in range(4):
                        held[k + 1][q, i, p, ch] = near[ch] + clear * far[ch]

        def kept(i, p):
            return held[k][q, bit * half + i, p]

        def received(i, p):
            return came[k][q, i, p]

        pl.when(bit == 0)(lambda: join(kept, received))
        pl.when(bit == 1)(lambda: join(received, kept))

    def put(side, q, value):
        at = ((side * chunks + lax.rem(q, chunks)) * TILE) * parts + q // chunks
        for ch in range(4):
            out_ref[ch, pl.ds(at, TILE, stride=parts), :] = value[ch]

    @pl.loop(0, pieces + LAG * steps + 1)
    def _(i):
        @pl.when(i < pieces)
        def _():
            pair_copy(i)(lambda copy: copy.wait_recv())
            pl.when(i + ahead < pieces)(lambda: pair_copy(i + ahead)(start))
            pl.when(has_next)(lambda: face_copy(0, i).start())
            pl.when(has_prev)(lambda: face_copy(1, i).start())

        @pl.when(jnp.logical_and(i >= 1, i <= pieces))
        def _():
            q = i - 1
            pl.when(has_prev)(lambda: face_copy(0, q).wait_recv())
            pl.when(has_next)(lambda: face_copy(1, q).wait_recv())
            shade(q)
            part_copy(0, q).start()

        for k in range(steps):

            @pl.when(jnp.logical_and(i >= 1 + LAG * (k + 1), i <= pieces + LAG * (k + 1)))
            def _(k=k):
                q = i - 1 - LAG * (k + 1)
                combine(k, q)
                if k + 1 < steps:
                    part_copy(k + 1, q).start()
                else:
                    last_copy(q).start()
                    put(x, q, held[steps][q, 0, x])

    @pl.loop(0, pieces)
    def _(q):
        pair_copy(q)(lambda copy: copy.wait_send())
        pl.when(has_next)(lambda: face_copy(0, q).wait_send())
        pl.when(has_prev)(lambda: face_copy(1, q).wait_send())
        for k in range(steps):
            part_copy(k, q).wait_send()
        last_copy(q).wait()
        put(1 - x, q, final[q])


def local(log_density):
    S, R, W = log_density.shape
    depth, rows = lax.axis_size("depth"), lax.axis_size("rows")
    groups = depth // 2
    fits = (
        4 <= depth <= LANES
        and (LANES * depth) % SPAN == 0
        and depth & (depth - 1) == 0
        and W % (LANES * depth) == 0
        and R % (2 * TILE) == 0
    )
    if not fits:
        return local_general(log_density)
    steps = groups.bit_length() - 1
    tiles = R // TILE
    chunks = tiles // 2
    part = LANES * depth
    parts = W // part
    pieces = parts * chunks
    F32 = jnp.float32
    partial = [pltpu.VMEM((pieces, groups >> k, 2, 4, TILE, LANES), F32) for k in range(steps + 1)]
    arrivals = [pltpu.VMEM((pieces, groups >> (k + 1), 2, 4, TILE, LANES), F32) for k in range(steps)]
    DMA = pltpu.SemaphoreType.DMA
    out = pl.pallas_call(
        functools.partial(kernel, depth, rows),
        out_shape=jax.ShapeDtypeStruct((4, R * parts, LANES), F32),
        in_specs=[pl.BlockSpec(memory_space=pl.ANY)],
        out_specs=pl.BlockSpec(memory_space=pltpu.VMEM),
        scratch_shapes=[
            pltpu.VMEM((2 * S + 2, chunks + 2, TILE, W + 2 * LANES), F32),
            pltpu.VMEM((2, 2, S, W), F32),
            pltpu.VMEM((2, S, TILE, W), F32),
            pltpu.VMEM((4, S, W), F32),
            pltpu.VMEM((part // BLOCK, BLOCK, BLOCK), jnp.bfloat16),
            pltpu.VMEM((4, TILE, part), F32),
            pltpu.VMEM((pieces, 4, TILE, LANES), F32),
            *partial,
            *arrivals,
            DMA, DMA((2,)), DMA,
            DMA((pieces,)), DMA((pieces,)),
            DMA, DMA,
            DMA((2,)), DMA((2,)),
            DMA((2, pieces)), DMA((2, pieces)),
            DMA((steps, pieces)), DMA((steps, pieces)),
            DMA((pieces,)), DMA((pieces,)),
        ],
        compiler_params=pltpu.CompilerParams(
            collective_id=0, has_side_effects=True, vmem_limit_bytes=52 * 1024 * 1024
        ),
    )(log_density.reshape(S, tiles, TILE, W))
    return out.reshape(4, R, 1, W // depth)


def solution(mesh):
    placed = (P("depth", "rows", None),)
    return jax.shard_map(
        local, mesh=mesh, in_specs=placed, out_specs=P(None, "rows", "depth", None), check_vma=False
    )
```
